256 devices in a mesh: tile: 64 (over z, y, x_hi), orient: 4 (over x_lo, core).
Axes of the slice: x: 4 (x_hi: 2, x_lo: 2; x = x_hi * 2 + x_lo), y: 4, z: 8, core: 2. Of those that a mesh axis runs over, the one named last changes fastest.
Arguments:
- micrograph: bfloat16 [64, 384, 384], P('tile'), may hold values from -6 to 6
- template_stack: bfloat16 [256, 16384], P(None, 'tile'), as said below
- orient_list: int32 [32], replicated, may hold values from 0 to 255
Outputs:
- peak: float32 [64, 384, 384], P('tile', 'orient')
- excess: float32 [64, 384, 384], P('tile', 'orient')
The draws below stay inside these ranges and needn't reach their ends.
Inputs may be any that keep to these rules, and one draw needn't show every extreme that they name: `template_stack`: template pixels, finite.
All inputs are finite; a program needn't handle non-finite values.
Results may differ from the reference program's by a relative error of at most 0.0065.
Values may be sent and summed in bfloat16 or wider, within the bound.
No kernel may reach another device: no remote copies, remote signals or barrier semaphores. Data moves between devices by JAX's collectives and lax.ppermute only.
A program may use at most 64 MiB of HBM per device.

```python
import math
import jax
import jax.numpy as jnp
from jax import lax

TILE = 512
TS = 128
CORE = 384
GRID_W = 8
STACK = 256
ORIENTS = 32
TILES = 64


def draw_template_stack(key, part):
    key = jax.random.fold_in(key, 11)
    key_base, key_rows, key_cols = jax.random.split(key, 3)
    row_scale = jnp.exp(jax.random.uniform(key_rows, (STACK, TS, 1), jnp.float32, 0.0, math.log(10.0)))
    col_scale = jnp.exp(jax.random.uniform(key_cols, (STACK, 1, TS), jnp.float32, 0.0, math.log(10.0)))
    base = jax.random.normal(key_base, (STACK, TS, TS), jnp.float32)
    return (base * row_scale * col_scale).reshape(STACK, TS * TS).astype(jnp.bfloat16)


def set_ends(array, rng, least, top_value):
    longest = array.shape.index(max(array.shape))
    spots = []
    for shift in (0, 1):
        where = [jax.random.randint(jax.random.fold_in(rng, axis), (), 0, length) for axis, length in enumerate(array.shape)]
        where[longest] = (where[longest] + shift) % array.shape[longest]
        spots.append(tuple(where))
    return array.at[spots[0]].set(least).at[spots[1]].set(top_value)


def block_scale(stream_key, shape, pieces, smallest, largest):
    gain, own = 1.0, jax.random.fold_in(stream_key, 6)
    for position, blocks in pieces:
        draws = jnp.exp(jax.random.uniform(jax.random.fold_in(own, position), (blocks,), jnp.float32, smallest / len(pieces), largest / len(pieces)))
        gain = gain * jnp.repeat(draws, shape[position] // blocks).reshape([-1 if axis == position else 1 for axis in range(len(shape))])
    return gain


def gaussian(own_key, extent, width, bound, cuts=(), kind=jnp.bfloat16):
    drawn = jax.random.normal(own_key, extent, jnp.float32) * width
    if len(cuts) > 0:
        drawn = block_scale(own_key, extent, cuts, -0.22, 0.18) * drawn
    return jnp.clip(drawn, min=-bound, max=bound).astype(kind)


def setup_inputs(seed: int = 0) -> dict:
    seeds = jax.random.split(jax.random.key(seed), 4)
    return {
        "micrograph": gaussian(seeds[0], (TILES, CORE, CORE), 1.0, 6.0, ((0, 64),)),
        "template_stack": draw_template_stack(jax.random.fold_in(seeds[3], 71), 0),
        "orient_list": set_ends(jax.random.randint(seeds[2], (ORIENTS,), 0, STACK), jax.random.fold_in(seeds[2], 1), 0, STACK - 1).astype(jnp.int32),
    }


def fourier_tables():
    steps_index = jnp.arange(TILE, dtype=jnp.int32)
    product = steps_index[:, None] * steps_index[None, :] % TILE
    angle = product.astype(jnp.float32) * (2.0 * math.pi / TILE)
    return (jnp.cos(angle).astype(jnp.bfloat16), jnp.sin(angle).astype(jnp.bfloat16))

def spectrum(pixels, row_cos, row_sin, col_cos, col_sin):
    first_real = jnp.dot(pixels, col_cos, preferred_element_type=jnp.float32)
    first_imaginary = -jnp.dot(pixels, col_sin, preferred_element_type=jnp.float32)
    stacked = jnp.concatenate([first_real, first_imaginary], 0).astype(jnp.bfloat16)
    left_real = jnp.concatenate([row_cos, row_sin], 1)
    left_imaginary = jnp.concatenate([-row_sin, row_cos], 1)
    out_real = jnp.dot(left_real, stacked, preferred_element_type=jnp.float32).astype(jnp.bfloat16)
    out_imaginary = jnp.dot(left_imaginary, stacked, preferred_element_type=jnp.float32).astype(jnp.bfloat16)
    return (out_real, out_imaginary)

def normalize(flat_pixels):
    values = flat_pixels.astype(jnp.float32)
    centered = values - jnp.mean(values)
    spread = jnp.sqrt(jnp.mean(centered * centered) + 1e-06)
    return (centered / (spread * TS)).astype(jnp.bfloat16).reshape(TS, TS)

def cross_spectrum(image_real, image_imaginary, piece_real, piece_imaginary):
    a_real = image_real.astype(jnp.float32)
    a_imaginary = image_imaginary.astype(jnp.float32)
    b_real = piece_real.astype(jnp.float32)
    b_imaginary = piece_imaginary.astype(jnp.float32)
    cross_real = (a_real * b_real + a_imaginary * b_imaginary).astype(jnp.bfloat16)
    cross_imaginary = (a_imaginary * b_real - a_real * b_imaginary).astype(jnp.bfloat16)
    return (cross_real, cross_imaginary)

def correlate(image_real, image_imaginary, template_real, template_imaginary, cosine, sine_table):
    cross_real, cross_imaginary = cross_spectrum(image_real, image_imaginary, template_real, template_imaginary)
    stacked = jnp.concatenate([cross_real, cross_imaginary], 0)
    left_real = jnp.concatenate([cosine[:CORE], -sine_table[:CORE]], 1)
    left_imaginary = jnp.concatenate([sine_table[:CORE], cosine[:CORE]], 1)
    inner_real = jnp.dot(left_real, stacked, preferred_element_type=jnp.float32).astype(jnp.bfloat16)
    inner_imaginary = jnp.dot(left_imaginary, stacked, preferred_element_type=jnp.float32).astype(jnp.bfloat16)
    inverse_right = jnp.concatenate([cosine[:, :CORE], -sine_table[:, :CORE]], 0)
    joined = jnp.concatenate([inner_real, inner_imaginary], 1)
    return jnp.dot(joined, inverse_right, preferred_element_type=jnp.float32) * (1.0 / (TILE * TILE))

def reference(micrograph, template_stack, orient_list):
    cosine, sine_table = fourier_tables()
    grid_rows = TILES // GRID_W
    assembled = micrograph.reshape(grid_rows, GRID_W, CORE, CORE).transpose(0, 2, 1, 3)
    assembled = assembled.reshape(grid_rows * CORE, GRID_W * CORE)
    assembled = jnp.pad(assembled, ((0, TS), (0, TS)))
    chosen = jnp.take(template_stack, orient_list, axis=0)

    def template_spectrum(flat_pixels):
        shaped = normalize(flat_pixels)
        return spectrum(shaped, cosine[:, :TS], sine_table[:, :TS], cosine[:TS, :], sine_table[:TS, :])
    template_real, template_imaginary = lax.map(template_spectrum, chosen)

    def one_tile(tile_index):
        grid_row = (tile_index // GRID_W).astype(jnp.int32)
        grid_col = (tile_index % GRID_W).astype(jnp.int32)
        padded = lax.dynamic_slice(assembled, (grid_row * CORE, grid_col * CORE), (TILE, TILE))
        image_real, image_imaginary = spectrum(padded, cosine, sine_table, cosine, sine_table)

        def advance(carried, spectra_pair):
            highest, running = carried
            corr = correlate(image_real, image_imaginary, spectra_pair[0], spectra_pair[1], cosine, sine_table)
            return ((jnp.maximum(highest, corr), running + corr), None)
        start_pair = (jnp.full((CORE, CORE), -1e+30, jnp.float32), jnp.zeros((CORE, CORE), jnp.float32))
        (highest, running), _ = lax.scan(advance, start_pair, (template_real, template_imaginary))
        return (highest, highest - running / ORIENTS)
    peak, excess = lax.map(one_tile, jnp.arange(TILES, dtype=jnp.int32))
    return (peak, excess)
```

```python
import functools
import math

import jax
import jax.numpy as jnp
import numpy as np
from jax import lax
from jax.experimental import pallas as pl
from jax.experimental.pallas import tpu as pltpu
from jax.sharding import PartitionSpec as P

TILE = 512
TS = 128
CORE = 384
GRID_W = 8
TILES = 64
ORI_DEV = 8
MEMBERS = 4
ROWS = 96
ROWS_IN = 224
LENGTH = 256
PAIRS = LENGTH // 2
HALF = TILE // 2
ORDER = (2, 3, 1, 0)


def bf16(table):
    return np.asarray(table, np.float64).astype(jnp.bfloat16)


def column_table():
    n = np.arange(TILE)[:, None]
    k = np.arange(HALF)[None, :]
    angle = (math.pi / TILE) * ((n * (2 * k + 1)) % (2 * TILE))
    return bf16(np.concatenate([np.cos(angle), -np.sin(angle)], 1))


def row_table(rows):
    j = np.arange(PAIRS)[:, None]
    m = np.arange(rows)[None, :]
    angle = (math.pi / LENGTH) * ((m * (2 * j + 1)) % (2 * LENGTH))
    c, s = np.cos(angle), np.sin(angle)
    return bf16(np.block([[c, s], [-s, c], [c, -s], [s, c]]))


def inverse_row_table():
    j = np.arange(PAIRS)[None, :]
    c = np.arange(ROWS)[:, None]
    angle = (math.pi / LENGTH) * ((c * (2 * j + 1)) % (2 * LENGTH))
    return bf16(np.concatenate([np.cos(angle), np.sin(angle)], 1))


def inverse_column_table():
    k = np.arange(HALF)[:, None]
    c = np.arange(CORE)[None, :]
    angle = (math.pi / TILE) * ((c * (2 * k + 1)) % (2 * TILE))
    scale = 2.0 / (LENGTH * TILE)
    return bf16(np.concatenate([np.cos(angle), -np.sin(angle)], 0) * scale)


def dot(a, b):
    return jnp.dot(a, b, preferred_element_type=jnp.float32)


def select_kernel(ids_ref, stack_ref, out_ref):
    row = lax.broadcasted_iota(jnp.int32, (2 * ORI_DEV, 256), 0)
    lane = lax.broadcasted_iota(jnp.int32, (2 * ORI_DEV, 256), 1)
    wanted = jnp.zeros((2 * ORI_DEV, 256), jnp.int32)
    for o in range(ORI_DEV):
        wanted = jnp.where(row % ORI_DEV == o, ids_ref[o], wanted)
    hot = jnp.where(lane == wanted, 1.0, 0.0).astype(jnp.bfloat16)
    picked = dot(hot, stack_ref[...])
    both = jnp.concatenate([picked[:ORI_DEV, :TS], picked[ORI_DEV:, TS:]], 0).astype(jnp.bfloat16)
    out_ref[...] = jnp.broadcast_to(both[None], out_ref.shape)


def image_kernel(member_ref, own_ref, right_ref, below_ref, corner_ref, col_ref, row_ref, out_ref, g_ref):
    def columns(first, second, start, count):
        g = dot(first, col_ref[:CORE]) + dot(second, col_ref[CORE:])
        g_ref[0, start : start + count] = g[:, :HALF].astype(jnp.bfloat16)
        g_ref[1, start : start + count] = g[:, HALF:].astype(jnp.bfloat16)

    columns(own_ref[...], right_ref[...], 0, CORE)
    columns(below_ref[...], corner_ref[...], CORE, TS)
    for s, bits in enumerate(ORDER):
        start = pl.multiple_of((member_ref[0] ^ bits) * ROWS, 32)
        piece = jnp.concatenate([g_ref[0, pl.ds(start, ROWS_IN)], g_ref[1, pl.ds(start, ROWS_IN)]], 0)
        out_ref[s] = dot(row_ref[...], piece).astype(jnp.bfloat16)


def template_kernel(pixels_ref, col_ref, row_ref, out_ref, shape_ref):
    values = pixels_ref[...].astype(jnp.float32).reshape(TS, ORI_DEV, TS)
    mean = jnp.sum(jnp.sum(values, 0), 1, keepdims=True) / (TS * TS)
    centered = values - mean[None]
    square = jnp.sum(jnp.sum(centered * centered, 0), 1, keepdims=True) / (TS * TS)
    spread = jnp.sqrt(square + 1e-06) * TS
    shape_ref[...] = (centered / spread[None]).reshape(TS * ORI_DEV, TS)
    for o in range(ORI_DEV):
        shape = shape_ref[pl.ds(o, TS, stride=ORI_DEV), :].astype(jnp.bfloat16)
        g = dot(shape, col_ref[...]).astype(jnp.bfloat16)
        g = jnp.concatenate([g[:, :HALF], g[:, HALF:]], 0)
        out_ref[o] = dot(row_ref[...], g).astype(jnp.bfloat16)


def block_kernel(image_ref, template_ref, inv_row_ref, inv_col_ref, high_ref, sum_ref, inner_ref):
    def part(ref, p):
        return ref[0, p * PAIRS : (p + 1) * PAIRS].astype(jnp.float32)

    for o in range(ORI_DEV):
        tr = template_ref.at[o : o + 1]

        def cross(p):
            a, b = part(image_ref, 2 * p), part(image_ref, 2 * p + 1)
            c, d = part(tr, 2 * p), part(tr, 2 * p + 1)
            return a * c + b * d, b * c - a * d

        plus_re, plus_im = cross(0)
        minus_re, minus_im = cross(1)
        mixed = jnp.concatenate(
            [
                jnp.concatenate([plus_re + minus_re, plus_im + minus_im], 1),
                jnp.concatenate([minus_im - plus_im, plus_re - minus_re], 1),
            ],
            0,
        ).astype(jnp.bfloat16)
        inner_ref[o * ROWS : (o + 1) * ROWS] = dot(inv_row_ref[...], mixed).astype(jnp.bfloat16)
    corr = dot(inner_ref[...], inv_col_ref[...]).reshape(ORI_DEV, ROWS, CORE)
    high_ref[...] = jnp.max(corr, 0).astype(high_ref.dtype)
    sum_ref[...] = jnp.sum(corr, 0).astype(sum_ref.dtype)


VMEM = pl.BlockSpec(memory_space=pltpu.VMEM)
SMEM = pl.BlockSpec(memory_space=pltpu.SMEM)
LIMIT = 40 * 1024 * 1024


def call(kernel, outs, specs, scratch=(), flops=0):
    return pl.pallas_call(
        kernel,
        out_shape=outs,
        in_specs=specs,
        out_specs=jax.tree.map(lambda _: VMEM, outs),
        scratch_shapes=list(scratch),
        compiler_params=pltpu.CompilerParams(vmem_limit_bytes=LIMIT),
        cost_estimate=pl.CostEstimate(flops=flops, bytes_accessed=2**21, transcendentals=0),
    )


def shape_of(dims, dtype=jnp.bfloat16):
    return jax.ShapeDtypeStruct(dims, dtype)


def halo(block, distance):
    route = []
    for t in range(TILES):
        column = t % GRID_W + distance % GRID_W
        source = t + distance
        if column < GRID_W and source < TILES:
            route.append((source, t))
    return lax.ppermute(block, "tile", route)


def shards(micrograph, template_stack, orient_list):
    member = lax.axis_index("orient")
    ids = lax.dynamic_slice_in_dim(orient_list, member * ORI_DEV, ORI_DEV)
    spread = call(select_kernel, shape_of((TILES, 2 * ORI_DEV, TS)), [SMEM, VMEM])(ids, template_stack)
    pixels = lax.all_to_all(spread, "tile", 0, 0)
    own = micrograph[0]
    right = halo(own[:, :TS], 1)
    below = halo(own[:TS], GRID_W)
    corner = halo(own[:TS, :TS], GRID_W + 1)
    columns = column_table()
    image = call(
        image_kernel,
        shape_of((MEMBERS, 4 * PAIRS, HALF)),
        [SMEM] + [VMEM] * 6,
        [pltpu.VMEM((2, TILE, HALF), jnp.bfloat16)],
        flops=1600000000,
    )(member[None], own, right, below, corner, columns, row_table(ROWS_IN))
    templates = call(
        template_kernel,
        shape_of((ORI_DEV, 4 * PAIRS, HALF)),
        [VMEM] * 3,
        [pltpu.VMEM((TS * ORI_DEV, TS), jnp.float32)],
        flops=1000000000,
    )(pixels, columns[:TS], row_table(TS))
    inverse_rows, inverse_columns = inverse_row_table(), inverse_column_table()
    highs, sums = [], []
    for s, bits in enumerate(ORDER):
        kind = jnp.bfloat16 if bits else jnp.float32
        high, total = call(
            block_kernel,
            (shape_of((ROWS, CORE), kind), shape_of((ROWS, CORE), kind)),
            [VMEM] * 4,
            [pltpu.VMEM((ORI_DEV * ROWS, TILE), jnp.bfloat16)],
            flops=1000000000,
        )(image[s : s + 1], templates, inverse_rows, inverse_columns)
        if bits:
            route = [(i, i ^ bits) for i in range(MEMBERS)]
            high, total = lax.ppermute((high, total), "orient", route)
        highs.append(high.astype(jnp.float32))
        sums.append(total.astype(jnp.float32))
    peak = functools.reduce(jnp.maximum, highs)
    excess = peak - functools.reduce(jnp.add, sums) / (MEMBERS * ORI_DEV)
    return (peak[None], excess[None])


def solution(mesh):
    placed = (P("tile", None, None), P(None, "tile"), P())
    return jax.shard_map(
        shards,
        mesh=mesh,
        in_specs=placed,
        out_specs=(P("tile", "orient", None), P("tile", "orient", None)),
        check_vma=False,
    )
```

```python
import math

import jax
import jax.numpy as jnp
import numpy as np
from jax import lax
from jax.experimental import pallas as pl
from jax.experimental.pallas import tpu as pltpu
from jax.sharding import PartitionSpec as P

TILE = 512
TS = 128
CORE = 384
GRID_W = 8
TILES = 64
ORI_DEV = 8
MEMBERS = 4
ROWS = 96
ROWS_IN = 224
LENGTH = 256
PAIRS = LENGTH // 2
HALF = TILE // 2
ORDER = (2, 3, 1, 0)


def bf16(table):
    return np.asarray(table, np.float64).astype(jnp.bfloat16)


def column_table():
    n = np.arange(TILE)[:, None]
    k = np.arange(HALF)[None, :]
    angle = (math.pi / TILE) * ((n * (2 * k + 1)) % (2 * TILE))
    return bf16(np.concatenate([np.cos(angle), -np.sin(angle)], 1))


def row_table(rows):
    j = np.arange(PAIRS)[:, None]
    m = np.arange(rows)[None, :]
    angle = (math.pi / LENGTH) * ((m * (2 * j + 1)) % (2 * LENGTH))
    c, s = np.cos(angle), np.sin(angle)
    return bf16(np.block([[c, s], [-s, c], [c, -s], [s, c]]))


def inverse_row_table():
    j = np.arange(PAIRS)[None, :]
    c = np.arange(ROWS)[:, None]
    angle = (math.pi / LENGTH) * ((c * (2 * j + 1)) % (2 * LENGTH))
    return bf16(np.concatenate([np.cos(angle), np.sin(angle)], 1))


def inverse_column_table():
    k = np.arange(HALF)[:, None]
    c = np.arange(CORE)[None, :]
    angle = (math.pi / TILE) * ((c * (2 * k + 1)) % (2 * TILE))
    scale = 2.0 / (LENGTH * TILE)
    return bf16(np.concatenate([np.cos(angle), -np.sin(angle)], 0) * scale)


def dot(a, b):
    return jnp.dot(a, b, preferred_element_type=jnp.float32)


def prepare_kernel(ids_ref, micro_ref, stack_ref, out_ref, right_ref, below_ref, corner_ref, sems):
    own = micro_ref.at[0]
    copies = [
        pltpu.make_async_copy(own.at[:, :TS], right_ref, sems.at[0]),
        pltpu.make_async_copy(own.at[:TS, :], below_ref, sems.at[1]),
        pltpu.make_async_copy(own.at[:TS, :TS], corner_ref, sems.at[2]),
    ]
    for copy in copies:
        copy.start()
    row = lax.broadcasted_iota(jnp.int32, (2 * ORI_DEV, 256), 0)
    lane = lax.broadcasted_iota(jnp.int32, (2 * ORI_DEV, 256), 1)
    wanted = jnp.zeros((2 * ORI_DEV, 256), jnp.int32)
    first = lax.axis_index("orient") * ORI_DEV
    for o in range(ORI_DEV):
        wanted = jnp.where(row % ORI_DEV == o, ids_ref[first + o], wanted)
    hot = jnp.where(lane == wanted, 1.0, 0.0).astype(jnp.bfloat16)
    picked = dot(hot, stack_ref[...])
    both = jnp.concatenate([picked[:ORI_DEV, :TS], picked[ORI_DEV:, TS:]], 0).astype(jnp.bfloat16)
    out_ref[...] = jnp.broadcast_to(both[None], out_ref.shape)
    for copy in copies:
        copy.wait()


def image_kernel(member_ref, own_ref, right_ref, below_ref, corner_ref, col_ref, row_ref, *rest):
    *out_refs, g_ref = rest

    def columns(first, second, start, count):
        g = dot(first, col_ref[:CORE]) + dot(second, col_ref[CORE:])
        g_ref[0, start : start + count] = g[:, :HALF].astype(jnp.bfloat16)
        g_ref[1, start : start + count] = g[:, HALF:].astype(jnp.bfloat16)

    columns(own_ref[...], right_ref[...], 0, CORE)
    columns(below_ref[...], corner_ref[...], CORE, TS)
    for s, bits in enumerate(ORDER):
        start = pl.multiple_of((member_ref[0] ^ bits) * ROWS, 32)
        piece = jnp.concatenate([g_ref[0, pl.ds(start, ROWS_IN)], g_ref[1, pl.ds(start, ROWS_IN)]], 0)
        out_refs[s][...] = dot(row_ref[...], piece).astype(jnp.bfloat16)


def template_kernel(pixels_ref, col_ref, row_ref, out_ref, shape_ref):
    values = pixels_ref[...].astype(jnp.float32).reshape(TS, ORI_DEV, TS)
    mean = jnp.sum(jnp.sum(values, 0), 1, keepdims=True) / (TS * TS)
    centered = values - mean[None]
    square = jnp.sum(jnp.sum(centered * centered, 0), 1, keepdims=True) / (TS * TS)
    spread = jnp.sqrt(square + 1e-06) * TS
    shape_ref[...] = (centered / spread[None]).reshape(TS * ORI_DEV, TS)
    for o in range(ORI_DEV):
        shape = shape_ref[pl.ds(o, TS, stride=ORI_DEV), :].astype(jnp.bfloat16)
        g = dot(shape, col_ref[...]).astype(jnp.bfloat16)
        g = jnp.concatenate([g[:, :HALF], g[:, HALF:]], 0)
        out_ref[o] = dot(row_ref[...], g).astype(jnp.bfloat16)


def block(image_ref, template_ref, inv_row_ref, inv_col_ref, out_ref, inner_ref):
    def part(ref, p):
        return ref[p * PAIRS : (p + 1) * PAIRS]

    for o in range(ORI_DEV):

        def cross(p):
            a, b = part(image_ref, 2 * p), part(image_ref, 2 * p + 1)
            c, d = part(template_ref.at[o], 2 * p), part(template_ref.at[o], 2 * p + 1)
            return a * c + b * d, b * c - a * d

        plus_re, plus_im = cross(0)
        minus_re, minus_im = cross(1)
        mixed = jnp.concatenate(
            [
                jnp.concatenate([plus_re + minus_re, plus_im + minus_im], 1),
                jnp.concatenate([minus_im - plus_im, plus_re - minus_re], 1),
            ],
            0,
        )
        inner_ref[o * ROWS : (o + 1) * ROWS] = dot(inv_row_ref[...], mixed).astype(jnp.bfloat16)
    corr = dot(inner_ref[...], inv_col_ref[...]).reshape(ORI_DEV, ROWS, CORE)
    out_ref[0] = jnp.max(corr, 0).astype(out_ref.dtype)
    out_ref[1] = jnp.sum(corr, 0).astype(out_ref.dtype)


def pair_kernel(first_ref, second_ref, template_ref, inv_row_ref, inv_col_ref, out_a, out_b, inner_a, inner_b):
    block(first_ref, template_ref, inv_row_ref, inv_col_ref, out_a, inner_a)
    block(second_ref, template_ref, inv_row_ref, inv_col_ref, out_b, inner_b)


def finish_kernel(own_ref, a_ref, b_ref, c_ref, peak_ref, excess_ref):
    others = [ref[...].astype(jnp.float32) for ref in (a_ref, b_ref, c_ref)]
    peak, total = own_ref[0], own_ref[1]
    for other in others:
        peak = jnp.maximum(peak, other[0])
        total = total + other[1]
    peak_ref[0] = peak
    excess_ref[0] = peak - total / (MEMBERS * ORI_DEV)


VMEM = pl.BlockSpec(memory_space=pltpu.VMEM)
SMEM = pl.BlockSpec(memory_space=pltpu.SMEM)
ANY = pl.BlockSpec(memory_space=pl.ANY)
LIMIT = 24 * 1024 * 1024
WHOLE = 60 * 1024 * 1024


def call(kernel, outs, specs, scratch=(), flops=0, out_specs=None, limit=LIMIT, moved=2**21):
    return pl.pallas_call(
        kernel,
        out_shape=outs,
        in_specs=specs,
        out_specs=out_specs or jax.tree.map(lambda _: VMEM, outs),
        scratch_shapes=list(scratch),
        compiler_params=pltpu.CompilerParams(vmem_limit_bytes=limit),
        cost_estimate=pl.CostEstimate(flops=flops, bytes_accessed=moved, transcendentals=0),
    )


def shape_of(dims, dtype=jnp.bfloat16):
    return jax.ShapeDtypeStruct(dims, dtype)


def halo(block, distance):
    route = []
    crosses = distance % GRID_W
    for t in range(TILES):
        source = t + distance
        if t % GRID_W + crosses < GRID_W and source < TILES:
            for o in range(MEMBERS):
                route.append((source * MEMBERS + (o ^ 2 if crosses else o), t * MEMBERS + o))
    return lax.ppermute(block, ("tile", "orient"), route)


def shards(micrograph, template_stack, orient_list):
    spread, right, below, corner = call(
        prepare_kernel,
        (
            shape_of((TILES, 2 * ORI_DEV, TS)),
            shape_of((CORE, TS)),
            shape_of((TS, CORE)),
            shape_of((TS, TS)),
        ),
        [SMEM, ANY, VMEM],
        [pltpu.SemaphoreType.DMA((3,))],
        out_specs=(VMEM, ANY, ANY, ANY),
        limit=WHOLE,
    )(orient_list, micrograph, template_stack)
    right = halo(right, 1)
    below = halo(below, GRID_W)
    corner = halo(corner, GRID_W + 1)
    pixels = lax.all_to_all(spread, "tile", 0, 0)
    columns = column_table()
    image = call(
        image_kernel,
        (shape_of((4 * PAIRS, HALF)),) * MEMBERS,
        [SMEM] + [VMEM] * 6,
        [pltpu.VMEM((2, TILE, HALF), jnp.bfloat16)],
        flops=20000000000,
    )(lax.axis_index("orient")[None], micrograph[0], right, below, corner, columns, row_table(ROWS_IN))
    templates = call(
        template_kernel,
        shape_of((ORI_DEV, 4 * PAIRS, HALF)),
        [VMEM] * 3,
        [pltpu.VMEM((TS * ORI_DEV, TS), jnp.float32)],
        flops=1000000000,
    )(pixels, columns[:TS], row_table(TS))
    inverse_rows, inverse_columns = inverse_row_table(), inverse_column_table()
    inner = pltpu.VMEM((ORI_DEV * ROWS, TILE), jnp.bfloat16)

    def pair(first, second, kind):
        return call(
            pair_kernel,
            (shape_of((2, ROWS, CORE)), shape_of((2, ROWS, CORE), kind)),
            [VMEM] * 5,
            [inner, inner],
            flops=2000000000,
        )(image[first], image[second], templates, inverse_rows, inverse_columns)

    def sent(piece, bits):
        return lax.ppermute(piece, "orient", [(i, i ^ bits) for i in range(MEMBERS)])

    far = pair(0, 1, jnp.bfloat16)
    near = pair(2, 3, jnp.float32)
    others = [sent(far[0], ORDER[0]), sent(far[1], ORDER[1]), sent(near[0], ORDER[2])]
    out = shape_of((1, ROWS, CORE), jnp.float32)
    return call(finish_kernel, (out, out), [VMEM] * 4)(near[1], *others)


def solution(mesh):
    placed = (P("tile", None, None), P(None, "tile"), P())
    return jax.shard_map(
        shards,
        mesh=mesh,
        in_specs=placed,
        out_specs=(P("tile", "orient", None), P("tile", "orient", None)),
        check_vma=False,
    )
```

```python
import math

import jax
import jax.numpy as jnp
import numpy as np
from jax import lax
from jax.experimental import pallas as pl
from jax.experimental.pallas import tpu as pltpu
from jax.sharding import PartitionSpec as P

TILE = 512
TS = 128
CORE = 384
GRID_W = 8
TILES = 64
ORI_DEV = 8
MEMBERS = 4
ROWS = 96
ROWS_IN = 224
LENGTH = 256
PAIRS = LENGTH // 2
HALF = TILE // 2
ORDER = (2, 3, 1, 0)


def bf16(table):
    return np.asarray(table, np.float64).astype(jnp.bfloat16)


def column_table():
    n = np.arange(TILE)[:, None]
    k = np.arange(HALF)[None, :]
    angle = (math.pi / TILE) * ((n * (2 * k + 1)) % (2 * TILE))
    return bf16(np.concatenate([np.cos(angle), -np.sin(angle)], 1))


def row_table(rows):
    j = np.arange(PAIRS)[:, None]
    m = np.arange(rows)[None, :]
    angle = (math.pi / LENGTH) * ((m * (2 * j + 1)) % (2 * LENGTH))
    c, s = np.cos(angle), np.sin(angle)
    return bf16(np.block([[c, s], [-s, c], [c, -s], [s, c]]))


def inverse_row_table():
    j = np.arange(PAIRS)[None, :]
    c = np.arange(ROWS)[:, None]
    angle = (math.pi / LENGTH) * ((c * (2 * j + 1)) % (2 * LENGTH))
    return bf16(np.concatenate([np.cos(angle), np.sin(angle)], 1))


def inverse_column_table():
    k = np.arange(HALF)[:, None]
    c = np.arange(CORE)[None, :]
    angle = (math.pi / TILE) * ((c * (2 * k + 1)) % (2 * TILE))
    scale = 2.0 / (LENGTH * TILE)
    return bf16(np.concatenate([np.cos(angle), -np.sin(angle)], 0) * scale)


def dot(a, b):
    return jnp.dot(a, b, preferred_element_type=jnp.float32)


def prepare_kernel(ids_ref, micro_hbm, stack_hbm, out_ref, right_ref, below_ref, corner_ref, micro_ref, stack_ref, sems):
    load_stack = pltpu.make_async_copy(stack_hbm, stack_ref, sems.at[0])
    load_micro = pltpu.make_async_copy(micro_hbm.at[0], micro_ref, sems.at[1])
    load_stack.start()
    load_micro.start()
    row = lax.broadcasted_iota(jnp.int32, (2 * ORI_DEV, 256), 0)
    lane = lax.broadcasted_iota(jnp.int32, (2 * ORI_DEV, 256), 1)
    wanted = jnp.zeros((2 * ORI_DEV, 256), jnp.int32)
    first = lax.axis_index("orient") * ORI_DEV
    for o in range(ORI_DEV):
        wanted = jnp.where(row % ORI_DEV == o, ids_ref[first + o], wanted)
    hot = jnp.where(lane == wanted, 1.0, 0.0).astype(jnp.bfloat16)
    load_stack.wait()
    picked = dot(hot, stack_ref[...])
    both = jnp.concatenate([picked[:ORI_DEV, :TS], picked[ORI_DEV:, TS:]], 0).astype(jnp.bfloat16)
    out_ref[...] = jnp.broadcast_to(both[None], out_ref.shape)
    load_micro.wait()
    right_ref[...] = micro_ref[:, :TS]
    below_ref[...] = micro_ref[:TS, :]
    corner_ref[...] = micro_ref[:TS, :TS]


def image_spectra(member_ref, own_ref, right_ref, below_ref, corner_ref, col_ref, row_ref, out_refs, g_ref):
    def columns(first, second, start, count):
        g = dot(first, col_ref[:CORE]) + dot(second, col_ref[CORE:])
        g_ref[0, start : start + count] = g[:, :HALF].astype(jnp.bfloat16)
        g_ref[1, start : start + count] = g[:, HALF:].astype(jnp.bfloat16)

    columns(own_ref[0], right_ref[...], 0, CORE)
    columns(below_ref[...], corner_ref[...], CORE, TS)
    for s, bits in enumerate(ORDER):
        start = pl.multiple_of((member_ref[0] ^ bits) * ROWS, 32)
        piece = jnp.concatenate([g_ref[0, pl.ds(start, ROWS_IN)], g_ref[1, pl.ds(start, ROWS_IN)]], 0)
        out_refs[s][...] = dot(row_ref[...], piece).astype(jnp.bfloat16)


def template_kernel(pixels_ref, col_hbm, row_hbm, out_ref, shape_ref, col_ref, row_ref, sems):
    loads = [
        pltpu.make_async_copy(col_hbm, col_ref, sems.at[0]),
        pltpu.make_async_copy(row_hbm, row_ref, sems.at[1]),
    ]
    for load in loads:
        load.start()
    values = pixels_ref[...].astype(jnp.float32).reshape(TS, ORI_DEV, TS)
    mean = jnp.sum(jnp.sum(values, 0), 1, keepdims=True) / (TS * TS)
    centered = values - mean[None]
    square = jnp.sum(jnp.sum(centered * centered, 0), 1, keepdims=True) / (TS * TS)
    spread = jnp.sqrt(square + 1e-06) * TS
    shape_ref[...] = (centered / spread[None]).reshape(TS * ORI_DEV, TS)
    for load in loads:
        load.wait()
    for o in range(ORI_DEV):
        shape = shape_ref[pl.ds(o, TS, stride=ORI_DEV), :].astype(jnp.bfloat16)
        g = dot(shape, col_ref[...]).astype(jnp.bfloat16)
        g = jnp.concatenate([g[:, :HALF], g[:, HALF:]], 0)
        out_ref[o] = dot(row_ref[...], g).astype(jnp.bfloat16)


def block(image_ref, template_ref, inv_row_ref, inv_col_ref, out_ref, inner_ref):
    def part(ref, p):
        return ref[p * PAIRS : (p + 1) * PAIRS]

    for o in range(ORI_DEV):

        def cross(p):
            a, b = part(image_ref, 2 * p), part(image_ref, 2 * p + 1)
            c, d = part(template_ref.at[o], 2 * p), part(template_ref.at[o], 2 * p + 1)
            return a * c + b * d, b * c - a * d

        plus_re, plus_im = cross(0)
        minus_re, minus_im = cross(1)
        mixed = jnp.concatenate(
            [
                jnp.concatenate([plus_re + minus_re, plus_im + minus_im], 1),
                jnp.concatenate([minus_im - plus_im, plus_re - minus_re], 1),
            ],
            0,
        )
        inner_ref[o * ROWS : (o + 1) * ROWS] = dot(inv_row_ref[...], mixed).astype(jnp.bfloat16)
    corr = dot(inner_ref[...], inv_col_ref[...]).reshape(ORI_DEV, ROWS, CORE)
    out_ref[0] = jnp.max(corr, 0).astype(out_ref.dtype)
    out_ref[1] = jnp.sum(corr, 0).astype(out_ref.dtype)


def image_kernel(*refs):
    image_spectra(*refs[:7], refs[8:12], refs[12])


def pair_kernel(first_ref, second_ref, template_ref, inv_row_ref, inv_col_ref, out_a, out_b, inner_a, inner_b):
    block(first_ref, template_ref, inv_row_ref, inv_col_ref, out_a, inner_a)
    block(second_ref, template_ref, inv_row_ref, inv_col_ref, out_b, inner_b)


def finish_kernel(own_ref, a_ref, b_ref, c_ref, peak_ref, excess_ref):
    others = [ref[...].astype(jnp.float32) for ref in (a_ref, b_ref, c_ref)]
    peak, total = own_ref[0], own_ref[1]
    for other in others:
        peak = jnp.maximum(peak, other[0])
        total = total + other[1]
    peak_ref[0] = peak
    excess_ref[0] = peak - total / (MEMBERS * ORI_DEV)


VMEM = pl.BlockSpec(memory_space=pltpu.VMEM)
SMEM = pl.BlockSpec(memory_space=pltpu.SMEM)
ANY = pl.BlockSpec(memory_space=pl.ANY)
HBM = pl.BlockSpec(memory_space=pltpu.HBM)
LIMIT = 24 * 1024 * 1024


def call(kernel, outs, specs, scratch=(), flops=0):
    return pl.pallas_call(
        kernel,
        out_shape=outs,
        in_specs=specs,
        out_specs=jax.tree.map(lambda _: VMEM, outs),
        scratch_shapes=list(scratch),
        compiler_params=pltpu.CompilerParams(vmem_limit_bytes=LIMIT),
        cost_estimate=pl.CostEstimate(flops=flops, bytes_accessed=2**21, transcendentals=0),
    )


def shape_of(dims, dtype=jnp.bfloat16):
    return jax.ShapeDtypeStruct(dims, dtype)


def pinned(array):
    return pltpu.with_memory_space_constraint(jnp.asarray(array), pltpu.HBM)


def halo(block, distance):
    route = []
    crosses = distance % GRID_W
    for t in range(TILES):
        source = t + distance
        if t % GRID_W + crosses < GRID_W and source < TILES:
            for o in range(MEMBERS):
                route.append((source * MEMBERS + (o ^ 2 if crosses else o), t * MEMBERS + o))
    return lax.ppermute(block, ("tile", "orient"), route)


def shards(micrograph, template_stack, orient_list):
    spread, right, below, corner = call(
        prepare_kernel,
        (
            shape_of((TILES, 2 * ORI_DEV, TS)),
            shape_of((CORE, TS)),
            shape_of((TS, CORE)),
            shape_of((TS, TS)),
        ),
        [SMEM, HBM, HBM],
        [
            pltpu.VMEM((CORE, CORE), jnp.bfloat16),
            pltpu.VMEM((256, 256), jnp.bfloat16),
            pltpu.SemaphoreType.DMA((2,)),
        ],
    )(orient_list, pinned(micrograph), pinned(template_stack))
    pixels = lax.all_to_all(spread, "tile", 0, 0)
    right = halo(right, 1)
    below = halo(below, GRID_W)
    corner = halo(corner, GRID_W + 1)
    columns = column_table()
    templates = call(
        template_kernel,
        shape_of((ORI_DEV, 4 * PAIRS, HALF)),
        [VMEM, HBM, HBM],
        [
            pltpu.VMEM((TS * ORI_DEV, TS), jnp.float32),
            pltpu.VMEM((TS, TILE), jnp.bfloat16),
            pltpu.VMEM((4 * PAIRS, 2 * TS), jnp.bfloat16),
            pltpu.SemaphoreType.DMA((2,)),
        ],
        flops=1000000000,
    )(pixels, pinned(columns[:TS]), pinned(row_table(TS)))
    image = call(
        image_kernel,
        (shape_of((4 * PAIRS, HALF)),) * MEMBERS,
        [SMEM] + [VMEM] * 6 + [ANY],
        [pltpu.VMEM((2, TILE, HALF), jnp.bfloat16)],
        flops=1600000000,
    )(lax.axis_index("orient")[None], micrograph, right, below, corner, columns, row_table(ROWS_IN), templates)
    tables = inverse_row_table(), inverse_column_table()
    inner = pltpu.VMEM((ORI_DEV * ROWS, TILE), jnp.bfloat16)

    def pair(first, second, kind):
        return call(
            pair_kernel,
            (shape_of((2, ROWS, CORE)), shape_of((2, ROWS, CORE), kind)),
            [VMEM] * 5,
            [inner, inner],
            flops=2000000000,
        )(image[first], image[second], templates, *tables)

    def sent(piece, bits):
        return lax.ppermute(piece, "orient", [(i, i ^ bits) for i in range(MEMBERS)])

    far = pair(0, 1, jnp.bfloat16)
    near = pair(2, 3, jnp.float32)
    others = [sent(far[0], ORDER[0]), sent(far[1], ORDER[1]), sent(near[0], ORDER[2])]
    out = shape_of((1, ROWS, CORE), jnp.float32)
    return call(finish_kernel, (out, out), [VMEM] * 4)(near[1], *others)


def solution(mesh):
    placed = (P("tile", None, None), P(None, "tile"), P())
    return jax.shard_map(
        shards,
        mesh=mesh,
        in_specs=placed,
        out_specs=(P("tile", "orient", None), P("tile", "orient", None)),
        check_vma=False,
    )
```

```python
import math

import jax
import jax.numpy as jnp
import numpy as np
from jax import lax
from jax.experimental import pallas as pl
from jax.experimental.pallas import tpu as pltpu
from jax.sharding import PartitionSpec as P

TILE = 512
TS = 128
CORE = 384
GRID_W = 8
TILES = 64
ORI_DEV = 8
MEMBERS = 4
ROWS = 96
ROWS_IN = 224
LENGTH = 256
PAIRS = LENGTH // 2
HALF = TILE // 2
ORDER = (2, 3, 1, 0)


def bf16(table):
    return np.asarray(table, np.float64).astype(jnp.bfloat16)


def column_table():
    n = np.arange(TILE)[:, None]
    k = np.arange(HALF)[None, :]
    angle = (math.pi / TILE) * ((n * (2 * k + 1)) % (2 * TILE))
    return bf16(np.concatenate([np.cos(angle), -np.sin(angle)], 1))


def row_table():
    j = np.arange(PAIRS)[:, None]
    m = np.arange(ROWS_IN)[None, :]
    angle = (math.pi / LENGTH) * ((m * (2 * j + 1)) % (2 * LENGTH))
    c, s = np.cos(angle), np.sin(angle)
    parts = []
    for cut in (slice(0, TS), slice(TS, ROWS_IN)):
        u, v = c[:, cut], s[:, cut]
        parts.append(np.block([[u, v], [-v, u], [u, -v], [v, u]]))
    return bf16(np.concatenate(parts, 1))


def inverse_row_table():
    j = np.arange(PAIRS)[None, :]
    c = np.arange(ROWS)[:, None]
    angle = (math.pi / LENGTH) * ((c * (2 * j + 1)) % (2 * LENGTH))
    return bf16(np.concatenate([np.cos(angle), np.sin(angle)], 1))


def inverse_column_table():
    k = np.arange(HALF)[:, None]
    c = np.arange(CORE)[None, :]
    angle = (math.pi / TILE) * ((c * (2 * k + 1)) % (2 * TILE))
    scale = 2.0 / (LENGTH * TILE)
    return bf16(np.concatenate([np.cos(angle), -np.sin(angle)], 0) * scale)


def dot(a, b):
    return jnp.dot(a, b, preferred_element_type=jnp.float32)


def prepare_kernel(
    ids_hbm, micro_hbm, stack_hbm, out_hbm, right_ref, below_ref, corner_ref, ids_ref, micro_ref, stack_ref, out_ref, sems
):
    load_ids = pltpu.make_async_copy(ids_hbm, ids_ref, sems.at[0])
    load_stack = pltpu.make_async_copy(stack_hbm, stack_ref, sems.at[1])
    load_micro = pltpu.make_async_copy(micro_hbm.at[0], micro_ref, sems.at[2])
    load_ids.start()
    load_stack.start()
    load_micro.start()
    row = lax.broadcasted_iota(jnp.int32, (2 * ORI_DEV, 256), 0)
    lane = lax.broadcasted_iota(jnp.int32, (2 * ORI_DEV, 256), 1)
    wanted = jnp.zeros((2 * ORI_DEV, 256), jnp.int32)
    first = lax.axis_index("orient") * ORI_DEV
    load_ids.wait()
    for o in range(ORI_DEV):
        wanted = jnp.where(row % ORI_DEV == o, ids_ref[first + o], wanted)
    hot = jnp.where(lane == wanted, 1.0, 0.0).astype(jnp.bfloat16)
    load_stack.wait()
    picked = dot(hot, stack_ref[...])
    both = jnp.concatenate([picked[:ORI_DEV, :TS], picked[ORI_DEV:, TS:]], 0).astype(jnp.bfloat16)
    out_ref[...] = jnp.broadcast_to(both[None], out_ref.shape)
    store = pltpu.make_async_copy(out_ref, out_hbm, sems.at[3])
    store.start()
    load_micro.wait()
    right_ref[...] = micro_ref[:, :TS]
    below_ref[...] = micro_ref[:TS, :]
    corner_ref[...] = micro_ref[:TS, :TS]
    store.wait()


def load_kernel(*refs):
    sources, targets, sems = refs[:5], refs[6:11], refs[11]
    loads = [pltpu.make_async_copy(a, b, sems.at[i]) for i, (a, b) in enumerate(zip(sources, targets))]
    for load in loads:
        load.start()
    for load in loads:
        load.wait()


def template_kernel(pixels_ref, col_ref, row_ref, out_ref, shape_ref):
    values = pixels_ref[...].astype(jnp.float32).reshape(TS, ORI_DEV, TS)
    mean = jnp.sum(jnp.sum(values, 0), 1, keepdims=True) / (TS * TS)
    centered = values - mean[None]
    square = jnp.sum(jnp.sum(centered * centered, 0), 1, keepdims=True) / (TS * TS)
    spread = jnp.sqrt(square + 1e-06) * TS
    shape_ref[...] = (centered / spread[None]).reshape(TS * ORI_DEV, TS)
    shapes = [shape_ref[pl.ds(o, TS, stride=ORI_DEV), :].astype(jnp.bfloat16) for o in range(ORI_DEV)]
    half = ORI_DEV // 2
    for start in (0, half):
        together = jnp.concatenate(shapes[start : start + half], 0)
        g = dot(together, col_ref[:TS]).astype(jnp.bfloat16)
        for o in range(half):
            mine = g[o * TS : (o + 1) * TS]
            mine = jnp.concatenate([mine[:, :HALF], mine[:, HALF:]], 0)
            out_ref[start + o] = dot(row_ref[:, : 2 * TS], mine).astype(jnp.bfloat16)


def image_columns(own_ref, right_ref, below_ref, corner_ref, col_ref, g_ref):
    def columns(first, second, start, count):
        g = dot(first, col_ref[:CORE]) + dot(second, col_ref[CORE:])
        g_ref[0, start : start + count] = g[:, :HALF].astype(jnp.bfloat16)
        g_ref[1, start : start + count] = g[:, HALF:].astype(jnp.bfloat16)

    columns(own_ref[0], right_ref[...], 0, CORE)
    columns(below_ref[...], corner_ref[...], CORE, TS)


def image_rows(member_ref, row_ref, g_ref, bits, out_ref):
    start = pl.multiple_of((member_ref[0] ^ bits) * ROWS, 32)
    cuts = [(start, TS), (pl.multiple_of(start + TS, 32), ROWS_IN - TS)]
    piece = jnp.concatenate([g_ref[p, pl.ds(*cut)] for cut in cuts for p in range(2)], 0)
    out_ref[...] = dot(row_ref[...], piece).astype(jnp.bfloat16)


def block(image_ref, template_ref, inv_row_ref, inv_col_ref, out_ref, inner_ref):
    def part(ref, p):
        return ref[p * PAIRS : (p + 1) * PAIRS]

    for o in range(ORI_DEV):

        def cross(p):
            a, b = part(image_ref, 2 * p), part(image_ref, 2 * p + 1)
            c, d = part(template_ref.at[o], 2 * p), part(template_ref.at[o], 2 * p + 1)
            return a * c + b * d, b * c - a * d

        plus_re, plus_im = cross(0)
        minus_re, minus_im = cross(1)
        mixed = jnp.concatenate(
            [
                jnp.concatenate([plus_re + minus_re, plus_im + minus_im], 1),
                jnp.concatenate([minus_im - plus_im, plus_re - minus_re], 1),
            ],
            0,
        )
        inner_ref[o * ROWS : (o + 1) * ROWS] = dot(inv_row_ref[...], mixed).astype(jnp.bfloat16)
    corr = dot(inner_ref[...], inv_col_ref[...]).reshape(ORI_DEV, ROWS, CORE)
    out_ref[0] = jnp.max(corr, 0).astype(out_ref.dtype)
    out_ref[1] = jnp.sum(corr, 0).astype(out_ref.dtype)


def image_kernel(member_ref, *refs):
    own_ref, right_ref, below_ref, corner_ref, col_ref, row_ref, *out_refs, g_ref = refs
    image_columns(own_ref, right_ref, below_ref, corner_ref, col_ref, g_ref)
    for bits, out_ref in zip(ORDER, out_refs):
        image_rows(member_ref, row_ref, g_ref, bits, out_ref)


def pair_kernel(first_ref, second_ref, template_ref, inv_row_ref, inv_col_ref, out_a, out_b, inner_a, inner_b):
    block(first_ref, template_ref, inv_row_ref, inv_col_ref, out_a, inner_a)
    block(second_ref, template_ref, inv_row_ref, inv_col_ref, out_b, inner_b)


def finish_kernel(own_ref, a_ref, b_ref, c_ref, peak_ref, excess_ref):
    others = [ref[...].astype(jnp.float32) for ref in (a_ref, b_ref, c_ref)]
    peak, total = own_ref[0], own_ref[1]
    for other in others:
        peak = jnp.maximum(peak, other[0])
        total = total + other[1]
    peak_ref[0] = peak
    excess_ref[0] = peak - total / (MEMBERS * ORI_DEV)


VMEM = pl.BlockSpec(memory_space=pltpu.VMEM)
SMEM = pl.BlockSpec(memory_space=pltpu.SMEM)
ANY = pl.BlockSpec(memory_space=pl.ANY)
HBM = pl.BlockSpec(memory_space=pltpu.HBM)
LIMIT = 24 * 1024 * 1024


def call(kernel, outs, specs, scratch=(), flops=0, out_specs=None):
    return pl.pallas_call(
        kernel,
        out_shape=outs,
        in_specs=specs,
        out_specs=out_specs or jax.tree.map(lambda _: VMEM, outs),
        scratch_shapes=list(scratch),
        compiler_params=pltpu.CompilerParams(vmem_limit_bytes=LIMIT),
        cost_estimate=pl.CostEstimate(flops=flops, bytes_accessed=2**21, transcendentals=0),
    )


def shape_of(dims, dtype=jnp.bfloat16):
    return jax.ShapeDtypeStruct(dims, dtype)


def pinned(array):
    return pltpu.with_memory_space_constraint(jnp.asarray(array), pltpu.HBM)


def halo(block, distance):
    route = []
    crosses = distance % GRID_W
    for t in range(TILES):
        source = t + distance
        if t % GRID_W + crosses < GRID_W and source < TILES:
            for o in range(MEMBERS):
                route.append((source * MEMBERS + (o ^ 2 if crosses else o), t * MEMBERS + o))
    return lax.ppermute(block, ("tile", "orient"), route)


def shards(micrograph, template_stack, orient_list):
    spread, right, below, corner = call(
        prepare_kernel,
        (
            shape_of((TILES, 2 * ORI_DEV, TS)),
            shape_of((CORE, TS)),
            shape_of((TS, CORE)),
            shape_of((TS, TS)),
        ),
        [HBM] * 3,
        [
            pltpu.SMEM((MEMBERS * ORI_DEV,), jnp.int32),
            pltpu.VMEM((CORE, CORE), jnp.bfloat16),
            pltpu.VMEM((256, 256), jnp.bfloat16),
            pltpu.VMEM((TILES, 2 * ORI_DEV, TS), jnp.bfloat16),
            pltpu.SemaphoreType.DMA((4,)),
        ],
        out_specs=(HBM, VMEM, VMEM, VMEM),
    )(pinned(orient_list), pinned(micrograph), pinned(template_stack))
    pixels = lax.all_to_all(spread, "tile", 0, 0)
    kept = [column_table(), row_table(), inverse_row_table(), inverse_column_table(), micrograph]
    columns, rows, *tables, own_block = call(
        load_kernel,
        tuple(shape_of(array.shape) for array in kept),
        [HBM] * 5 + [ANY],
        [pltpu.SemaphoreType.DMA((5,))],
        flops=1000000000,
    )(*[pinned(array) for array in kept], corner)
    right = halo(right, 1)
    below = halo(below, GRID_W)
    corner = halo(corner, GRID_W + 1)
    member = lax.axis_index("orient")[None]
    templates = call(
        template_kernel,
        shape_of((ORI_DEV, 4 * PAIRS, HALF)),
        [VMEM] * 3,
        [pltpu.VMEM((TS * ORI_DEV, TS), jnp.float32)],
        flops=1000000000,
    )(pixels, columns, rows)
    image = call(
        image_kernel,
        (shape_of((4 * PAIRS, HALF)),) * MEMBERS,
        [SMEM] + [VMEM] * 6,
        [pltpu.VMEM((2, TILE, HALF), jnp.bfloat16)],
        flops=1600000000,
    )(member, own_block, right, below, corner, columns, rows)
    inner = pltpu.VMEM((ORI_DEV * ROWS, TILE), jnp.bfloat16)

    def pair(first, second, kind):
        return call(
            pair_kernel,
            (shape_of((2, ROWS, CORE)), shape_of((2, ROWS, CORE), kind)),
            [VMEM] * 5,
            [inner, inner],
            flops=2000000000,
        )(image[first], image[second], templates, *tables)

    def sent(piece, bits):
        return lax.ppermute(piece, "orient", [(i, i ^ bits) for i in range(MEMBERS)])

    far = pair(0, 1, jnp.bfloat16)
    near = pair(2, 3, jnp.float32)
    others = [sent(far[0], ORDER[0]), sent(far[1], ORDER[1]), sent(near[0], ORDER[2])]
    out = shape_of((1, ROWS, CORE), jnp.float32)
    return call(finish_kernel, (out, out), [VMEM] * 4)(near[1], *others)


def solution(mesh):
    placed = (P("tile", None, None), P(None, "tile"), P())
    return jax.shard_map(
        shards,
        mesh=mesh,
        in_specs=placed,
        out_specs=(P("tile", "orient", None), P("tile", "orient", None)),
        check_vma=False,
    )
```

```python
import math

import jax
import jax.numpy as jnp
import numpy as np
from jax import lax
from jax.experimental import pallas as pl
from jax.experimental.pallas import tpu as pltpu
from jax.sharding import PartitionSpec as P

TILE = 512
TS = 128
CORE = 384
GRID_W = 8
TILES = 64
ORI_DEV = 8
MEMBERS = 4
ROWS = 96
ROWS_IN = 224
LENGTH = 256
PAIRS = LENGTH // 2
HALF = TILE // 2
CORE_BIT, CHIP_BIT = 1, 2


def bf16(table):
    return np.asarray(table, np.float64).astype(jnp.bfloat16)


def column_table():
    n = np.arange(TILE)[:, None]
    k = np.arange(HALF)[None, :]
    angle = (math.pi / TILE) * ((n * (2 * k + 1)) % (2 * TILE))
    return bf16(np.concatenate([np.cos(angle), -np.sin(angle)], 1))


def row_table():
    j = np.arange(PAIRS)[:, None]
    m = np.arange(ROWS_IN)[None, :]
    angle = (math.pi / LENGTH) * ((m * (2 * j + 1)) % (2 * LENGTH))
    c, s = np.cos(angle), np.sin(angle)
    parts = []
    for cut in (slice(0, TS), slice(TS, ROWS_IN)):
        u, v = c[:, cut], s[:, cut]
        parts.append(np.block([[u, v], [-v, u], [u, -v], [v, u]]))
    return bf16(np.concatenate(parts, 1))


def inverse_row_table():
    j = np.arange(PAIRS)[None, :]
    c = np.arange(ROWS)[:, None]
    angle = (math.pi / LENGTH) * ((c * (2 * j + 1)) % (2 * LENGTH))
    return bf16(np.concatenate([np.cos(angle), np.sin(angle)], 1))


def inverse_column_table():
    k = np.arange(HALF)[:, None]
    c = np.arange(CORE)[None, :]
    angle = (math.pi / TILE) * ((c * (2 * k + 1)) % (2 * TILE))
    scale = 2.0 / (LENGTH * TILE)
    return bf16(np.concatenate([np.cos(angle), -np.sin(angle)], 0) * scale)


def dot(a, b):
    return jnp.dot(a, b, preferred_element_type=jnp.float32)


def prepare_kernel(
    ids_hbm, micro_hbm, stack_hbm, out_hbm, right_ref, below_ref, corner_ref, ids_ref, micro_ref, stack_ref, out_ref, sems
):
    load_ids = pltpu.make_async_copy(ids_hbm, ids_ref, sems.at[0])
    load_stack = pltpu.make_async_copy(stack_hbm, stack_ref, sems.at[1])
    load_micro = pltpu.make_async_copy(micro_hbm.at[0], micro_ref, sems.at[2])
    load_ids.start()
    load_stack.start()
    load_micro.start()
    row = lax.broadcasted_iota(jnp.int32, (2 * ORI_DEV, 256), 0)
    lane = lax.broadcasted_iota(jnp.int32, (2 * ORI_DEV, 256), 1)
    wanted = jnp.zeros((2 * ORI_DEV, 256), jnp.int32)
    first = lax.axis_index("orient") * ORI_DEV
    load_ids.wait()
    for o in range(ORI_DEV):
        wanted = jnp.where(row % ORI_DEV == o, ids_ref[first + o], wanted)
    hot = jnp.where(lane == wanted, 1.0, 0.0).astype(jnp.bfloat16)
    load_stack.wait()
    picked = dot(hot, stack_ref[...])
    both = jnp.concatenate([picked[:ORI_DEV, :TS], picked[ORI_DEV:, TS:]], 0).astype(jnp.bfloat16)
    out_ref[...] = jnp.broadcast_to(both[None], out_ref.shape)
    store = pltpu.make_async_copy(out_ref, out_hbm, sems.at[3])
    store.start()
    load_micro.wait()
    right_ref[...] = micro_ref[:, :TS]
    below_ref[...] = micro_ref[:TS, :]
    corner_ref[...] = micro_ref[:TS, :TS]
    store.wait()


def load_kernel(*refs):
    sources, targets, sems = refs[:5], refs[6:11], refs[11]
    loads = [pltpu.make_async_copy(a, b, sems.at[i]) for i, (a, b) in enumerate(zip(sources, targets))]
    for load in loads:
        load.start()
    for load in loads:
        load.wait()


def template_kernel(pixels_ref, col_ref, row_ref, out_ref, shape_ref):
    values = pixels_ref[...].astype(jnp.float32).reshape(TS, ORI_DEV, TS)
    mean = jnp.sum(jnp.sum(values, 0), 1, keepdims=True) / (TS * TS)
    centered = values - mean[None]
    square = jnp.sum(jnp.sum(centered * centered, 0), 1, keepdims=True) / (TS * TS)
    spread = jnp.sqrt(square + 1e-06) * TS
    shape_ref[...] = (centered / spread[None]).reshape(TS * ORI_DEV, TS)
    shapes = [shape_ref[pl.ds(o, TS, stride=ORI_DEV), :].astype(jnp.bfloat16) for o in range(ORI_DEV)]
    half = ORI_DEV // 2
    for start in (0, half):
        together = jnp.concatenate(shapes[start : start + half], 0)
        g = dot(together, col_ref[:TS]).astype(jnp.bfloat16)
        for o in range(half):
            mine = g[o * TS : (o + 1) * TS]
            mine = jnp.concatenate([mine[:, :HALF], mine[:, HALF:]], 0)
            out_ref[start + o] = dot(row_ref[:, : 2 * TS], mine).astype(jnp.bfloat16)


def image_columns(own_ref, right_ref, below_ref, corner_ref, col_ref, g_ref):
    def columns(first, second, start, count):
        g = dot(first, col_ref[:CORE]) + dot(second, col_ref[CORE:])
        g_ref[0, start : start + count] = g[:, :HALF].astype(jnp.bfloat16)
        g_ref[1, start : start + count] = g[:, HALF:].astype(jnp.bfloat16)

    columns(own_ref[0], right_ref[...], 0, CORE)
    columns(below_ref[...], corner_ref[...], CORE, TS)


def image_rows(member_ref, row_ref, g_ref, bits, out_ref):
    start = pl.multiple_of((member_ref[0] ^ bits) * ROWS, 32)
    cuts = [(start, TS), (pl.multiple_of(start + TS, 32), ROWS_IN - TS)]
    piece = jnp.concatenate([g_ref[p, pl.ds(*cut)] for cut in cuts for p in range(2)], 0)
    out_ref[...] = dot(row_ref[...], piece).astype(jnp.bfloat16)


def block(image_ref, template_refs, inv_row_ref, inv_col_ref, out_ref, inner_ref):
    def part(ref, p):
        return ref[p * PAIRS : (p + 1) * PAIRS]

    def corr(template_ref):
        for o in range(ORI_DEV):

            def cross(p):
                a, b = part(image_ref, 2 * p), part(image_ref, 2 * p + 1)
                c, d = part(template_ref.at[o], 2 * p), part(template_ref.at[o], 2 * p + 1)
                return a * c + b * d, b * c - a * d

            plus_re, plus_im = cross(0)
            minus_re, minus_im = cross(1)
            mixed = jnp.concatenate(
                [
                    jnp.concatenate([plus_re + minus_re, plus_im + minus_im], 1),
                    jnp.concatenate([minus_im - plus_im, plus_re - minus_re], 1),
                ],
                0,
            )
            inner_ref[o * ROWS : (o + 1) * ROWS] = dot(inv_row_ref[...], mixed).astype(jnp.bfloat16)
        out = dot(inner_ref[...], inv_col_ref[...]).reshape(ORI_DEV, ROWS, CORE)
        return jnp.max(out, 0), jnp.sum(out, 0)

    high_a, sum_a = corr(template_refs[0])
    high_b, sum_b = corr(template_refs[1])
    out_ref[0] = jnp.maximum(high_a, high_b).astype(out_ref.dtype)
    out_ref[1] = (sum_a + sum_b).astype(out_ref.dtype)


def image_kernel(member_ref, *refs):
    own_ref, right_ref, below_ref, corner_ref, col_ref, row_ref, far_ref, near_ref, g_ref = refs
    image_columns(own_ref, right_ref, below_ref, corner_ref, col_ref, g_ref)
    image_rows(member_ref, row_ref, g_ref, CHIP_BIT, far_ref)
    image_rows(member_ref, row_ref, g_ref, 0, near_ref)


def block_kernel(image_ref, mine_ref, other_ref, inv_row_ref, inv_col_ref, out_ref, inner_ref):
    block(image_ref, (mine_ref, other_ref), inv_row_ref, inv_col_ref, out_ref, inner_ref)


def finish_kernel(own_ref, far_ref, peak_ref, excess_ref):
    far = far_ref[...].astype(jnp.float32)
    peak = jnp.maximum(own_ref[0], far[0])
    peak_ref[0] = peak
    excess_ref[0] = peak - (own_ref[1] + far[1]) / (MEMBERS * ORI_DEV)


VMEM = pl.BlockSpec(memory_space=pltpu.VMEM)
SMEM = pl.BlockSpec(memory_space=pltpu.SMEM)
ANY = pl.BlockSpec(memory_space=pl.ANY)
HBM = pl.BlockSpec(memory_space=pltpu.HBM)
LIMIT = 24 * 1024 * 1024


def call(kernel, outs, specs, scratch=(), flops=0, out_specs=None):
    return pl.pallas_call(
        kernel,
        out_shape=outs,
        in_specs=specs,
        out_specs=out_specs or jax.tree.map(lambda _: VMEM, outs),
        scratch_shapes=list(scratch),
        compiler_params=pltpu.CompilerParams(vmem_limit_bytes=LIMIT),
        cost_estimate=pl.CostEstimate(flops=flops, bytes_accessed=2**21, transcendentals=0),
    )


def shape_of(dims, dtype=jnp.bfloat16):
    return jax.ShapeDtypeStruct(dims, dtype)


def pinned(array):
    return pltpu.with_memory_space_constraint(jnp.asarray(array), pltpu.HBM)


def halo(block, distance):
    route = []
    crosses = distance % GRID_W
    for t in range(TILES):
        source = t + distance
        if t % GRID_W + crosses < GRID_W and source < TILES:
            for o in range(MEMBERS):
                route.append((source * MEMBERS + (o ^ 2 if crosses else o), t * MEMBERS + o))
    return lax.ppermute(block, ("tile", "orient"), route)


def shards(micrograph, template_stack, orient_list):
    spread, right, below, corner = call(
        prepare_kernel,
        (
            shape_of((TILES, 2 * ORI_DEV, TS)),
            shape_of((CORE, TS)),
            shape_of((TS, CORE)),
            shape_of((TS, TS)),
        ),
        [HBM] * 3,
        [
            pltpu.SMEM((MEMBERS * ORI_DEV,), jnp.int32),
            pltpu.VMEM((CORE, CORE), jnp.bfloat16),
            pltpu.VMEM((256, 256), jnp.bfloat16),
            pltpu.VMEM((TILES, 2 * ORI_DEV, TS), jnp.bfloat16),
            pltpu.SemaphoreType.DMA((4,)),
        ],
        out_specs=(HBM, VMEM, VMEM, VMEM),
    )(pinned(orient_list), pinned(micrograph), pinned(template_stack))
    pixels = lax.all_to_all(spread, "tile", 0, 0)
    kept = [column_table(), row_table(), inverse_row_table(), inverse_column_table(), micrograph]
    columns, rows, *tables, own_block = call(
        load_kernel,
        tuple(shape_of(array.shape) for array in kept),
        [HBM] * 5 + [ANY],
        [pltpu.SemaphoreType.DMA((5,))],
        flops=1000000000,
    )(*[pinned(array) for array in kept], corner)
    right = halo(right, 1)
    below = halo(below, GRID_W)
    corner = halo(corner, GRID_W + 1)
    member = lax.axis_index("orient")[None]

    def sent(piece, bits):
        return lax.ppermute(piece, "orient", [(i, i ^ bits) for i in range(MEMBERS)])

    templates = [
        call(
            template_kernel,
            shape_of((ORI_DEV, 4 * PAIRS, HALF)),
            [VMEM] * 3,
            [pltpu.VMEM((TS * ORI_DEV, TS), jnp.float32)],
            flops=10000000000,
        )(group, columns, rows)
        for group in (pixels, sent(pixels, CORE_BIT))
    ]
    spectra = shape_of((4 * PAIRS, HALF))
    image = call(
        image_kernel,
        (spectra, spectra),
        [SMEM] + [VMEM] * 6,
        [pltpu.VMEM((2, TILE, HALF), jnp.bfloat16)],
        flops=1600000000,
    )(member, own_block, right, below, corner, columns, rows)
    far, own = [
        call(
            block_kernel,
            shape_of((2, ROWS, CORE), kind),
            [VMEM] * 5,
            [pltpu.VMEM((ORI_DEV * ROWS, TILE), jnp.bfloat16)],
            flops=2000000000,
        )(spectrum, *templates, *tables)
        for spectrum, kind in zip(image, (jnp.bfloat16, jnp.float32))
    ]
    out = shape_of((1, ROWS, CORE), jnp.float32)
    return call(finish_kernel, (out, out), [VMEM] * 2)(own, sent(far, CHIP_BIT))


def solution(mesh):
    placed = (P("tile", None, None), P(None, "tile"), P())
    return jax.shard_map(
        shards,
        mesh=mesh,
        in_specs=placed,
        out_specs=(P("tile", "orient", None), P("tile", "orient", None)),
        check_vma=False,
    )
```

```python
import math

import jax
import jax.numpy as jnp
import numpy as np
from jax import lax
from jax.experimental import pallas as pl
from jax.experimental.pallas import tpu as pltpu
from jax.sharding import PartitionSpec as P

TILE = 512
TS = 128
CORE = 384
GRID_W = 8
TILES = 64
ORI_DEV = 8
MEMBERS = 4
ROWS = 96
ROWS_IN = 224
LENGTH = 256
PAIRS = LENGTH // 2
HALF = TILE // 2
CORE_BIT, CHIP_BIT = 1, 2


def bf16(table):
    return np.asarray(table, np.float64).astype(jnp.bfloat16)


def column_table():
    n = np.arange(TILE)[:, None]
    k = np.arange(HALF)[None, :]
    angle = (math.pi / TILE) * ((n * (2 * k + 1)) % (2 * TILE))
    return bf16(np.concatenate([np.cos(angle), -np.sin(angle)], 1))


def row_table():
    j = np.arange(PAIRS)[:, None]
    m = np.arange(ROWS_IN)[None, :]
    angle = (math.pi / LENGTH) * ((m * (2 * j + 1)) % (2 * LENGTH))
    c, s = np.cos(angle), np.sin(angle)
    parts = []
    for cut in (slice(0, TS), slice(TS, ROWS_IN)):
        u, v = c[:, cut], s[:, cut]
        parts.append(np.block([[u, v], [-v, u], [u, -v], [v, u]]))
    return bf16(np.concatenate(parts, 1))


def inverse_row_table():
    j = np.arange(PAIRS)[None, :]
    c = np.arange(ROWS)[:, None]
    angle = (math.pi / LENGTH) * ((c * (2 * j + 1)) % (2 * LENGTH))
    return bf16(np.concatenate([np.cos(angle), np.sin(angle)], 1))


def inverse_column_table():
    k = np.arange(HALF)[:, None]
    c = np.arange(CORE)[None, :]
    angle = (math.pi / TILE) * ((c * (2 * k + 1)) % (2 * TILE))
    scale = 2.0 / (LENGTH * TILE)
    return bf16(np.concatenate([np.cos(angle), -np.sin(angle)], 0) * scale)


def dot(a, b):
    return jnp.dot(a, b, preferred_element_type=jnp.float32)


def prepare_kernel(
    ids_hbm, micro_hbm, stack_hbm, out_hbm, right_ref, below_ref, corner_ref, ids_ref, micro_ref, stack_ref, out_ref, sems
):
    load_ids = pltpu.make_async_copy(ids_hbm, ids_ref, sems.at[0])
    load_stack = pltpu.make_async_copy(stack_hbm, stack_ref, sems.at[1])
    load_micro = pltpu.make_async_copy(micro_hbm.at[0], micro_ref, sems.at[2])
    load_ids.start()
    load_stack.start()
    load_micro.start()
    row = lax.broadcasted_iota(jnp.int32, (2 * ORI_DEV, 256), 0)
    lane = lax.broadcasted_iota(jnp.int32, (2 * ORI_DEV, 256), 1)
    wanted = jnp.zeros((2 * ORI_DEV, 256), jnp.int32)
    first = lax.axis_index("orient") * ORI_DEV
    load_ids.wait()
    for o in range(ORI_DEV):
        wanted = jnp.where(row % ORI_DEV == o, ids_ref[first + o], wanted)
    hot = jnp.where(lane == wanted, 1.0, 0.0).astype(jnp.bfloat16)
    load_stack.wait()
    picked = dot(hot, stack_ref[...])
    both = jnp.concatenate([picked[:ORI_DEV, :TS], picked[ORI_DEV:, TS:]], 0).astype(jnp.bfloat16)
    out_ref[...] = jnp.broadcast_to(both[None], out_ref.shape)
    store = pltpu.make_async_copy(out_ref, out_hbm, sems.at[3])
    store.start()
    load_micro.wait()
    right_ref[...] = micro_ref[:, :TS]
    below_ref[...] = micro_ref[:TS, :]
    corner_ref[...] = micro_ref[:TS, :TS]
    store.wait()


def load_kernel(*refs):
    sources, targets, sems = refs[:5], refs[6:11], refs[11]
    loads = [pltpu.make_async_copy(a, b, sems.at[i]) for i, (a, b) in enumerate(zip(sources, targets))]
    for load in loads:
        load.start()
    for load in loads:
        load.wait()


def template_kernel(pixels_ref, col_ref, row_ref, out_ref, shape_ref):
    values = pixels_ref[...].astype(jnp.float32).reshape(TS, ORI_DEV, TS)
    mean = jnp.sum(jnp.sum(values, 0), 1, keepdims=True) / (TS * TS)
    centered = values - mean[None]
    square = jnp.sum(jnp.sum(centered * centered, 0), 1, keepdims=True) / (TS * TS)
    spread = jnp.sqrt(square + 1e-06) * TS
    shape_ref[...] = (centered / spread[None]).reshape(TS * ORI_DEV, TS)
    shapes = [shape_ref[pl.ds(o, TS, stride=ORI_DEV), :].astype(jnp.bfloat16) for o in range(ORI_DEV)]
    half = ORI_DEV // 2
    for start in (0, half):
        together = jnp.concatenate(shapes[start : start + half], 0)
        g = dot(together, col_ref[:TS]).astype(jnp.bfloat16)
        for o in range(half):
            mine = g[o * TS : (o + 1) * TS]
            mine = jnp.concatenate([mine[:, :HALF], mine[:, HALF:]], 0)
            out_ref[start + o] = dot(row_ref[:, : 2 * TS], mine).astype(jnp.bfloat16)


def image_columns(own_ref, right_ref, below_ref, corner_ref, col_ref, g_ref):
    def columns(first, second, start, count):
        g = dot(first, col_ref[:CORE]) + dot(second, col_ref[CORE:])
        g_ref[0, start : start + count] = g[:, :HALF].astype(jnp.bfloat16)
        g_ref[1, start : start + count] = g[:, HALF:].astype(jnp.bfloat16)

    columns(own_ref[0], right_ref[...], 0, CORE)
    columns(below_ref[...], corner_ref[...], CORE, TS)


def image_rows(member_ref, row_ref, g_ref, bits, out_ref):
    start = pl.multiple_of((member_ref[0] ^ bits) * ROWS, 32)
    cuts = [(start, TS), (pl.multiple_of(start + TS, 32), ROWS_IN - TS)]
    piece = jnp.concatenate([g_ref[p, pl.ds(*cut)] for cut in cuts for p in range(2)], 0)
    out_ref[...] = dot(row_ref[...], piece).astype(jnp.bfloat16)


def block(image_ref, template_refs, inv_row_ref, inv_col_ref, out_ref, inner_ref):
    def part(ref, p):
        return ref[p * PAIRS : (p + 1) * PAIRS]

    def corr(template_ref):
        for o in range(ORI_DEV):

            def cross(p):
                a, b = part(image_ref, 2 * p), part(image_ref, 2 * p + 1)
                c, d = part(template_ref.at[o], 2 * p), part(template_ref.at[o], 2 * p + 1)
                return a * c + b * d, b * c - a * d

            plus_re, plus_im = cross(0)
            minus_re, minus_im = cross(1)
            mixed = jnp.concatenate(
                [
                    jnp.concatenate([plus_re + minus_re, plus_im + minus_im], 1),
                    jnp.concatenate([minus_im - plus_im, plus_re - minus_re], 1),
                ],
                0,
            )
            inner_ref[o * ROWS : (o + 1) * ROWS] = dot(inv_row_ref[...], mixed).astype(jnp.bfloat16)
        out = dot(inner_ref[...], inv_col_ref[...]).reshape(ORI_DEV, ROWS, CORE)
        return jnp.max(out, 0), jnp.sum(out, 0)

    high_a, sum_a = corr(template_refs[0])
    high_b, sum_b = corr(template_refs[1])
    out_ref[0] = jnp.maximum(high_a, high_b).astype(out_ref.dtype)
    out_ref[1] = (sum_a + sum_b).astype(out_ref.dtype)


def image_kernel(member_ref, *refs):
    own_ref, right_ref, below_ref, corner_ref, col_ref, row_ref, _, far_ref, near_ref, g_ref = refs
    image_columns(own_ref, right_ref, below_ref, corner_ref, col_ref, g_ref)
    image_rows(member_ref, row_ref, g_ref, CHIP_BIT, far_ref)
    image_rows(member_ref, row_ref, g_ref, 0, near_ref)


def block_kernel(image_ref, mine_ref, other_ref, inv_row_ref, inv_col_ref, out_ref, inner_ref):
    block(image_ref, (mine_ref, other_ref), inv_row_ref, inv_col_ref, out_ref, inner_ref)


def finish_kernel(own_ref, far_ref, peak_ref, excess_ref):
    far = far_ref[...].astype(jnp.float32)
    peak = jnp.maximum(own_ref[0], far[0])
    peak_ref[0] = peak
    excess_ref[0] = peak - (own_ref[1] + far[1]) / (MEMBERS * ORI_DEV)


VMEM = pl.BlockSpec(memory_space=pltpu.VMEM)
SMEM = pl.BlockSpec(memory_space=pltpu.SMEM)
ANY = pl.BlockSpec(memory_space=pl.ANY)
HBM = pl.BlockSpec(memory_space=pltpu.HBM)
LIMIT = 24 * 1024 * 1024


def call(kernel, outs, specs, scratch=(), flops=0, out_specs=None):
    return pl.pallas_call(
        kernel,
        out_shape=outs,
        in_specs=specs,
        out_specs=out_specs or jax.tree.map(lambda _: VMEM, outs),
        scratch_shapes=list(scratch),
        compiler_params=pltpu.CompilerParams(vmem_limit_bytes=LIMIT),
        cost_estimate=pl.CostEstimate(flops=flops, bytes_accessed=2**21, transcendentals=0),
    )


def shape_of(dims, dtype=jnp.bfloat16):
    return jax.ShapeDtypeStruct(dims, dtype)


def pinned(array):
    return pltpu.with_memory_space_constraint(jnp.asarray(array), pltpu.HBM)


def halo(block, distance):
    route = []
    crosses = distance % GRID_W
    for t in range(TILES):
        source = t + distance
        if t % GRID_W + crosses < GRID_W and source < TILES:
            for o in range(MEMBERS):
                route.append((source * MEMBERS + (o ^ 2 if crosses else o), t * MEMBERS + o))
    return lax.ppermute(block, ("tile", "orient"), route)


def shards(micrograph, template_stack, orient_list):
    spread, right, below, corner = call(
        prepare_kernel,
        (
            shape_of((TILES, 2 * ORI_DEV, TS)),
            shape_of((CORE, TS)),
            shape_of((TS, CORE)),
            shape_of((TS, TS)),
        ),
        [HBM] * 3,
        [
            pltpu.SMEM((MEMBERS * ORI_DEV,), jnp.int32),
            pltpu.VMEM((CORE, CORE), jnp.bfloat16),
            pltpu.VMEM((256, 256), jnp.bfloat16),
            pltpu.VMEM((TILES, 2 * ORI_DEV, TS), jnp.bfloat16),
            pltpu.SemaphoreType.DMA((4,)),
        ],
        out_specs=(HBM, VMEM, VMEM, VMEM),
    )(pinned(orient_list), pinned(micrograph), pinned(template_stack))
    pixels = lax.all_to_all(spread, "tile", 0, 0)
    kept = [column_table(), row_table(), inverse_row_table(), inverse_column_table(), micrograph]
    columns, rows, *tables, own_block = call(
        load_kernel,
        tuple(shape_of(array.shape) for array in kept),
        [HBM] * 5 + [ANY],
        [pltpu.SemaphoreType.DMA((5,))],
        flops=1000000000,
    )(*[pinned(array) for array in kept], corner)
    right = halo(right, 1)
    below = halo(below, GRID_W)
    corner = halo(corner, GRID_W + 1)
    member = lax.axis_index("orient")[None]

    def sent(piece, bits):
        return lax.ppermute(piece, "orient", [(i, i ^ bits) for i in range(MEMBERS)])

    templates = [
        call(
            template_kernel,
            shape_of((ORI_DEV, 4 * PAIRS, HALF)),
            [VMEM] * 3,
            [pltpu.VMEM((TS * ORI_DEV, TS), jnp.float32)],
            flops=10000000000,
        )(group, columns, rows)
        for group in (pixels, sent(pixels, CORE_BIT))
    ]
    spectra = shape_of((4 * PAIRS, HALF))
    image = call(
        image_kernel,
        (spectra, spectra),
        [SMEM] + [VMEM] * 6 + [ANY],
        [pltpu.VMEM((2, TILE, HALF), jnp.bfloat16)],
        flops=1600000000,
    )(member, own_block, right, below, corner, columns, rows, templates[0])
    far, own = [
        call(
            block_kernel,
            shape_of((2, ROWS, CORE), kind),
            [VMEM] * 5,
            [pltpu.VMEM((ORI_DEV * ROWS, TILE), jnp.bfloat16)],
            flops=2000000000,
        )(spectrum, *templates, *tables)
        for spectrum, kind in zip(image, (jnp.bfloat16, jnp.float32))
    ]
    out = shape_of((1, ROWS, CORE), jnp.float32)
    return call(finish_kernel, (out, out), [VMEM] * 2)(own, sent(far, CHIP_BIT))


def solution(mesh):
    placed = (P("tile", None, None), P(None, "tile"), P())
    return jax.shard_map(
        shards,
        mesh=mesh,
        in_specs=placed,
        out_specs=(P("tile", "orient", None), P("tile", "orient", None)),
        check_vma=False,
    )
```

```python
import math

import jax
import jax.numpy as jnp
import numpy as np
from jax import lax
from jax.experimental import pallas as pl
from jax.experimental.pallas import tpu as pltpu
from jax.sharding import PartitionSpec as P

TILE = 512
TS = 128
CORE = 384
GRID_W = 8
TILES = 64
ORI_DEV = 8
MEMBERS = 4
ROWS = 96
ROWS_IN = 224
LENGTH = 256
PAIRS = LENGTH // 2
HALF = TILE // 2
CORE_BIT, CHIP_BIT = 1, 2


def bf16(table):
    return np.asarray(table, np.float64).astype(jnp.bfloat16)


def column_table():
    n = np.arange(TILE)[:, None]
    k = np.arange(HALF)[None, :]
    angle = (math.pi / TILE) * ((n * (2 * k + 1)) % (2 * TILE))
    return bf16(np.concatenate([np.cos(angle), -np.sin(angle)], 1))


def row_table():
    j = np.arange(PAIRS)[:, None]
    m = np.arange(ROWS_IN)[None, :]
    angle = (math.pi / LENGTH) * ((m * (2 * j + 1)) % (2 * LENGTH))
    c, s = np.cos(angle), np.sin(angle)
    parts = []
    for cut in (slice(0, TS), slice(TS, ROWS_IN)):
        u, v = c[:, cut], s[:, cut]
        parts.append(np.block([[u, v], [-v, u], [u, -v], [v, u]]))
    return bf16(np.concatenate(parts, 1))


def inverse_row_table():
    j = np.arange(PAIRS)[None, :]
    c = np.arange(ROWS)[:, None]
    angle = (math.pi / LENGTH) * ((c * (2 * j + 1)) % (2 * LENGTH))
    return bf16(np.concatenate([np.cos(angle), np.sin(angle)], 1))


def inverse_column_table():
    k = np.arange(HALF)[:, None]
    c = np.arange(CORE)[None, :]
    angle = (math.pi / TILE) * ((c * (2 * k + 1)) % (2 * TILE))
    scale = 2.0 / (LENGTH * TILE)
    return bf16(np.concatenate([np.cos(angle), -np.sin(angle)], 0) * scale)


def dot(a, b):
    return jnp.dot(a, b, preferred_element_type=jnp.float32)


def prepare_kernel(
    ids_hbm, micro_hbm, stack_hbm, out_hbm, right_ref, below_ref, corner_ref, ids_ref, micro_ref, stack_ref, out_ref, sems
):
    load_ids = pltpu.make_async_copy(ids_hbm, ids_ref, sems.at[0])
    load_stack = pltpu.make_async_copy(stack_hbm, stack_ref, sems.at[1])
    load_micro = pltpu.make_async_copy(micro_hbm.at[0], micro_ref, sems.at[2])
    load_ids.start()
    load_stack.start()
    load_micro.start()
    row = lax.broadcasted_iota(jnp.int32, (2 * ORI_DEV, 256), 0)
    lane = lax.broadcasted_iota(jnp.int32, (2 * ORI_DEV, 256), 1)
    wanted = jnp.zeros((2 * ORI_DEV, 256), jnp.int32)
    first = lax.axis_index("orient") * ORI_DEV
    load_ids.wait()
    for o in range(ORI_DEV):
        wanted = jnp.where(row % ORI_DEV == o, ids_ref[first + o], wanted)
    hot = jnp.where(lane == wanted, 1.0, 0.0).astype(jnp.bfloat16)
    load_stack.wait()
    picked = dot(hot, stack_ref[...])
    both = jnp.concatenate([picked[:ORI_DEV, :TS], picked[ORI_DEV:, TS:]], 0).astype(jnp.bfloat16)
    out_ref[...] = jnp.broadcast_to(both[None], out_ref.shape)
    store = pltpu.make_async_copy(out_ref, out_hbm, sems.at[3])
    store.start()
    load_micro.wait()
    right_ref[...] = micro_ref[:, :TS]
    below_ref[...] = micro_ref[:TS, :]
    corner_ref[...] = micro_ref[:TS, :TS]
    store.wait()


def load_kernel(*refs):
    sources, targets, sems = refs[:5], refs[6:11], refs[11]
    loads = [pltpu.make_async_copy(a, b, sems.at[i]) for i, (a, b) in enumerate(zip(sources, targets))]
    for load in loads:
        load.start()
    for load in loads:
        load.wait()


def normalize_kernel(pixels_ref, out_ref, shape_ref):
    values = pixels_ref[...].astype(jnp.float32).reshape(TS, ORI_DEV, TS)
    mean = jnp.sum(jnp.sum(values, 0), 1, keepdims=True) / (TS * TS)
    centered = values - mean[None]
    square = jnp.sum(jnp.sum(centered * centered, 0), 1, keepdims=True) / (TS * TS)
    spread = jnp.sqrt(square + 1e-06) * TS
    shape_ref[...] = (centered / spread[None]).reshape(TS * ORI_DEV, TS)
    for o in range(ORI_DEV):
        out_ref[o * TS : (o + 1) * TS] = shape_ref[pl.ds(o, TS, stride=ORI_DEV), :].astype(jnp.bfloat16)


def template_kernel(shapes_ref, col_ref, row_ref, out_ref):
    half = ORI_DEV // 2
    for start in (0, half):
        together = shapes_ref[start * TS : (start + half) * TS]
        g = dot(together, col_ref[:TS]).astype(jnp.bfloat16)
        for o in range(half):
            mine = g[o * TS : (o + 1) * TS]
            mine = jnp.concatenate([mine[:, :HALF], mine[:, HALF:]], 0)
            out_ref[start + o] = dot(row_ref[:, : 2 * TS], mine).astype(jnp.bfloat16)


def image_columns(own_ref, right_ref, below_ref, corner_ref, col_ref, g_ref):
    def columns(first, second, start, count):
        g = dot(first, col_ref[:CORE]) + dot(second, col_ref[CORE:])
        g_ref[0, start : start + count] = g[:, :HALF].astype(jnp.bfloat16)
        g_ref[1, start : start + count] = g[:, HALF:].astype(jnp.bfloat16)

    columns(own_ref[0], right_ref[...], 0, CORE)
    columns(below_ref[...], corner_ref[...], CORE, TS)


def image_rows(member_ref, row_ref, g_ref, bits, out_ref):
    start = pl.multiple_of((member_ref[0] ^ bits) * ROWS, 32)
    cuts = [(start, TS), (pl.multiple_of(start + TS, 32), ROWS_IN - TS)]
    piece = jnp.concatenate([g_ref[p, pl.ds(*cut)] for cut in cuts for p in range(2)], 0)
    out_ref[...] = dot(row_ref[...], piece).astype(jnp.bfloat16)


def block(image_ref, template_refs, inv_row_ref, inv_col_ref, out_ref, inner_ref):
    def part(ref, p):
        return ref[p * PAIRS : (p + 1) * PAIRS]

    def corr(template_ref):
        for o in range(ORI_DEV):

            def cross(p):
                a, b = part(image_ref, 2 * p), part(image_ref, 2 * p + 1)
                c, d = part(template_ref.at[o], 2 * p), part(template_ref.at[o], 2 * p + 1)
                return a * c + b * d, b * c - a * d

            plus_re, plus_im = cross(0)
            minus_re, minus_im = cross(1)
            mixed = jnp.concatenate(
                [
                    jnp.concatenate([plus_re + minus_re, plus_im + minus_im], 1),
                    jnp.concatenate([minus_im - plus_im, plus_re - minus_re], 1),
                ],
                0,
            )
            inner_ref[o * ROWS : (o + 1) * ROWS] = dot(inv_row_ref[...], mixed).astype(jnp.bfloat16)
        out = dot(inner_ref[...], inv_col_ref[...]).reshape(ORI_DEV, ROWS, CORE)
        return jnp.max(out, 0), jnp.sum(out, 0)

    high_a, sum_a = corr(template_refs[0])
    high_b, sum_b = corr(template_refs[1])
    out_ref[0] = jnp.maximum(high_a, high_b).astype(out_ref.dtype)
    out_ref[1] = (sum_a + sum_b).astype(out_ref.dtype)


def image_kernel(member_ref, *refs):
    own_ref, right_ref, below_ref, corner_ref, col_ref, row_ref, _, far_ref, g_ref = refs
    image_columns(own_ref, right_ref, below_ref, corner_ref, col_ref, g_ref)
    image_rows(member_ref, row_ref, g_ref, CHIP_BIT, far_ref)


def far_kernel(image_ref, mine_ref, other_ref, inv_row_ref, inv_col_ref, out_ref, inner_ref):
    block(image_ref, (mine_ref, other_ref), inv_row_ref, inv_col_ref, out_ref, inner_ref)


def own_kernel(member_ref, row_ref, g_ref, mine_ref, other_ref, inv_row_ref, inv_col_ref, out_ref, image_ref, inner_ref):
    image_rows(member_ref, row_ref, g_ref, 0, image_ref)
    block(image_ref, (mine_ref, other_ref), inv_row_ref, inv_col_ref, out_ref, inner_ref)


def finish_kernel(own_ref, far_ref, peak_ref, excess_ref):
    far = far_ref[...].astype(jnp.float32)
    peak = jnp.maximum(own_ref[0], far[0])
    peak_ref[0] = peak
    excess_ref[0] = peak - (own_ref[1] + far[1]) / (MEMBERS * ORI_DEV)


VMEM = pl.BlockSpec(memory_space=pltpu.VMEM)
SMEM = pl.BlockSpec(memory_space=pltpu.SMEM)
ANY = pl.BlockSpec(memory_space=pl.ANY)
HBM = pl.BlockSpec(memory_space=pltpu.HBM)
LIMIT = 24 * 1024 * 1024


def call(kernel, outs, specs, scratch=(), flops=0, out_specs=None):
    return pl.pallas_call(
        kernel,
        out_shape=outs,
        in_specs=specs,
        out_specs=out_specs or jax.tree.map(lambda _: VMEM, outs),
        scratch_shapes=list(scratch),
        compiler_params=pltpu.CompilerParams(vmem_limit_bytes=LIMIT),
        cost_estimate=pl.CostEstimate(flops=flops, bytes_accessed=2**21, transcendentals=0),
    )


def shape_of(dims, dtype=jnp.bfloat16):
    return jax.ShapeDtypeStruct(dims, dtype)


def pinned(array):
    return pltpu.with_memory_space_constraint(jnp.asarray(array), pltpu.HBM)


def halo(block, distance):
    route = []
    crosses = distance % GRID_W
    for t in range(TILES):
        source = t + distance
        if t % GRID_W + crosses < GRID_W and source < TILES:
            for o in range(MEMBERS):
                route.append((source * MEMBERS + (o ^ 2 if crosses else o), t * MEMBERS + o))
    return lax.ppermute(block, ("tile", "orient"), route)


def shards(micrograph, template_stack, orient_list):
    spread, right, below, corner = call(
        prepare_kernel,
        (
            shape_of((TILES, 2 * ORI_DEV, TS)),
            shape_of((CORE, TS)),
            shape_of((TS, CORE)),
            shape_of((TS, TS)),
        ),
        [HBM] * 3,
        [
            pltpu.SMEM((MEMBERS * ORI_DEV,), jnp.int32),
            pltpu.VMEM((CORE, CORE), jnp.bfloat16),
            pltpu.VMEM((256, 256), jnp.bfloat16),
            pltpu.VMEM((TILES, 2 * ORI_DEV, TS), jnp.bfloat16),
            pltpu.SemaphoreType.DMA((4,)),
        ],
        out_specs=(HBM, VMEM, VMEM, VMEM),
    )(pinned(orient_list), pinned(micrograph), pinned(template_stack))
    pixels = lax.all_to_all(spread, "tile", 0, 0)
    kept = [column_table(), row_table(), inverse_row_table(), inverse_column_table(), micrograph]
    columns, rows, *tables, own_block = call(
        load_kernel,
        tuple(shape_of(array.shape) for array in kept),
        [HBM] * 5 + [ANY],
        [pltpu.SemaphoreType.DMA((5,))],
        flops=1000000000,
    )(*[pinned(array) for array in kept], corner)
    right = halo(right, 1)
    below = halo(below, GRID_W)
    corner = halo(corner, GRID_W + 1)
    member = lax.axis_index("orient")[None]

    def sent(piece, bits):
        return lax.ppermute(piece, "orient", [(i, i ^ bits) for i in range(MEMBERS)])

    shapes = call(
        normalize_kernel,
        shape_of((ORI_DEV * TS, TS)),
        [VMEM],
        [pltpu.VMEM((TS * ORI_DEV, TS), jnp.float32)],
        flops=100000000,
    )(pixels)
    templates = [
        call(
            template_kernel,
            shape_of((ORI_DEV, 4 * PAIRS, HALF)),
            [VMEM] * 3,
            flops=10000000000,
        )(group, columns, rows)
        for group in (shapes, sent(shapes, CORE_BIT))
    ]
    spectrum = shape_of((4 * PAIRS, HALF))
    image, g = call(
        image_kernel,
        (spectrum, shape_of((2, TILE, HALF))),
        [SMEM] + [VMEM] * 6 + [ANY],
        flops=1600000000,
    )(member, own_block, right, below, corner, columns, rows, templates[0])
    inner = pltpu.VMEM((ORI_DEV * ROWS, TILE), jnp.bfloat16)
    far = call(
        far_kernel,
        shape_of((2, ROWS, CORE)),
        [VMEM] * 5,
        [inner],
        flops=2000000000,
    )(image, *templates, *tables)
    own = call(
        own_kernel,
        shape_of((2, ROWS, CORE), jnp.float32),
        [SMEM] + [VMEM] * 6,
        [pltpu.VMEM((4 * PAIRS, HALF), jnp.bfloat16), inner],
        flops=2000000000,
    )(member, rows, g, *templates, *tables)
    out = shape_of((1, ROWS, CORE), jnp.float32)
    return call(finish_kernel, (out, out), [VMEM] * 2)(own, sent(far, CHIP_BIT))


def solution(mesh):
    placed = (P("tile", None, None), P(None, "tile"), P())
    return jax.shard_map(
        shards,
        mesh=mesh,
        in_specs=placed,
        out_specs=(P("tile", "orient", None), P("tile", "orient", None)),
        check_vma=False,
    )
```

```python
import math

import jax
import jax.numpy as jnp
import numpy as np
from jax import lax
from jax.experimental import pallas as pl
from jax.experimental.pallas import tpu as pltpu
from jax.sharding import PartitionSpec as P

TILE = 512
TS = 128
CORE = 384
GRID_W = 8
TILES = 64
ORI_DEV = 8
MEMBERS = 4
ROWS = 96
ROWS_IN = 224
LENGTH = 256
PAIRS = LENGTH // 2
HALF = TILE // 2
CORE_BIT, CHIP_BIT = 1, 2


def bf16(table):
    return np.asarray(table, np.float64).astype(jnp.bfloat16)


def column_table():
    n = np.arange(TILE)[:, None]
    k = np.arange(HALF)[None, :]
    angle = (math.pi / TILE) * ((n * (2 * k + 1)) % (2 * TILE))
    return bf16(np.concatenate([np.cos(angle), -np.sin(angle)], 1))


def row_table():
    j = np.arange(PAIRS)[:, None]
    m = np.arange(ROWS_IN)[None, :]
    angle = (math.pi / LENGTH) * ((m * (2 * j + 1)) % (2 * LENGTH))
    c, s = np.cos(angle), np.sin(angle)
    parts = []
    for cut in (slice(0, TS), slice(TS, ROWS_IN)):
        u, v = c[:, cut], s[:, cut]
        parts.append(np.block([[u, v], [-v, u], [u, -v], [v, u]]))
    return bf16(np.concatenate(parts, 1))


def inverse_row_table():
    j = np.arange(PAIRS)[None, :]
    c = np.arange(ROWS)[:, None]
    angle = (math.pi / LENGTH) * ((c * (2 * j + 1)) % (2 * LENGTH))
    return bf16(np.concatenate([np.cos(angle), np.sin(angle)], 1))


def inverse_column_table():
    k = np.arange(HALF)[:, None]
    c = np.arange(CORE)[None, :]
    angle = (math.pi / TILE) * ((c * (2 * k + 1)) % (2 * TILE))
    scale = 2.0 / (LENGTH * TILE)
    return bf16(np.concatenate([np.cos(angle), -np.sin(angle)], 0) * scale)


def dot(a, b):
    return jnp.dot(a, b, preferred_element_type=jnp.float32)


def prepare_kernel(
    ids_hbm, micro_hbm, stack_hbm, out_hbm, right_ref, below_ref, corner_ref, ids_ref, micro_ref, stack_ref, out_ref, sems
):
    load_ids = pltpu.make_async_copy(ids_hbm, ids_ref, sems.at[0])
    load_stack = pltpu.make_async_copy(stack_hbm, stack_ref, sems.at[1])
    load_micro = pltpu.make_async_copy(micro_hbm.at[0], micro_ref, sems.at[2])
    load_ids.start()
    load_stack.start()
    load_micro.start()
    row = lax.broadcasted_iota(jnp.int32, (2 * ORI_DEV, 256), 0)
    lane = lax.broadcasted_iota(jnp.int32, (2 * ORI_DEV, 256), 1)
    wanted = jnp.zeros((2 * ORI_DEV, 256), jnp.int32)
    first = lax.axis_index("orient") * ORI_DEV
    load_ids.wait()
    for o in range(ORI_DEV):
        wanted = jnp.where(row % ORI_DEV == o, ids_ref[first + o], wanted)
    hot = jnp.where(lane == wanted, 1.0, 0.0).astype(jnp.bfloat16)
    load_stack.wait()
    picked = dot(hot, stack_ref[...])
    both = jnp.concatenate([picked[:ORI_DEV, :TS], picked[ORI_DEV:, TS:]], 0).astype(jnp.bfloat16)
    out_ref[...] = jnp.broadcast_to(both[None], out_ref.shape)
    store = pltpu.make_async_copy(out_ref, out_hbm, sems.at[3])
    store.start()
    load_micro.wait()
    right_ref[...] = micro_ref[:, :TS]
    below_ref[...] = micro_ref[:TS, :]
    corner_ref[...] = micro_ref[:TS, :TS]
    store.wait()


def load_kernel(*refs):
    sources, targets, sems = refs[:5], refs[6:11], refs[11]
    loads = [pltpu.make_async_copy(a, b, sems.at[i]) for i, (a, b) in enumerate(zip(sources, targets))]
    for load in loads:
        load.start()
    for load in loads:
        load.wait()


def template_kernel(pixels_ref, col_ref, row_ref, out_ref, shape_ref):
    values = pixels_ref[...].astype(jnp.float32).reshape(TS, ORI_DEV, TS)
    mean = jnp.sum(jnp.sum(values, 0), 1, keepdims=True) / (TS * TS)
    centered = values - mean[None]
    square = jnp.sum(jnp.sum(centered * centered, 0), 1, keepdims=True) / (TS * TS)
    spread = jnp.sqrt(square + 1e-06) * TS
    shape_ref[...] = (centered / spread[None]).reshape(TS * ORI_DEV, TS)
    shapes = [shape_ref[pl.ds(o, TS, stride=ORI_DEV), :].astype(jnp.bfloat16) for o in range(ORI_DEV)]
    half = ORI_DEV // 2
    for start in (0, half):
        together = jnp.concatenate(shapes[start : start + half], 0)
        g = dot(together, col_ref[:TS]).astype(jnp.bfloat16)
        for o in range(half):
            mine = g[o * TS : (o + 1) * TS]
            mine = jnp.concatenate([mine[:, :HALF], mine[:, HALF:]], 0)
            out_ref[start + o] = dot(row_ref[:, : 2 * TS], mine).astype(jnp.bfloat16)


def image_columns(own_ref, right_ref, below_ref, corner_ref, col_ref, g_ref):
    def columns(first, second, start, count):
        g = dot(first, col_ref[:CORE]) + dot(second, col_ref[CORE:])
        g_ref[0, start : start + count] = g[:, :HALF].astype(jnp.bfloat16)
        g_ref[1, start : start + count] = g[:, HALF:].astype(jnp.bfloat16)

    columns(own_ref[0], right_ref[...], 0, CORE)
    columns(below_ref[...], corner_ref[...], CORE, TS)


def image_rows(member_ref, row_ref, g_ref, bits, out_ref):
    start = pl.multiple_of((member_ref[0] ^ bits) * ROWS, 32)
    cuts = [(start, TS), (pl.multiple_of(start + TS, 32), ROWS_IN - TS)]
    piece = jnp.concatenate([g_ref[p, pl.ds(*cut)] for cut in cuts for p in range(2)], 0)
    out_ref[...] = dot(row_ref[...], piece).astype(jnp.bfloat16)


def block(image_ref, template_refs, inv_row_ref, inv_col_ref, out_ref, inner_ref):
    def part(ref, p):
        return ref[p * PAIRS : (p + 1) * PAIRS]

    def corr(template_ref):
        for o in range(ORI_DEV):

            def cross(p):
                a, b = part(image_ref, 2 * p), part(image_ref, 2 * p + 1)
                c, d = part(template_ref.at[o], 2 * p), part(template_ref.at[o], 2 * p + 1)
                return a * c + b * d, b * c - a * d

            plus_re, plus_im = cross(0)
            minus_re, minus_im = cross(1)
            mixed = jnp.concatenate(
                [
                    jnp.concatenate([plus_re + minus_re, plus_im + minus_im], 1),
                    jnp.concatenate([minus_im - plus_im, plus_re - minus_re], 1),
                ],
                0,
            )
            inner_ref[o * ROWS : (o + 1) * ROWS] = dot(inv_row_ref[...], mixed).astype(jnp.bfloat16)
        out = dot(inner_ref[...], inv_col_ref[...]).reshape(ORI_DEV, ROWS, CORE)
        return jnp.max(out, 0), jnp.sum(out, 0)

    high_a, sum_a = corr(template_refs[0])
    high_b, sum_b = corr(template_refs[1])
    out_ref[0] = jnp.maximum(high_a, high_b).astype(out_ref.dtype)
    out_ref[1] = (sum_a + sum_b).astype(out_ref.dtype)


def image_kernel(member_ref, *refs):
    corner_ref, right_ref, below_ref, own_ref, col_ref, row_ref, far_ref, g_ref = refs
    image_columns(own_ref, right_ref, below_ref, corner_ref, col_ref, g_ref)
    image_rows(member_ref, row_ref, g_ref, CHIP_BIT, far_ref)


def far_kernel(image_ref, mine_ref, other_ref, inv_row_ref, inv_col_ref, out_ref, inner_ref):
    block(image_ref, (mine_ref, other_ref), inv_row_ref, inv_col_ref, out_ref, inner_ref)


def own_kernel(member_ref, row_ref, g_ref, mine_ref, other_ref, inv_row_ref, inv_col_ref, out_ref, image_ref, inner_ref):
    image_rows(member_ref, row_ref, g_ref, 0, image_ref)
    block(image_ref, (mine_ref, other_ref), inv_row_ref, inv_col_ref, out_ref, inner_ref)


def finish_kernel(own_ref, far_ref, peak_ref, excess_ref):
    far = far_ref[...].astype(jnp.float32)
    peak = jnp.maximum(own_ref[0], far[0])
    peak_ref[0] = peak
    excess_ref[0] = peak - (own_ref[1] + far[1]) / (MEMBERS * ORI_DEV)


VMEM = pl.BlockSpec(memory_space=pltpu.VMEM)
SMEM = pl.BlockSpec(memory_space=pltpu.SMEM)
ANY = pl.BlockSpec(memory_space=pl.ANY)
HBM = pl.BlockSpec(memory_space=pltpu.HBM)
LIMIT = 24 * 1024 * 1024


def call(kernel, outs, specs, scratch=(), flops=0, out_specs=None):
    return pl.pallas_call(
        kernel,
        out_shape=outs,
        in_specs=specs,
        out_specs=out_specs or jax.tree.map(lambda _: VMEM, outs),
        scratch_shapes=list(scratch),
        compiler_params=pltpu.CompilerParams(vmem_limit_bytes=LIMIT),
        cost_estimate=pl.CostEstimate(flops=flops, bytes_accessed=2**21, transcendentals=0),
    )


def shape_of(dims, dtype=jnp.bfloat16):
    return jax.ShapeDtypeStruct(dims, dtype)


def pinned(array):
    return pltpu.with_memory_space_constraint(jnp.asarray(array), pltpu.HBM)


def halo(block, distance):
    route = []
    crosses = distance % GRID_W
    for t in range(TILES):
        source = t + distance
        if t % GRID_W + crosses < GRID_W and source < TILES:
            for o in range(MEMBERS):
                route.append((source * MEMBERS + (o ^ 2 if crosses else o), t * MEMBERS + o))
    return lax.ppermute(block, ("tile", "orient"), route)


def shards(micrograph, template_stack, orient_list):
    spread, right, below, corner = call(
        prepare_kernel,
        (
            shape_of((TILES, 2 * ORI_DEV, TS)),
            shape_of((CORE, TS)),
            shape_of((TS, CORE)),
            shape_of((TS, TS)),
        ),
        [HBM] * 3,
        [
            pltpu.SMEM((MEMBERS * ORI_DEV,), jnp.int32),
            pltpu.VMEM((CORE, CORE), jnp.bfloat16),
            pltpu.VMEM((256, 256), jnp.bfloat16),
            pltpu.VMEM((TILES, 2 * ORI_DEV, TS), jnp.bfloat16),
            pltpu.SemaphoreType.DMA((4,)),
        ],
        out_specs=(HBM, VMEM, VMEM, VMEM),
    )(pinned(orient_list), pinned(micrograph), pinned(template_stack))
    pixels = lax.all_to_all(spread, "tile", 0, 0)
    kept = [column_table(), row_table(), inverse_row_table(), inverse_column_table(), micrograph]
    columns, rows, *tables, own_block = call(
        load_kernel,
        tuple(shape_of(array.shape) for array in kept),
        [HBM] * 5 + [ANY],
        [pltpu.SemaphoreType.DMA((5,))],
        flops=10000000000,
    )(*[pinned(array) for array in kept], corner)
    corner = halo(corner, GRID_W + 1)
    right = halo(right, 1)
    below = halo(below, GRID_W)
    member = lax.axis_index("orient")[None]

    def sent(piece, bits):
        return lax.ppermute(piece, "orient", [(i, i ^ bits) for i in range(MEMBERS)])

    templates = [
        call(
            template_kernel,
            shape_of((ORI_DEV, 4 * PAIRS, HALF)),
            [VMEM] * 3,
            [pltpu.VMEM((TS * ORI_DEV, TS), jnp.float32)],
            flops=10000000000,
        )(group, columns, rows)
        for group in (pixels, sent(pixels, CORE_BIT))
    ]
    spectrum = shape_of((4 * PAIRS, HALF))
    image, g = call(
        image_kernel,
        (spectrum, shape_of((2, TILE, HALF))),
        [SMEM] + [VMEM] * 6,
        flops=1600000000,
    )(member, corner, right, below, own_block, columns, rows)
    inner = pltpu.VMEM((ORI_DEV * ROWS, TILE), jnp.bfloat16)
    far = call(
        far_kernel,
        shape_of((2, ROWS, CORE)),
        [VMEM] * 5,
        [inner],
        flops=2000000000,
    )(image, *templates, *tables)
    own = call(
        own_kernel,
        shape_of((2, ROWS, CORE), jnp.float32),
        [SMEM] + [VMEM] * 6,
        [pltpu.VMEM((4 * PAIRS, HALF), jnp.bfloat16), inner],
        flops=2000000000,
    )(member, rows, g, *templates, *tables)
    out = shape_of((1, ROWS, CORE), jnp.float32)
    return call(finish_kernel, (out, out), [VMEM] * 2)(own, sent(far, CHIP_BIT))


def solution(mesh):
    placed = (P("tile", None, None), P(None, "tile"), P())
    return jax.shard_map(
        shards,
        mesh=mesh,
        in_specs=placed,
        out_specs=(P("tile", "orient", None), P("tile", "orient", None)),
        check_vma=False,
    )
```

```python
import math

import jax
import jax.numpy as jnp
import numpy as np
from jax import lax
from jax.experimental import pallas as pl
from jax.experimental.pallas import tpu as pltpu
from jax.sharding import PartitionSpec as P

TILE = 512
TS = 128
CORE = 384
GRID_W = 8
TILES = 64
ORI_DEV = 8
MEMBERS = 4
ROWS = 96
ROWS_IN = 224
LENGTH = 256
PAIRS = LENGTH // 2
HALF = TILE // 2
CORE_BIT, CHIP_BIT = 1, 2


def bf16(table):
    return np.asarray(table, np.float64).astype(jnp.bfloat16)


def column_table():
    n = np.arange(TILE)[:, None]
    k = np.arange(HALF)[None, :]
    angle = (math.pi / TILE) * ((n * (2 * k + 1)) % (2 * TILE))
    return bf16(np.concatenate([np.cos(angle), -np.sin(angle)], 1))


def row_table():
    j = np.arange(PAIRS)[:, None]
    m = np.arange(ROWS_IN)[None, :]
    angle = (math.pi / LENGTH) * ((m * (2 * j + 1)) % (2 * LENGTH))
    c, s = np.cos(angle), np.sin(angle)
    parts = []
    for cut in (slice(0, TS), slice(TS, ROWS_IN)):
        u, v = c[:, cut], s[:, cut]
        parts.append(np.block([[u, v], [-v, u], [u, -v], [v, u]]))
    return bf16(np.concatenate(parts, 1))


def inverse_row_table():
    j = np.arange(PAIRS)[None, :]
    c = np.arange(ROWS)[:, None]
    angle = (math.pi / LENGTH) * ((c * (2 * j + 1)) % (2 * LENGTH))
    return bf16(np.concatenate([np.cos(angle), np.sin(angle)], 1))


def inverse_column_table():
    k = np.arange(HALF)[:, None]
    c = np.arange(CORE)[None, :]
    angle = (math.pi / TILE) * ((c * (2 * k + 1)) % (2 * TILE))
    scale = 2.0 / (LENGTH * TILE)
    return bf16(np.concatenate([np.cos(angle), -np.sin(angle)], 0) * scale)


def dot(a, b):
    return jnp.dot(a, b, preferred_element_type=jnp.float32)


def prepare_kernel(
    ids_hbm, micro_hbm, stack_hbm, out_hbm, right_ref, below_ref, corner_ref, ids_ref, micro_ref, stack_ref, out_ref, sems
):
    load_ids = pltpu.make_async_copy(ids_hbm, ids_ref, sems.at[0])
    load_stack = pltpu.make_async_copy(stack_hbm, stack_ref, sems.at[1])
    load_micro = pltpu.make_async_copy(micro_hbm.at[0], micro_ref, sems.at[2])
    load_ids.start()
    load_stack.start()
    load_micro.start()
    row = lax.broadcasted_iota(jnp.int32, (4 * ORI_DEV, 256), 0)
    lane = lax.broadcasted_iota(jnp.int32, (4 * ORI_DEV, 256), 1)
    wanted = jnp.zeros((4 * ORI_DEV, 256), jnp.int32)
    member, side = lax.axis_index("orient"), lax.axis_index("tile") % 2
    load_ids.wait()
    for to_side in range(2):
        first = (member ^ (CHIP_BIT * (side ^ to_side))) * ORI_DEV
        for o in range(ORI_DEV):
            here = (row % ORI_DEV == o) & (row // (2 * ORI_DEV) == to_side)
            wanted = jnp.where(here, ids_ref[first + o], wanted)
    hot = jnp.where(lane == wanted, 1.0, 0.0).astype(jnp.bfloat16)
    load_stack.wait()
    picked = dot(hot, stack_ref[...])
    for to_side in range(2):
        top, middle, end = (2 * to_side * ORI_DEV + k * ORI_DEV for k in range(3))
        both = jnp.concatenate([picked[top:middle, :TS], picked[middle:end, TS:]], 0).astype(jnp.bfloat16)
        out_ref[:, to_side] = jnp.broadcast_to(both[None], (TILES // 2, 2 * ORI_DEV, TS))
    store = pltpu.make_async_copy(out_ref, out_hbm, sems.at[3])
    store.start()
    load_micro.wait()
    right_ref[...] = micro_ref[:, :TS]
    below_ref[...] = micro_ref[:TS, :]
    corner_ref[...] = micro_ref[:TS, :TS]
    store.wait()


def load_kernel(*refs):
    sources, targets, sems = refs[:5], refs[6:11], refs[11]
    loads = [pltpu.make_async_copy(a, b, sems.at[i]) for i, (a, b) in enumerate(zip(sources, targets))]
    for load in loads:
        load.start()
    for load in loads:
        load.wait()


def template_kernel(pixels_ref, col_ref, row_ref, out_ref, shape_ref):
    values = pixels_ref[...].astype(jnp.float32).reshape(TS, ORI_DEV, TS)
    mean = jnp.sum(jnp.sum(values, 0), 1, keepdims=True) / (TS * TS)
    centered = values - mean[None]
    square = jnp.sum(jnp.sum(centered * centered, 0), 1, keepdims=True) / (TS * TS)
    spread = jnp.sqrt(square + 1e-06) * TS
    shape_ref[...] = (centered * (1.0 / spread)[None]).reshape(TS * ORI_DEV, TS)
    shapes = [shape_ref[pl.ds(o, TS, stride=ORI_DEV), :].astype(jnp.bfloat16) for o in range(ORI_DEV)]
    g = dot(jnp.concatenate(shapes, 0), col_ref[:TS]).astype(jnp.bfloat16)
    for o in range(ORI_DEV):
        mine = g[o * TS : (o + 1) * TS]
        mine = jnp.concatenate([mine[:, :HALF], mine[:, HALF:]], 0)
        out_ref[o] = dot(row_ref[:, : 2 * TS], mine).astype(jnp.bfloat16)


def image_columns(own_ref, right_ref, below_ref, corner_ref, col_ref, g_ref):
    def columns(first, second, start, count):
        g = dot(first, col_ref[:CORE]) + dot(second, col_ref[CORE:])
        g_ref[0, start : start + count] = g[:, :HALF].astype(jnp.bfloat16)
        g_ref[1, start : start + count] = g[:, HALF:].astype(jnp.bfloat16)

    columns(own_ref[0], right_ref[...], 0, CORE)
    columns(below_ref[...], corner_ref[...], CORE, TS)


def image_rows(member_ref, row_ref, g_ref, bits, out_ref):
    start = pl.multiple_of((member_ref[0] ^ bits) * ROWS, 32)
    cuts = [(start, TS), (pl.multiple_of(start + TS, 32), ROWS_IN - TS)]
    piece = jnp.concatenate([g_ref[p, pl.ds(*cut)] for cut in cuts for p in range(2)], 0)
    out_ref[...] = dot(row_ref[...], piece).astype(jnp.bfloat16)


def block(image_ref, template_refs, inv_row_ref, inv_col_ref, out_ref, inner_ref):
    def part(ref, p):
        return ref[p * PAIRS : (p + 1) * PAIRS]

    def corr(template_ref):
        for o in range(ORI_DEV):

            def cross(p):
                a, b = part(image_ref, 2 * p), part(image_ref, 2 * p + 1)
                c, d = part(template_ref.at[o], 2 * p), part(template_ref.at[o], 2 * p + 1)
                return a * c + b * d, b * c - a * d

            plus_re, plus_im = cross(0)
            minus_re, minus_im = cross(1)
            mixed = jnp.concatenate(
                [
                    jnp.concatenate([plus_re + minus_re, plus_im + minus_im], 1),
                    jnp.concatenate([minus_im - plus_im, plus_re - minus_re], 1),
                ],
                0,
            )
            inner_ref[o * ROWS : (o + 1) * ROWS] = dot(inv_row_ref[...], mixed).astype(jnp.bfloat16)
        out = dot(inner_ref[...], inv_col_ref[...]).reshape(ORI_DEV, ROWS, CORE)
        return jnp.max(out, 0), jnp.sum(out, 0)

    high_a, sum_a = corr(template_refs[0])
    high_b, sum_b = corr(template_refs[1])
    out_ref[0] = jnp.maximum(high_a, high_b).astype(out_ref.dtype)
    out_ref[1] = (sum_a + sum_b).astype(out_ref.dtype)


def image_kernel(member_ref, *refs):
    corner_ref, right_ref, below_ref, own_ref, col_ref, row_ref, far_ref, g_ref = refs
    image_columns(own_ref, right_ref, below_ref, corner_ref, col_ref, g_ref)
    image_rows(member_ref, row_ref, g_ref, CHIP_BIT, far_ref)


def far_kernel(image_ref, mine_ref, other_ref, inv_row_ref, inv_col_ref, out_ref, inner_ref):
    block(image_ref, (mine_ref, other_ref), inv_row_ref, inv_col_ref, out_ref, inner_ref)


def own_kernel(member_ref, row_ref, g_ref, mine_ref, other_ref, inv_row_ref, inv_col_ref, out_ref, image_ref, inner_ref):
    image_rows(member_ref, row_ref, g_ref, 0, image_ref)
    block(image_ref, (mine_ref, other_ref), inv_row_ref, inv_col_ref, out_ref, inner_ref)


def finish_kernel(own_ref, far_ref, peak_ref, excess_ref):
    far = far_ref[...].astype(jnp.float32)
    peak = jnp.maximum(own_ref[0], far[0])
    peak_ref[0] = peak
    excess_ref[0] = peak - (own_ref[1] + far[1]) / (MEMBERS * ORI_DEV)


VMEM = pl.BlockSpec(memory_space=pltpu.VMEM)
SMEM = pl.BlockSpec(memory_space=pltpu.SMEM)
ANY = pl.BlockSpec(memory_space=pl.ANY)
HBM = pl.BlockSpec(memory_space=pltpu.HBM)
LIMIT = 24 * 1024 * 1024


def call(kernel, outs, specs, scratch=(), flops=0, out_specs=None):
    return pl.pallas_call(
        kernel,
        out_shape=outs,
        in_specs=specs,
        out_specs=out_specs or jax.tree.map(lambda _: VMEM, outs),
        scratch_shapes=list(scratch),
        compiler_params=pltpu.CompilerParams(vmem_limit_bytes=LIMIT),
        cost_estimate=pl.CostEstimate(flops=flops, bytes_accessed=2**21, transcendentals=0),
    )


def shape_of(dims, dtype=jnp.bfloat16):
    return jax.ShapeDtypeStruct(dims, dtype)


def pinned(array):
    return pltpu.with_memory_space_constraint(jnp.asarray(array), pltpu.HBM)


def near_groups():
    return [
        [t * MEMBERS + (chip ^ (CHIP_BIT * (t % 2))) + core for t in range(TILES)] for chip in (0, CHIP_BIT) for core in (0, 1)
    ]


def halo(block, distance):
    route = []
    crosses = distance % GRID_W
    for t in range(TILES):
        source = t + distance
        if t % GRID_W + crosses < GRID_W and source < TILES:
            for o in range(MEMBERS):
                route.append((source * MEMBERS + (o ^ 2 if crosses else o), t * MEMBERS + o))
    return lax.ppermute(block, ("tile", "orient"), route)


def shards(micrograph, template_stack, orient_list):
    spread, right, below, corner = call(
        prepare_kernel,
        (
            shape_of((TILES // 2, 2, 2 * ORI_DEV, TS)),
            shape_of((CORE, TS)),
            shape_of((TS, CORE)),
            shape_of((TS, TS)),
        ),
        [HBM] * 3,
        [
            pltpu.SMEM((MEMBERS * ORI_DEV,), jnp.int32),
            pltpu.VMEM((CORE, CORE), jnp.bfloat16),
            pltpu.VMEM((256, 256), jnp.bfloat16),
            pltpu.VMEM((TILES // 2, 2, 2 * ORI_DEV, TS), jnp.bfloat16),
            pltpu.SemaphoreType.DMA((4,)),
        ],
        out_specs=(HBM, VMEM, VMEM, VMEM),
    )(pinned(orient_list), pinned(micrograph), pinned(template_stack))
    pixels = lax.all_to_all(
        spread.reshape(TILES, 2 * ORI_DEV, TS), ("tile", "orient"), 0, 0, axis_index_groups=near_groups()
    )
    kept = [column_table(), row_table(), inverse_row_table(), inverse_column_table(), micrograph]
    columns, rows, *tables, own_block = call(
        load_kernel,
        tuple(shape_of(array.shape) for array in kept),
        [HBM] * 5 + [ANY],
        [pltpu.SemaphoreType.DMA((5,))],
        flops=10000000000,
    )(*[pinned(array) for array in kept], corner)
    corner = halo(corner, GRID_W + 1)
    right = halo(right, 1)
    below = halo(below, GRID_W)
    member = lax.axis_index("orient")[None]

    def sent(piece, bits):
        return lax.ppermute(piece, "orient", [(i, i ^ bits) for i in range(MEMBERS)])

    templates = [
        call(
            template_kernel,
            shape_of((ORI_DEV, 4 * PAIRS, HALF)),
            [VMEM] * 3,
            [pltpu.VMEM((TS * ORI_DEV, TS), jnp.float32)],
            flops=10000000000,
        )(group, columns, rows)
        for group in (pixels, sent(pixels, CORE_BIT))
    ]
    spectrum = shape_of((4 * PAIRS, HALF))
    image, g = call(
        image_kernel,
        (spectrum, shape_of((2, TILE, HALF))),
        [SMEM] + [VMEM] * 6,
        flops=1600000000,
    )(member, corner, right, below, own_block, columns, rows)
    inner = pltpu.VMEM((ORI_DEV * ROWS, TILE), jnp.bfloat16)
    far = call(
        far_kernel,
        shape_of((2, ROWS, CORE)),
        [VMEM] * 5,
        [inner],
        flops=2000000000,
    )(image, *templates, *tables)
    own = call(
        own_kernel,
        shape_of((2, ROWS, CORE), jnp.float32),
        [SMEM] + [VMEM] * 6,
        [pltpu.VMEM((4 * PAIRS, HALF), jnp.bfloat16), inner],
        flops=2000000000,
    )(member, rows, g, *templates, *tables)
    out = shape_of((1, ROWS, CORE), jnp.float32)
    return call(finish_kernel, (out, out), [VMEM] * 2)(own, sent(far, CHIP_BIT))


def solution(mesh):
    placed = (P("tile", None, None), P(None, "tile"), P())
    return jax.shard_map(
        shards,
        mesh=mesh,
        in_specs=placed,
        out_specs=(P("tile", "orient", None), P("tile", "orient", None)),
        check_vma=False,
    )
```

```python
import math

import jax
import jax.numpy as jnp
import numpy as np
from jax import lax
from jax.experimental import pallas as pl
from jax.experimental.pallas import tpu as pltpu
from jax.sharding import PartitionSpec as P

TILE = 512
TS = 128
CORE = 384
GRID_W = 8
TILES = 64
ORI_DEV = 8
MEMBERS = 4
ROWS = 96
ROWS_IN = 224
LENGTH = 256
PAIRS = LENGTH // 2
HALF = TILE // 2
CORE_BIT, CHIP_BIT = 1, 2


def bf16(table):
    return np.asarray(table, np.float64).astype(jnp.bfloat16)


def column_table():
    n = np.arange(TILE)[:, None]
    k = np.arange(HALF)[None, :]
    angle = (math.pi / TILE) * ((n * (2 * k + 1)) % (2 * TILE))
    return bf16(np.concatenate([np.cos(angle), -np.sin(angle)], 1))


def row_table():
    j = np.arange(PAIRS)[:, None]
    m = np.arange(ROWS_IN)[None, :]
    angle = (math.pi / LENGTH) * ((m * (2 * j + 1)) % (2 * LENGTH))
    c, s = np.cos(angle), np.sin(angle)
    parts = []
    for cut in (slice(0, TS), slice(TS, ROWS_IN)):
        u, v = c[:, cut], s[:, cut]
        parts.append(np.block([[u, v], [-v, u], [u, -v], [v, u]]))
    return bf16(np.concatenate(parts, 1))


def inverse_row_table():
    j = np.arange(PAIRS)[None, :]
    c = np.arange(ROWS)[:, None]
    angle = (math.pi / LENGTH) * ((c * (2 * j + 1)) % (2 * LENGTH))
    return bf16(np.concatenate([np.cos(angle), np.sin(angle)], 1))


def inverse_column_table():
    k = np.arange(HALF)[:, None]
    c = np.arange(CORE)[None, :]
    angle = (math.pi / TILE) * ((c * (2 * k + 1)) % (2 * TILE))
    scale = 2.0 / (LENGTH * TILE)
    return bf16(np.concatenate([np.cos(angle), -np.sin(angle)], 0) * scale)


def dot(a, b):
    return jnp.dot(a, b, preferred_element_type=jnp.float32)


def prepare_kernel(
    ids_hbm, micro_hbm, stack_hbm, out_hbm, right_ref, below_ref, corner_ref, ids_ref, micro_ref, stack_ref, out_ref, sems
):
    load_ids = pltpu.make_async_copy(ids_hbm, ids_ref, sems.at[0])
    load_stack = pltpu.make_async_copy(stack_hbm, stack_ref, sems.at[1])
    load_micro = pltpu.make_async_copy(micro_hbm.at[0], micro_ref, sems.at[2])
    load_ids.start()
    load_stack.start()
    load_micro.start()
    row = lax.broadcasted_iota(jnp.int32, (4 * ORI_DEV, 256), 0)
    lane = lax.broadcasted_iota(jnp.int32, (4 * ORI_DEV, 256), 1)
    wanted = jnp.zeros((4 * ORI_DEV, 256), jnp.int32)
    member, side = lax.axis_index("orient"), lax.axis_index("tile") % 2
    load_ids.wait()
    for to_side in range(2):
        first = (member ^ (CHIP_BIT * (side ^ to_side))) * ORI_DEV
        for o in range(ORI_DEV):
            here = (row % ORI_DEV == o) & (row // (2 * ORI_DEV) == to_side)
            wanted = jnp.where(here, ids_ref[first + o], wanted)
    hot = jnp.where(lane == wanted, 1.0, 0.0).astype(jnp.bfloat16)
    load_stack.wait()
    picked = dot(hot, stack_ref[...])
    for to_side in range(2):
        top, middle, end = (2 * to_side * ORI_DEV + k * ORI_DEV for k in range(3))
        both = jnp.concatenate([picked[top:middle, :TS], picked[middle:end, TS:]], 0).astype(jnp.bfloat16)
        out_ref[:, to_side] = jnp.broadcast_to(both[None], (TILES // 2, 2 * ORI_DEV, TS))
    store = pltpu.make_async_copy(out_ref, out_hbm, sems.at[3])
    store.start()
    load_micro.wait()
    right_ref[...] = micro_ref[:, :TS]
    below_ref[...] = micro_ref[:TS, :]
    corner_ref[...] = micro_ref[:TS, :TS]
    store.wait()


def load_kernel(*refs):
    sources, targets, sems = refs[:5], refs[6:11], refs[11]
    loads = [pltpu.make_async_copy(a, b, sems.at[i]) for i, (a, b) in enumerate(zip(sources, targets))]
    for load in loads:
        load.start()
    for load in loads:
        load.wait()


def template_kernel(pixels_ref, col_ref, row_ref, out_ref, shape_ref):
    values = pixels_ref[...].astype(jnp.float32).reshape(TS, ORI_DEV, TS)
    mean = jnp.sum(jnp.sum(values, 0), 1, keepdims=True) / (TS * TS)
    centered = values - mean[None]
    square = jnp.sum(jnp.sum(centered * centered, 0), 1, keepdims=True) / (TS * TS)
    spread = jnp.sqrt(square + 1e-06) * TS
    shape_ref[...] = (centered * (1.0 / spread)[None]).reshape(TS * ORI_DEV, TS)
    shapes = [shape_ref[pl.ds(o, TS, stride=ORI_DEV), :].astype(jnp.bfloat16) for o in range(ORI_DEV)]
    g = dot(jnp.concatenate(shapes, 0), col_ref[:TS]).astype(jnp.bfloat16)
    for o in range(ORI_DEV):
        mine = g[o * TS : (o + 1) * TS]
        mine = jnp.concatenate([mine[:, :HALF], mine[:, HALF:]], 0)
        out_ref[o] = dot(row_ref[:, : 2 * TS], mine).astype(jnp.bfloat16)


def image_columns(own_ref, right_ref, below_ref, corner_ref, col_ref, g_ref):
    def columns(first, second, start, count):
        g = dot(first, col_ref[:CORE]) + dot(second, col_ref[CORE:])
        g_ref[0, start : start + count] = g[:, :HALF].astype(jnp.bfloat16)
        g_ref[1, start : start + count] = g[:, HALF:].astype(jnp.bfloat16)

    columns(own_ref[0], right_ref[...], 0, CORE)
    columns(below_ref[...], corner_ref[...], CORE, TS)


def image_rows(member_ref, row_ref, g_ref, bits, out_ref):
    start = pl.multiple_of((member_ref[0] ^ bits) * ROWS, 32)
    cuts = [(start, TS), (pl.multiple_of(start + TS, 32), ROWS_IN - TS)]
    piece = jnp.concatenate([g_ref[p, pl.ds(*cut)] for cut in cuts for p in range(2)], 0)
    out_ref[...] = dot(row_ref[...], piece).astype(jnp.bfloat16)


def block(image_ref, template_refs, inv_row_ref, inv_col_ref, out_ref, inner_ref):
    def part(ref, p):
        return ref[p * PAIRS : (p + 1) * PAIRS]

    def corr(template_ref):
        for o in range(ORI_DEV):

            def cross(p):
                a, b = part(image_ref, 2 * p), part(image_ref, 2 * p + 1)
                c, d = part(template_ref.at[o], 2 * p), part(template_ref.at[o], 2 * p + 1)
                return a * c + b * d, b * c - a * d

            plus_re, plus_im = cross(0)
            minus_re, minus_im = cross(1)
            mixed = jnp.concatenate(
                [
                    jnp.concatenate([plus_re + minus_re, plus_im + minus_im], 1),
                    jnp.concatenate([minus_im - plus_im, plus_re - minus_re], 1),
                ],
                0,
            )
            inner_ref[o * ROWS : (o + 1) * ROWS] = dot(inv_row_ref[...], mixed).astype(jnp.bfloat16)
        out = dot(inner_ref[...], inv_col_ref[...]).reshape(ORI_DEV, ROWS, CORE)
        return jnp.max(out, 0), jnp.sum(out, 0)

    high, total = corr(template_refs[0])
    for template_ref in template_refs[1:]:
        more, added = corr(template_ref)
        high, total = jnp.maximum(high, more), total + added
    out_ref[0] = high.astype(out_ref.dtype)
    out_ref[1] = total.astype(out_ref.dtype)


def image_kernel(member_ref, *refs):
    corner_ref, right_ref, below_ref, own_ref, col_ref, row_ref, across_ref, same_ref, g_ref = refs
    image_columns(own_ref, right_ref, below_ref, corner_ref, col_ref, g_ref)
    image_rows(member_ref, row_ref, g_ref, CHIP_BIT + CORE_BIT, across_ref)
    image_rows(member_ref, row_ref, g_ref, CHIP_BIT, same_ref)


def far_kernel(image_ref, template_ref, inv_row_ref, inv_col_ref, out_ref, inner_ref):
    block(image_ref, (template_ref,), inv_row_ref, inv_col_ref, out_ref, inner_ref)


def merge_kernel(mine_ref, other_ref, out_ref):
    other = other_ref[...].astype(jnp.float32)
    out_ref[0] = jnp.maximum(mine_ref[0], other[0]).astype(out_ref.dtype)
    out_ref[1] = (mine_ref[1] + other[1]).astype(out_ref.dtype)


def own_kernel(member_ref, row_ref, g_ref, mine_ref, other_ref, inv_row_ref, inv_col_ref, out_ref, image_ref, inner_ref):
    image_rows(member_ref, row_ref, g_ref, 0, image_ref)
    block(image_ref, (mine_ref, other_ref), inv_row_ref, inv_col_ref, out_ref, inner_ref)


def finish_kernel(own_ref, far_ref, peak_ref, excess_ref):
    far = far_ref[...].astype(jnp.float32)
    peak = jnp.maximum(own_ref[0], far[0])
    peak_ref[0] = peak
    excess_ref[0] = peak - (own_ref[1] + far[1]) / (MEMBERS * ORI_DEV)


VMEM = pl.BlockSpec(memory_space=pltpu.VMEM)
SMEM = pl.BlockSpec(memory_space=pltpu.SMEM)
ANY = pl.BlockSpec(memory_space=pl.ANY)
HBM = pl.BlockSpec(memory_space=pltpu.HBM)
LIMIT = 24 * 1024 * 1024


def call(kernel, outs, specs, scratch=(), flops=0, out_specs=None):
    return pl.pallas_call(
        kernel,
        out_shape=outs,
        in_specs=specs,
        out_specs=out_specs or jax.tree.map(lambda _: VMEM, outs),
        scratch_shapes=list(scratch),
        compiler_params=pltpu.CompilerParams(vmem_limit_bytes=LIMIT),
        cost_estimate=pl.CostEstimate(flops=flops, bytes_accessed=2**21, transcendentals=0),
    )


def shape_of(dims, dtype=jnp.bfloat16):
    return jax.ShapeDtypeStruct(dims, dtype)


def pinned(array):
    return pltpu.with_memory_space_constraint(jnp.asarray(array), pltpu.HBM)


def near_groups():
    return [
        [t * MEMBERS + (chip ^ (CHIP_BIT * (t % 2))) + core for t in range(TILES)] for chip in (0, CHIP_BIT) for core in (0, 1)
    ]


def halo(block, distance):
    route = []
    crosses = distance % GRID_W
    for t in range(TILES):
        source = t + distance
        if t % GRID_W + crosses < GRID_W and source < TILES:
            for o in range(MEMBERS):
                route.append((source * MEMBERS + (o ^ 2 if crosses else o), t * MEMBERS + o))
    return lax.ppermute(block, ("tile", "orient"), route)


def shards(micrograph, template_stack, orient_list):
    spread, right, below, corner = call(
        prepare_kernel,
        (
            shape_of((TILES // 2, 2, 2 * ORI_DEV, TS)),
            shape_of((CORE, TS)),
            shape_of((TS, CORE)),
            shape_of((TS, TS)),
        ),
        [HBM] * 3,
        [
            pltpu.SMEM((MEMBERS * ORI_DEV,), jnp.int32),
            pltpu.VMEM((CORE, CORE), jnp.bfloat16),
            pltpu.VMEM((256, 256), jnp.bfloat16),
            pltpu.VMEM((TILES // 2, 2, 2 * ORI_DEV, TS), jnp.bfloat16),
            pltpu.SemaphoreType.DMA((4,)),
        ],
        out_specs=(HBM, VMEM, VMEM, VMEM),
    )(pinned(orient_list), pinned(micrograph), pinned(template_stack))
    pixels = lax.all_to_all(
        spread.reshape(TILES, 2 * ORI_DEV, TS), ("tile", "orient"), 0, 0, axis_index_groups=near_groups()
    )
    kept = [column_table(), row_table(), inverse_row_table(), inverse_column_table(), micrograph]
    columns, rows, *tables, own_block = call(
        load_kernel,
        tuple(shape_of(array.shape) for array in kept),
        [HBM] * 5 + [ANY],
        [pltpu.SemaphoreType.DMA((5,))],
        flops=10000000000,
    )(*[pinned(array) for array in kept], corner)
    corner = halo(corner, GRID_W + 1)
    right = halo(right, 1)
    below = halo(below, GRID_W)
    member = lax.axis_index("orient")[None]

    def sent(piece, bits):
        return lax.ppermute(piece, "orient", [(i, i ^ bits) for i in range(MEMBERS)])


    def spectra(group):
        return call(
            template_kernel,
            shape_of((ORI_DEV, 4 * PAIRS, HALF)),
            [VMEM] * 3,
            [pltpu.VMEM((TS * ORI_DEV, TS), jnp.float32)],
            flops=10000000000,
        )(group, columns, rows)

    spectrum = shape_of((4 * PAIRS, HALF))
    image_across, image_same, g = call(
        image_kernel,
        (spectrum, spectrum, shape_of((2, TILE, HALF))),
        [SMEM] + [VMEM] * 6,
        flops=1600000000,
    )(member, corner, right, below, own_block, columns, rows)
    inner = pltpu.VMEM((ORI_DEV * ROWS, TILE), jnp.bfloat16)
    piece, wide = shape_of((2, ROWS, CORE)), shape_of((2, ROWS, CORE), jnp.float32)

    def far(image, out):
        return call(far_kernel, out, [VMEM] * 4, [inner], flops=1000000000)(image, mine, *tables)

    mine = spectra(pixels)
    across = sent(far(image_across, piece), CORE_BIT)
    same = far(image_same, wide)
    merged = call(merge_kernel, piece, [VMEM] * 2, flops=100000000)(same, across)
    merged = sent(merged, CHIP_BIT)
    other = spectra(sent(pixels, CORE_BIT))
    own = call(
        own_kernel,
        wide,
        [SMEM] + [VMEM] * 6,
        [pltpu.VMEM((4 * PAIRS, HALF), jnp.bfloat16), inner],
        flops=2000000000,
    )(member, rows, g, mine, other, *tables)
    out = shape_of((1, ROWS, CORE), jnp.float32)
    return call(finish_kernel, (out, out), [VMEM] * 2)(own, merged)


def solution(mesh):
    placed = (P("tile", None, None), P(None, "tile"), P())
    return jax.shard_map(
        shards,
        mesh=mesh,
        in_specs=placed,
        out_specs=(P("tile", "orient", None), P("tile", "orient", None)),
        check_vma=False,
    )
```

```python
import math

import jax
import jax.numpy as jnp
import numpy as np
from jax import lax
from jax.experimental import pallas as pl
from jax.experimental.pallas import tpu as pltpu
from jax.sharding import PartitionSpec as P

TILE = 512
TS = 128
CORE = 384
GRID_W = 8
TILES = 64
ORI_DEV = 8
MEMBERS = 4
ROWS = 96
ROWS_IN = 224
LENGTH = 256
PAIRS = LENGTH // 2
HALF = TILE // 2
CORE_BIT, CHIP_BIT = 1, 2


def bf16(table):
    return np.asarray(table, np.float64).astype(jnp.bfloat16)


def column_table():
    n = np.arange(TILE)[:, None]
    k = np.arange(HALF)[None, :]
    angle = (math.pi / TILE) * ((n * (2 * k + 1)) % (2 * TILE))
    return bf16(np.concatenate([np.cos(angle), -np.sin(angle)], 1))


def row_table():
    j = np.arange(PAIRS)[:, None]
    m = np.arange(ROWS_IN)[None, :]
    angle = (math.pi / LENGTH) * ((m * (2 * j + 1)) % (2 * LENGTH))
    c, s = np.cos(angle), np.sin(angle)
    parts = []
    for cut in (slice(0, TS), slice(TS, ROWS_IN)):
        u, v = c[:, cut], s[:, cut]
        parts.append(np.block([[u, v], [-v, u], [u, -v], [v, u]]))
    return bf16(np.concatenate(parts, 1))


def inverse_row_table():
    j = np.arange(PAIRS)[None, :]
    c = np.arange(ROWS)[:, None]
    angle = (math.pi / LENGTH) * ((c * (2 * j + 1)) % (2 * LENGTH))
    return bf16(np.concatenate([np.cos(angle), np.sin(angle)], 1))


def inverse_column_table():
    k = np.arange(HALF)[:, None]
    c = np.arange(CORE)[None, :]
    angle = (math.pi / TILE) * ((c * (2 * k + 1)) % (2 * TILE))
    scale = 2.0 / (LENGTH * TILE)
    return bf16(np.concatenate([np.cos(angle), -np.sin(angle)], 0) * scale)


def dot(a, b):
    return jnp.dot(a, b, preferred_element_type=jnp.float32)


def prepare_kernel(
    ids_hbm, micro_hbm, stack_hbm, out_hbm, right_ref, below_ref, corner_ref, ids_ref, micro_ref, stack_ref, out_ref, sems
):
    load_ids = pltpu.make_async_copy(ids_hbm, ids_ref, sems.at[0])
    load_stack = pltpu.make_async_copy(stack_hbm, stack_ref, sems.at[1])
    load_micro = pltpu.make_async_copy(micro_hbm.at[0], micro_ref, sems.at[2])
    load_ids.start()
    load_stack.start()
    load_micro.start()
    row = lax.broadcasted_iota(jnp.int32, (4 * ORI_DEV, 256), 0)
    lane = lax.broadcasted_iota(jnp.int32, (4 * ORI_DEV, 256), 1)
    wanted = jnp.zeros((4 * ORI_DEV, 256), jnp.int32)
    member, side = lax.axis_index("orient"), lax.axis_index("tile") % 2
    load_ids.wait()
    for to_side in range(2):
        first = (member ^ (CHIP_BIT * (side ^ to_side))) * ORI_DEV
        for o in range(ORI_DEV):
            here = (row % ORI_DEV == o) & (row // (2 * ORI_DEV) == to_side)
            wanted = jnp.where(here, ids_ref[first + o], wanted)
    hot = jnp.where(lane == wanted, 1.0, 0.0).astype(jnp.bfloat16)
    load_stack.wait()
    picked = dot(hot, stack_ref[...])
    for to_side in range(2):
        top, middle, end = (2 * to_side * ORI_DEV + k * ORI_DEV for k in range(3))
        both = jnp.concatenate([picked[top:middle, :TS], picked[middle:end, TS:]], 0).astype(jnp.bfloat16)
        out_ref[:, to_side] = jnp.broadcast_to(both[None], (TILES // 2, 2 * ORI_DEV, TS))
    store = pltpu.make_async_copy(out_ref, out_hbm, sems.at[3])
    store.start()
    load_micro.wait()
    right_ref[...] = micro_ref[:, :TS]
    below_ref[...] = micro_ref[:TS, :]
    corner_ref[...] = micro_ref[:TS, :TS]
    store.wait()


def load_kernel(*refs):
    sources, targets, sems = refs[:5], refs[6:11], refs[11]
    loads = [pltpu.make_async_copy(a, b, sems.at[i]) for i, (a, b) in enumerate(zip(sources, targets))]
    for load in loads:
        load.start()
    for load in loads:
        load.wait()


def template_kernel(pixels_ref, col_ref, row_ref, out_ref, shape_ref):
    values = pixels_ref[...].astype(jnp.float32).reshape(TS, ORI_DEV, TS)
    mean = jnp.sum(jnp.sum(values, 0), 1, keepdims=True) / (TS * TS)
    centered = values - mean[None]
    square = jnp.sum(jnp.sum(centered * centered, 0), 1, keepdims=True) / (TS * TS)
    spread = jnp.sqrt(square + 1e-06) * TS
    shape_ref[...] = (centered * (1.0 / spread)[None]).reshape(TS * ORI_DEV, TS)
    shapes = [shape_ref[pl.ds(o, TS, stride=ORI_DEV), :].astype(jnp.bfloat16) for o in range(ORI_DEV)]
    g = dot(jnp.concatenate(shapes, 0), col_ref[:TS]).astype(jnp.bfloat16)
    for o in range(ORI_DEV):
        mine = g[o * TS : (o + 1) * TS]
        mine = jnp.concatenate([mine[:, :HALF], mine[:, HALF:]], 0)
        out_ref[o] = dot(row_ref[:, : 2 * TS], mine).astype(jnp.bfloat16)


def image_columns(own_ref, right_ref, below_ref, corner_ref, col_ref, g_ref):
    def columns(first, second, start, count):
        g = dot(first, col_ref[:CORE]) + dot(second, col_ref[CORE:])
        g_ref[0, start : start + count] = g[:, :HALF].astype(jnp.bfloat16)
        g_ref[1, start : start + count] = g[:, HALF:].astype(jnp.bfloat16)

    columns(own_ref[0], right_ref[...], 0, CORE)
    columns(below_ref[...], corner_ref[...], CORE, TS)


def image_rows(member_ref, row_ref, g_ref, bits, out_ref):
    start = pl.multiple_of((member_ref[0] ^ bits) * ROWS, 32)
    cuts = [(start, TS), (pl.multiple_of(start + TS, 32), ROWS_IN - TS)]
    piece = jnp.concatenate([g_ref[p, pl.ds(*cut)] for cut in cuts for p in range(2)], 0)
    out_ref[...] = dot(row_ref[...], piece).astype(jnp.bfloat16)


def block(image_ref, template_refs, inv_row_ref, inv_col_ref, out_ref, inner_ref):
    def part(ref, p):
        return ref[p * PAIRS : (p + 1) * PAIRS]

    def corr(template_ref):
        for o in range(ORI_DEV):

            def cross(p):
                a, b = part(image_ref, 2 * p), part(image_ref, 2 * p + 1)
                c, d = part(template_ref.at[o], 2 * p), part(template_ref.at[o], 2 * p + 1)
                return a * c + b * d, b * c - a * d

            plus_re, plus_im = cross(0)
            minus_re, minus_im = cross(1)
            mixed = jnp.concatenate(
                [
                    jnp.concatenate([plus_re + minus_re, plus_im + minus_im], 1),
                    jnp.concatenate([minus_im - plus_im, plus_re - minus_re], 1),
                ],
                0,
            )
            inner_ref[o * ROWS : (o + 1) * ROWS] = dot(inv_row_ref[...], mixed).astype(jnp.bfloat16)
        out = dot(inner_ref[...], inv_col_ref[...]).reshape(ORI_DEV, ROWS, CORE)
        return jnp.max(out, 0), jnp.sum(out, 0)

    high, total = corr(template_refs[0])
    for template_ref in template_refs[1:]:
        more, added = corr(template_ref)
        high, total = jnp.maximum(high, more), total + added
    out_ref[0] = high.astype(out_ref.dtype)
    out_ref[1] = total.astype(out_ref.dtype)


def image_kernel(member_ref, *refs):
    corner_ref, right_ref, below_ref, own_ref, col_ref, row_ref, across_ref, same_ref, g_ref = refs
    image_columns(own_ref, right_ref, below_ref, corner_ref, col_ref, g_ref)
    image_rows(member_ref, row_ref, g_ref, CHIP_BIT + CORE_BIT, across_ref)
    image_rows(member_ref, row_ref, g_ref, CHIP_BIT, same_ref)


def far_kernel(image_ref, template_ref, inv_row_ref, inv_col_ref, out_ref, inner_ref):
    block(image_ref, (template_ref,), inv_row_ref, inv_col_ref, out_ref, inner_ref)


def merge_kernel(mine_ref, other_ref, out_ref):
    other = other_ref[...].astype(jnp.float32)
    out_ref[0] = jnp.maximum(mine_ref[0], other[0]).astype(out_ref.dtype)
    out_ref[1] = (mine_ref[1] + other[1]).astype(out_ref.dtype)


def own_kernel(member_ref, row_ref, g_ref, mine_ref, other_ref, inv_row_ref, inv_col_ref, out_ref, image_ref, inner_ref):
    image_rows(member_ref, row_ref, g_ref, 0, image_ref)
    block(image_ref, (mine_ref, other_ref), inv_row_ref, inv_col_ref, out_ref, inner_ref)


def finish_kernel(own_ref, far_ref, peak_ref, excess_ref):
    far = far_ref[...].astype(jnp.float32)
    peak = jnp.maximum(own_ref[0], far[0])
    peak_ref[0] = peak
    excess_ref[0] = peak - (own_ref[1] + far[1]) / (MEMBERS * ORI_DEV)


VMEM = pl.BlockSpec(memory_space=pltpu.VMEM)
SMEM = pl.BlockSpec(memory_space=pltpu.SMEM)
ANY = pl.BlockSpec(memory_space=pl.ANY)
HBM = pl.BlockSpec(memory_space=pltpu.HBM)
LIMIT = 24 * 1024 * 1024


def call(kernel, outs, specs, scratch=(), flops=0, out_specs=None):
    return pl.pallas_call(
        kernel,
        out_shape=outs,
        in_specs=specs,
        out_specs=out_specs or jax.tree.map(lambda _: VMEM, outs),
        scratch_shapes=list(scratch),
        compiler_params=pltpu.CompilerParams(vmem_limit_bytes=LIMIT),
        cost_estimate=pl.CostEstimate(flops=flops, bytes_accessed=2**21, transcendentals=0),
    )


def shape_of(dims, dtype=jnp.bfloat16):
    return jax.ShapeDtypeStruct(dims, dtype)


def pinned(array):
    return pltpu.with_memory_space_constraint(jnp.asarray(array), pltpu.HBM)


def near_groups():
    return [
        [t * MEMBERS + (chip ^ (CHIP_BIT * (t % 2))) + core for t in range(TILES)] for chip in (0, CHIP_BIT) for core in (0, 1)
    ]


def halo(block, distance):
    route = []
    crosses = distance % GRID_W
    for t in range(TILES):
        source = t + distance
        if t % GRID_W + crosses < GRID_W and source < TILES:
            for o in range(MEMBERS):
                route.append((source * MEMBERS + (o ^ 2 if crosses else o), t * MEMBERS + o))
    return lax.ppermute(block, ("tile", "orient"), route)


def shards(micrograph, template_stack, orient_list):
    spread, right, below, corner = call(
        prepare_kernel,
        (
            shape_of((TILES // 2, 2, 2 * ORI_DEV, TS)),
            shape_of((CORE, TS)),
            shape_of((TS, CORE)),
            shape_of((TS, TS)),
        ),
        [HBM] * 3,
        [
            pltpu.SMEM((MEMBERS * ORI_DEV,), jnp.int32),
            pltpu.VMEM((CORE, CORE), jnp.bfloat16),
            pltpu.VMEM((256, 256), jnp.bfloat16),
            pltpu.VMEM((TILES // 2, 2, 2 * ORI_DEV, TS), jnp.bfloat16),
            pltpu.SemaphoreType.DMA((4,)),
        ],
        out_specs=(HBM, VMEM, VMEM, VMEM),
    )(pinned(orient_list), pinned(micrograph), pinned(template_stack))
    pixels = lax.all_to_all(
        spread.reshape(TILES, 2 * ORI_DEV, TS), ("tile", "orient"), 0, 0, axis_index_groups=near_groups()
    )
    kept = [column_table(), row_table(), inverse_row_table(), inverse_column_table(), micrograph]
    columns, rows, *tables, own_block = call(
        load_kernel,
        tuple(shape_of(array.shape) for array in kept),
        [HBM] * 5 + [ANY],
        [pltpu.SemaphoreType.DMA((5,))],
        flops=10000000000,
    )(*[pinned(array) for array in kept], corner)
    corner = halo(corner, GRID_W + 1)
    right = halo(right, 1)
    below = halo(below, GRID_W)
    member = lax.axis_index("orient")[None]

    def sent(piece, bits):
        return lax.ppermute(piece, "orient", [(i, i ^ bits) for i in range(MEMBERS)])


    def spectra(group):
        return call(
            template_kernel,
            shape_of((ORI_DEV, 4 * PAIRS, HALF)),
            [VMEM] * 3,
            [pltpu.VMEM((TS * ORI_DEV, TS), jnp.float32)],
            flops=1000000000,
        )(group, columns, rows)

    spectrum = shape_of((4 * PAIRS, HALF))
    image_across, image_same, g = call(
        image_kernel,
        (spectrum, spectrum, shape_of((2, TILE, HALF))),
        [SMEM] + [VMEM] * 6,
        flops=1600000000,
    )(member, corner, right, below, own_block, columns, rows)
    inner = pltpu.VMEM((ORI_DEV * ROWS, TILE), jnp.bfloat16)
    piece, wide = shape_of((2, ROWS, CORE)), shape_of((2, ROWS, CORE), jnp.float32)

    def far(image, out):
        return call(far_kernel, out, [VMEM] * 4, [inner], flops=10000000000)(image, mine, *tables)

    mine = spectra(pixels)
    across = sent(far(image_across, piece), CORE_BIT)
    same = far(image_same, wide)
    merged = call(merge_kernel, piece, [VMEM] * 2, flops=100000000)(same, across)
    merged = sent(merged, CHIP_BIT)
    other = spectra(sent(pixels, CORE_BIT))
    own = call(
        own_kernel,
        wide,
        [SMEM] + [VMEM] * 6,
        [pltpu.VMEM((4 * PAIRS, HALF), jnp.bfloat16), inner],
        flops=2000000000,
    )(member, rows, g, mine, other, *tables)
    out = shape_of((1, ROWS, CORE), jnp.float32)
    return call(finish_kernel, (out, out), [VMEM] * 2)(own, merged)


def solution(mesh):
    placed = (P("tile", None, None), P(None, "tile"), P())
    return jax.shard_map(
        shards,
        mesh=mesh,
        in_specs=placed,
        out_specs=(P("tile", "orient", None), P("tile", "orient", None)),
        check_vma=False,
    )
```

```python
import math

import jax
import jax.numpy as jnp
import numpy as np
from jax import lax
from jax.experimental import pallas as pl
from jax.experimental.pallas import tpu as pltpu
from jax.sharding import PartitionSpec as P

TILE = 512
TS = 128
CORE = 384
GRID_W = 8
TILES = 64
ORI_DEV = 8
MEMBERS = 4
ROWS = 96
ROWS_IN = 224
LENGTH = 256
PAIRS = LENGTH // 2
HALF = TILE // 2
CORE_BIT, CHIP_BIT = 1, 2


def bf16(table):
    return np.asarray(table, np.float64).astype(jnp.bfloat16)


def column_table():
    n = np.arange(TILE)[:, None]
    k = np.arange(HALF)[None, :]
    angle = (math.pi / TILE) * ((n * (2 * k + 1)) % (2 * TILE))
    return bf16(np.concatenate([np.cos(angle), -np.sin(angle)], 1))


def row_table():
    j = np.arange(PAIRS)[:, None]
    m = np.arange(ROWS_IN)[None, :]
    angle = (math.pi / LENGTH) * ((m * (2 * j + 1)) % (2 * LENGTH))
    c, s = np.cos(angle), np.sin(angle)
    parts = []
    for cut in (slice(0, TS), slice(TS, ROWS_IN)):
        u, v = c[:, cut], s[:, cut]
        parts.append(np.block([[u, v], [-v, u], [u, -v], [v, u]]))
    return bf16(np.concatenate(parts, 1))


def inverse_row_table():
    j = np.arange(PAIRS)[None, :]
    c = np.arange(ROWS)[:, None]
    angle = (math.pi / LENGTH) * ((c * (2 * j + 1)) % (2 * LENGTH))
    return bf16(np.concatenate([np.cos(angle), np.sin(angle)], 1))


def inverse_column_table():
    k = np.arange(HALF)[:, None]
    c = np.arange(CORE)[None, :]
    angle = (math.pi / TILE) * ((c * (2 * k + 1)) % (2 * TILE))
    scale = 2.0 / (LENGTH * TILE)
    return bf16(np.concatenate([np.cos(angle), -np.sin(angle)], 0) * scale)


def dot(a, b):
    return jnp.dot(a, b, preferred_element_type=jnp.float32)


def prepare_kernel(
    ids_hbm, micro_hbm, stack_hbm, out_hbm, right_ref, below_ref, corner_ref, ids_ref, micro_ref, stack_ref, out_ref, sems
):
    load_ids = pltpu.make_async_copy(ids_hbm, ids_ref, sems.at[0])
    load_stack = pltpu.make_async_copy(stack_hbm, stack_ref, sems.at[1])
    load_micro = pltpu.make_async_copy(micro_hbm.at[0], micro_ref, sems.at[2])
    load_ids.start()
    load_stack.start()
    load_micro.start()
    row = lax.broadcasted_iota(jnp.int32, (4 * ORI_DEV, 256), 0)
    lane = lax.broadcasted_iota(jnp.int32, (4 * ORI_DEV, 256), 1)
    wanted = jnp.zeros((4 * ORI_DEV, 256), jnp.int32)
    member, side = lax.axis_index("orient"), lax.axis_index("tile") % 2
    load_ids.wait()
    for to_side in range(2):
        first = (member ^ (CHIP_BIT * (side ^ to_side))) * ORI_DEV
        for o in range(ORI_DEV):
            here = (row % ORI_DEV == o) & (row // (2 * ORI_DEV) == to_side)
            wanted = jnp.where(here, ids_ref[first + o], wanted)
    hot = jnp.where(lane == wanted, 1.0, 0.0).astype(jnp.bfloat16)
    load_stack.wait()
    picked = dot(hot, stack_ref[...])
    for to_side in range(2):
        top, middle, end = (2 * to_side * ORI_DEV + k * ORI_DEV for k in range(3))
        both = jnp.concatenate([picked[top:middle, :TS], picked[middle:end, TS:]], 0).astype(jnp.bfloat16)
        out_ref[:, to_side] = jnp.broadcast_to(both[None], (TILES // 2, 2 * ORI_DEV, TS))
    store = pltpu.make_async_copy(out_ref, out_hbm, sems.at[3])
    store.start()
    load_micro.wait()
    right_ref[...] = micro_ref[:, :TS]
    below_ref[...] = micro_ref[:TS, :]
    corner_ref[...] = micro_ref[:TS, :TS]
    store.wait()


def load_kernel(*refs):
    sources, targets, sems = refs[:5], refs[6:11], refs[11]
    loads = [pltpu.make_async_copy(a, b, sems.at[i]) for i, (a, b) in enumerate(zip(sources, targets))]
    for load in loads:
        load.start()
    for load in loads:
        load.wait()


def template_kernel(pixels_ref, col_ref, row_ref, out_ref, shape_ref):
    values = pixels_ref[...].astype(jnp.float32).reshape(TS, ORI_DEV, TS)
    mean = jnp.sum(jnp.sum(values, 0), 1, keepdims=True) / (TS * TS)
    centered = values - mean[None]
    square = jnp.sum(jnp.sum(centered * centered, 0), 1, keepdims=True) / (TS * TS)
    spread = jnp.sqrt(square + 1e-06) * TS
    shape_ref[...] = (centered * (1.0 / spread)[None]).reshape(TS * ORI_DEV, TS)
    shapes = [shape_ref[pl.ds(o, TS, stride=ORI_DEV), :].astype(jnp.bfloat16) for o in range(ORI_DEV)]
    g = dot(jnp.concatenate(shapes, 0), col_ref[:TS]).astype(jnp.bfloat16)
    for o in range(ORI_DEV):
        mine = g[o * TS : (o + 1) * TS]
        mine = jnp.concatenate([mine[:, :HALF], mine[:, HALF:]], 0)
        out_ref[o] = dot(row_ref[:, : 2 * TS], mine).astype(jnp.bfloat16)


def image_columns(own_ref, right_ref, below_ref, corner_ref, col_ref, g_ref):
    def columns(first, second, start, count):
        g = dot(first, col_ref[:CORE]) + dot(second, col_ref[CORE:])
        g_ref[0, start : start + count] = g[:, :HALF].astype(jnp.bfloat16)
        g_ref[1, start : start + count] = g[:, HALF:].astype(jnp.bfloat16)

    columns(own_ref[0], right_ref[...], 0, CORE)
    columns(below_ref[...], corner_ref[...], CORE, TS)


def image_rows(member_ref, row_ref, g_ref, bits, out_ref):
    start = pl.multiple_of((member_ref[0] ^ bits) * ROWS, 32)
    cuts = [(start, TS), (pl.multiple_of(start + TS, 32), ROWS_IN - TS)]
    piece = jnp.concatenate([g_ref[p, pl.ds(*cut)] for cut in cuts for p in range(2)], 0)
    out_ref[...] = dot(row_ref[...], piece).astype(jnp.bfloat16)


def block(image_ref, template_refs, inv_row_ref, inv_col_ref, out_ref, inner_ref):
    def part(ref, p):
        return ref[p * PAIRS : (p + 1) * PAIRS]

    def corr(template_ref):
        for o in range(ORI_DEV):

            def cross(p):
                a, b = part(image_ref, 2 * p), part(image_ref, 2 * p + 1)
                c, d = part(template_ref.at[o], 2 * p), part(template_ref.at[o], 2 * p + 1)
                return a * c + b * d, b * c - a * d

            plus_re, plus_im = cross(0)
            minus_re, minus_im = cross(1)
            mixed = jnp.concatenate(
                [
                    jnp.concatenate([plus_re + minus_re, plus_im + minus_im], 1),
                    jnp.concatenate([minus_im - plus_im, plus_re - minus_re], 1),
                ],
                0,
            )
            inner_ref[o * ROWS : (o + 1) * ROWS] = dot(inv_row_ref[...], mixed).astype(jnp.bfloat16)
        out = dot(inner_ref[...], inv_col_ref[...]).reshape(ORI_DEV, ROWS, CORE)
        return jnp.max(out, 0), jnp.sum(out, 0)

    high, total = corr(template_refs[0])
    for template_ref in template_refs[1:]:
        more, added = corr(template_ref)
        high, total = jnp.maximum(high, more), total + added
    out_ref[0] = high.astype(out_ref.dtype)
    out_ref[1] = total.astype(out_ref.dtype)


def image_kernel(member_ref, *refs):
    corner_ref, right_ref, below_ref, own_ref, col_ref, row_ref, across_ref, same_ref, g_ref = refs
    image_columns(own_ref, right_ref, below_ref, corner_ref, col_ref, g_ref)
    image_rows(member_ref, row_ref, g_ref, CHIP_BIT + CORE_BIT, across_ref)
    image_rows(member_ref, row_ref, g_ref, CHIP_BIT, same_ref)


def far_kernel(image_ref, template_ref, inv_row_ref, inv_col_ref, out_ref, inner_ref):
    block(image_ref, (template_ref,), inv_row_ref, inv_col_ref, out_ref, inner_ref)


def merge_kernel(mine_ref, other_ref, out_ref):
    other = other_ref[...].astype(jnp.float32)
    out_ref[0] = jnp.maximum(mine_ref[0], other[0]).astype(out_ref.dtype)
    out_ref[1] = (mine_ref[1] + other[1]).astype(out_ref.dtype)


def own_kernel(member_ref, row_ref, g_ref, template_ref, inv_row_ref, inv_col_ref, _, out_ref, image_ref, inner_ref):
    image_rows(member_ref, row_ref, g_ref, 0, image_ref)
    block(image_ref, (template_ref,), inv_row_ref, inv_col_ref, out_ref, inner_ref)


def rest_kernel(image_ref, template_ref, inv_row_ref, inv_col_ref, part_ref, out_ref, inner_ref):
    block(image_ref, (template_ref,), inv_row_ref, inv_col_ref, out_ref, inner_ref)
    out_ref[0] = jnp.maximum(out_ref[0], part_ref[0])
    out_ref[1] = out_ref[1] + part_ref[1]


def finish_kernel(own_ref, far_ref, peak_ref, excess_ref):
    far = far_ref[...].astype(jnp.float32)
    peak = jnp.maximum(own_ref[0], far[0])
    peak_ref[0] = peak
    excess_ref[0] = peak - (own_ref[1] + far[1]) / (MEMBERS * ORI_DEV)


VMEM = pl.BlockSpec(memory_space=pltpu.VMEM)
SMEM = pl.BlockSpec(memory_space=pltpu.SMEM)
ANY = pl.BlockSpec(memory_space=pl.ANY)
HBM = pl.BlockSpec(memory_space=pltpu.HBM)
LIMIT = 24 * 1024 * 1024


def call(kernel, outs, specs, scratch=(), flops=0, out_specs=None):
    return pl.pallas_call(
        kernel,
        out_shape=outs,
        in_specs=specs,
        out_specs=out_specs or jax.tree.map(lambda _: VMEM, outs),
        scratch_shapes=list(scratch),
        compiler_params=pltpu.CompilerParams(vmem_limit_bytes=LIMIT),
        cost_estimate=pl.CostEstimate(flops=flops, bytes_accessed=2**21, transcendentals=0),
    )


def shape_of(dims, dtype=jnp.bfloat16):
    return jax.ShapeDtypeStruct(dims, dtype)


def pinned(array):
    return pltpu.with_memory_space_constraint(jnp.asarray(array), pltpu.HBM)


def near_groups():
    return [
        [t * MEMBERS + (chip ^ (CHIP_BIT * (t % 2))) + core for t in range(TILES)] for chip in (0, CHIP_BIT) for core in (0, 1)
    ]


def halo(block, distance):
    route = []
    crosses = distance % GRID_W
    for t in range(TILES):
        source = t + distance
        if t % GRID_W + crosses < GRID_W and source < TILES:
            for o in range(MEMBERS):
                route.append((source * MEMBERS + (o ^ 2 if crosses else o), t * MEMBERS + o))
    return lax.ppermute(block, ("tile", "orient"), route)


def shards(micrograph, template_stack, orient_list):
    spread, right, below, corner = call(
        prepare_kernel,
        (
            shape_of((TILES // 2, 2, 2 * ORI_DEV, TS)),
            shape_of((CORE, TS)),
            shape_of((TS, CORE)),
            shape_of((TS, TS)),
        ),
        [HBM] * 3,
        [
            pltpu.SMEM((MEMBERS * ORI_DEV,), jnp.int32),
            pltpu.VMEM((CORE, CORE), jnp.bfloat16),
            pltpu.VMEM((256, 256), jnp.bfloat16),
            pltpu.VMEM((TILES // 2, 2, 2 * ORI_DEV, TS), jnp.bfloat16),
            pltpu.SemaphoreType.DMA((4,)),
        ],
        out_specs=(HBM, VMEM, VMEM, VMEM),
    )(pinned(orient_list), pinned(micrograph), pinned(template_stack))
    pixels = lax.all_to_all(
        spread.reshape(TILES, 2 * ORI_DEV, TS), ("tile", "orient"), 0, 0, axis_index_groups=near_groups()
    )
    kept = [column_table(), row_table(), inverse_row_table(), inverse_column_table(), micrograph]
    columns, rows, *tables, own_block = call(
        load_kernel,
        tuple(shape_of(array.shape) for array in kept),
        [HBM] * 5 + [ANY],
        [pltpu.SemaphoreType.DMA((5,))],
        flops=10000000000,
    )(*[pinned(array) for array in kept], corner)
    corner = halo(corner, GRID_W + 1)
    right = halo(right, 1)
    below = halo(below, GRID_W)
    member = lax.axis_index("orient")[None]

    def sent(piece, bits):
        return lax.ppermute(piece, "orient", [(i, i ^ bits) for i in range(MEMBERS)])


    def spectra(group):
        return call(
            template_kernel,
            shape_of((ORI_DEV, 4 * PAIRS, HALF)),
            [VMEM] * 3,
            [pltpu.VMEM((TS * ORI_DEV, TS), jnp.float32)],
            flops=1000000000,
        )(group, columns, rows)

    spectrum = shape_of((4 * PAIRS, HALF))
    image_across, image_same, g = call(
        image_kernel,
        (spectrum, spectrum, shape_of((2, TILE, HALF))),
        [SMEM] + [VMEM] * 6,
        flops=1600000000,
    )(member, corner, right, below, own_block, columns, rows)
    inner = pltpu.VMEM((ORI_DEV * ROWS, TILE), jnp.bfloat16)
    piece, wide = shape_of((2, ROWS, CORE)), shape_of((2, ROWS, CORE), jnp.float32)

    def far(image, out):
        return call(far_kernel, out, [VMEM] * 4, [inner], flops=10000000000)(image, mine, *tables)

    mine = spectra(pixels)
    across = sent(far(image_across, piece), CORE_BIT)
    same = far(image_same, wide)
    merged = call(merge_kernel, piece, [VMEM] * 2, flops=100000000)(same, across)
    part, image_own = call(
        own_kernel,
        (wide, spectrum),
        [SMEM] + [VMEM] * 5 + [ANY],
        [inner],
        flops=20000000000,
    )(member, rows, g, mine, *tables, merged)
    merged = sent(merged, CHIP_BIT)
    other = spectra(sent(pixels, CORE_BIT))
    own = call(rest_kernel, wide, [VMEM] * 5, [inner], flops=1000000000)(image_own, other, *tables, part)
    out = shape_of((1, ROWS, CORE), jnp.float32)
    return call(finish_kernel, (out, out), [VMEM] * 2)(own, merged)


def solution(mesh):
    placed = (P("tile", None, None), P(None, "tile"), P())
    return jax.shard_map(
        shards,
        mesh=mesh,
        in_specs=placed,
        out_specs=(P("tile", "orient", None), P("tile", "orient", None)),
        check_vma=False,
    )
```

```python
import math

import jax
import jax.numpy as jnp
import numpy as np
from jax import lax
from jax.experimental import pallas as pl
from jax.experimental.pallas import tpu as pltpu
from jax.sharding import PartitionSpec as P

TILE = 512
TS = 128
CORE = 384
GRID_W = 8
TILES = 64
ORI_DEV = 8
MEMBERS = 4
ROWS = 96
ROWS_IN = 224
LENGTH = 256
PAIRS = LENGTH // 2
HALF = TILE // 2
CORE_BIT, CHIP_BIT = 1, 2


def bf16(table):
    return np.asarray(table, np.float64).astype(jnp.bfloat16)


def column_table():
    n = np.arange(TILE)[:, None]
    k = np.arange(HALF)[None, :]
    angle = (math.pi / TILE) * ((n * (2 * k + 1)) % (2 * TILE))
    return bf16(np.concatenate([np.cos(angle), -np.sin(angle)], 1))


def row_table():
    j = np.arange(PAIRS)[:, None]
    m = np.arange(ROWS_IN)[None, :]
    angle = (math.pi / LENGTH) * ((m * (2 * j + 1)) % (2 * LENGTH))
    c, s = np.cos(angle), np.sin(angle)
    parts = []
    for cut in (slice(0, TS), slice(TS, ROWS_IN)):
        u, v = c[:, cut], s[:, cut]
        parts.append(np.block([[u, v], [-v, u], [u, -v], [v, u]]))
    return bf16(np.concatenate(parts, 1))


def inverse_row_table():
    j = np.arange(PAIRS)[None, :]
    c = np.arange(ROWS)[:, None]
    angle = (math.pi / LENGTH) * ((c * (2 * j + 1)) % (2 * LENGTH))
    return bf16(np.concatenate([np.cos(angle), np.sin(angle)], 1))


def inverse_column_table():
    k = np.arange(HALF)[:, None]
    c = np.arange(CORE)[None, :]
    angle = (math.pi / TILE) * ((c * (2 * k + 1)) % (2 * TILE))
    scale = 2.0 / (LENGTH * TILE)
    return bf16(np.concatenate([np.cos(angle), -np.sin(angle)], 0) * scale)


def dot(a, b):
    return jnp.dot(a, b, preferred_element_type=jnp.float32)


def prepare_kernel(
    ids_hbm, micro_hbm, stack_hbm, out_hbm, right_ref, below_ref, corner_ref, ids_ref, micro_ref, stack_ref, out_ref, sems
):
    load_ids = pltpu.make_async_copy(ids_hbm, ids_ref, sems.at[0])
    load_stack = pltpu.make_async_copy(stack_hbm, stack_ref, sems.at[1])
    load_micro = pltpu.make_async_copy(micro_hbm.at[0], micro_ref, sems.at[2])
    load_ids.start()
    load_stack.start()
    load_micro.start()
    row = lax.broadcasted_iota(jnp.int32, (4 * ORI_DEV, 256), 0)
    lane = lax.broadcasted_iota(jnp.int32, (4 * ORI_DEV, 256), 1)
    wanted = jnp.zeros((4 * ORI_DEV, 256), jnp.int32)
    member, side = lax.axis_index("orient"), lax.axis_index("tile") % 2
    load_ids.wait()
    for to_side in range(2):
        first = (member ^ (CHIP_BIT * (side ^ to_side))) * ORI_DEV
        for o in range(ORI_DEV):
            here = (row % ORI_DEV == o) & (row // (2 * ORI_DEV) == to_side)
            wanted = jnp.where(here, ids_ref[first + o], wanted)
    hot = jnp.where(lane == wanted, 1.0, 0.0).astype(jnp.bfloat16)
    load_stack.wait()
    picked = dot(hot, stack_ref[...])
    for to_side in range(2):
        top, middle, end = (2 * to_side * ORI_DEV + k * ORI_DEV for k in range(3))
        both = jnp.concatenate([picked[top:middle, :TS], picked[middle:end, TS:]], 0).astype(jnp.bfloat16)
        out_ref[:, to_side] = jnp.broadcast_to(both[None], (TILES // 2, 2 * ORI_DEV, TS))
    store = pltpu.make_async_copy(out_ref, out_hbm, sems.at[3])
    store.start()
    load_micro.wait()
    right_ref[...] = micro_ref[:, :TS]
    below_ref[...] = micro_ref[:TS, :]
    corner_ref[...] = micro_ref[:TS, :TS]
    store.wait()


def load_kernel(*refs):
    sources, targets, sems = refs[:5], refs[6:11], refs[11]
    loads = [pltpu.make_async_copy(a, b, sems.at[i]) for i, (a, b) in enumerate(zip(sources, targets))]
    for load in loads:
        load.start()
    for load in loads:
        load.wait()


def template_kernel(pixels_ref, col_ref, row_ref, out_ref, shape_ref):
    values = pixels_ref[...].astype(jnp.float32).reshape(TS, ORI_DEV, TS)
    mean = jnp.sum(jnp.sum(values, 0), 1, keepdims=True) / (TS * TS)
    centered = values - mean[None]
    square = jnp.sum(jnp.sum(centered * centered, 0), 1, keepdims=True) / (TS * TS)
    spread = jnp.sqrt(square + 1e-06) * TS
    shape_ref[...] = (centered * (1.0 / spread)[None]).reshape(TS * ORI_DEV, TS)
    shapes = [shape_ref[pl.ds(o, TS, stride=ORI_DEV), :].astype(jnp.bfloat16) for o in range(ORI_DEV)]
    g = dot(jnp.concatenate(shapes, 0), col_ref[:TS]).astype(jnp.bfloat16)
    for o in range(ORI_DEV):
        mine = g[o * TS : (o + 1) * TS]
        mine = jnp.concatenate([mine[:, :HALF], mine[:, HALF:]], 0)
        out_ref[o] = dot(row_ref[:, : 2 * TS], mine).astype(jnp.bfloat16)


def image_columns(own_ref, right_ref, below_ref, corner_ref, col_ref, g_ref):
    def columns(first, second, start, count):
        g = dot(first, col_ref[:CORE]) + dot(second, col_ref[CORE:])
        g_ref[0, start : start + count] = g[:, :HALF].astype(jnp.bfloat16)
        g_ref[1, start : start + count] = g[:, HALF:].astype(jnp.bfloat16)

    columns(own_ref[0], right_ref[...], 0, CORE)
    columns(below_ref[...], corner_ref[...], CORE, TS)


def image_rows(member_ref, row_ref, g_ref, bits, out_ref):
    start = pl.multiple_of((member_ref[0] ^ bits) * ROWS, 32)
    cuts = [(start, TS), (pl.multiple_of(start + TS, 32), ROWS_IN - TS)]
    piece = jnp.concatenate([g_ref[p, pl.ds(*cut)] for cut in cuts for p in range(2)], 0)
    out_ref[...] = dot(row_ref[...], piece).astype(jnp.bfloat16)


def block(image_ref, template_refs, inv_row_ref, inv_col_ref, out_ref, inner_ref):
    def part(ref, p):
        return ref[p * PAIRS : (p + 1) * PAIRS]

    def corr(template_ref):
        for o in range(ORI_DEV):

            def cross(p):
                a, b = part(image_ref, 2 * p), part(image_ref, 2 * p + 1)
                c, d = part(template_ref.at[o], 2 * p), part(template_ref.at[o], 2 * p + 1)
                return a * c + b * d, b * c - a * d

            plus_re, plus_im = cross(0)
            minus_re, minus_im = cross(1)
            mixed = jnp.concatenate(
                [
                    jnp.concatenate([plus_re + minus_re, plus_im + minus_im], 1),
                    jnp.concatenate([minus_im - plus_im, plus_re - minus_re], 1),
                ],
                0,
            )
            inner_ref[o * ROWS : (o + 1) * ROWS] = dot(inv_row_ref[...], mixed).astype(jnp.bfloat16)
        out = dot(inner_ref[...], inv_col_ref[...]).reshape(ORI_DEV, ROWS, CORE)
        return jnp.max(out, 0), jnp.sum(out, 0)

    high, total = corr(template_refs[0])
    for template_ref in template_refs[1:]:
        more, added = corr(template_ref)
        high, total = jnp.maximum(high, more), total + added
    out_ref[0] = high.astype(out_ref.dtype)
    out_ref[1] = total.astype(out_ref.dtype)


def image_kernel(member_ref, *refs):
    corner_ref, right_ref, below_ref, own_ref, col_ref, row_ref, across_ref, same_ref, g_ref = refs
    image_columns(own_ref, right_ref, below_ref, corner_ref, col_ref, g_ref)
    image_rows(member_ref, row_ref, g_ref, CHIP_BIT + CORE_BIT, across_ref)
    image_rows(member_ref, row_ref, g_ref, CHIP_BIT, same_ref)


def far_kernel(image_ref, template_ref, inv_row_ref, inv_col_ref, out_ref, inner_ref):
    block(image_ref, (template_ref,), inv_row_ref, inv_col_ref, out_ref, inner_ref)


def merge_kernel(mine_ref, other_ref, pixels_ref, out_ref, copy_ref):
    copy_ref[...] = pixels_ref[...]
    other = other_ref[...].astype(jnp.float32)
    out_ref[0] = jnp.maximum(mine_ref[0], other[0]).astype(out_ref.dtype)
    out_ref[1] = (mine_ref[1] + other[1]).astype(out_ref.dtype)


def own_kernel(member_ref, row_ref, g_ref, template_ref, inv_row_ref, inv_col_ref, _, out_ref, image_ref, inner_ref):
    image_rows(member_ref, row_ref, g_ref, 0, image_ref)
    block(image_ref, (template_ref,), inv_row_ref, inv_col_ref, out_ref, inner_ref)


def rest_kernel(image_ref, template_ref, inv_row_ref, inv_col_ref, part_ref, out_ref, inner_ref):
    block(image_ref, (template_ref,), inv_row_ref, inv_col_ref, out_ref, inner_ref)
    out_ref[0] = jnp.maximum(out_ref[0], part_ref[0])
    out_ref[1] = out_ref[1] + part_ref[1]


def finish_kernel(own_ref, far_ref, peak_ref, excess_ref):
    far = far_ref[...].astype(jnp.float32)
    peak = jnp.maximum(own_ref[0], far[0])
    peak_ref[0] = peak
    excess_ref[0] = peak - (own_ref[1] + far[1]) / (MEMBERS * ORI_DEV)


VMEM = pl.BlockSpec(memory_space=pltpu.VMEM)
SMEM = pl.BlockSpec(memory_space=pltpu.SMEM)
ANY = pl.BlockSpec(memory_space=pl.ANY)
HBM = pl.BlockSpec(memory_space=pltpu.HBM)
LIMIT = 24 * 1024 * 1024


def call(kernel, outs, specs, scratch=(), flops=0, out_specs=None):
    return pl.pallas_call(
        kernel,
        out_shape=outs,
        in_specs=specs,
        out_specs=out_specs or jax.tree.map(lambda _: VMEM, outs),
        scratch_shapes=list(scratch),
        compiler_params=pltpu.CompilerParams(vmem_limit_bytes=LIMIT),
        cost_estimate=pl.CostEstimate(flops=flops, bytes_accessed=2**21, transcendentals=0),
    )


def shape_of(dims, dtype=jnp.bfloat16):
    return jax.ShapeDtypeStruct(dims, dtype)


def pinned(array):
    return pltpu.with_memory_space_constraint(jnp.asarray(array), pltpu.HBM)


def near_groups():
    return [
        [t * MEMBERS + (chip ^ (CHIP_BIT * (t % 2))) + core for t in range(TILES)] for chip in (0, CHIP_BIT) for core in (0, 1)
    ]


def halo(block, distance):
    route = []
    crosses = distance % GRID_W
    for t in range(TILES):
        source = t + distance
        if t % GRID_W + crosses < GRID_W and source < TILES:
            for o in range(MEMBERS):
                route.append((source * MEMBERS + (o ^ 2 if crosses else o), t * MEMBERS + o))
    return lax.ppermute(block, ("tile", "orient"), route)


def shards(micrograph, template_stack, orient_list):
    spread, right, below, corner = call(
        prepare_kernel,
        (
            shape_of((TILES // 2, 2, 2 * ORI_DEV, TS)),
            shape_of((CORE, TS)),
            shape_of((TS, CORE)),
            shape_of((TS, TS)),
        ),
        [HBM] * 3,
        [
            pltpu.SMEM((MEMBERS * ORI_DEV,), jnp.int32),
            pltpu.VMEM((CORE, CORE), jnp.bfloat16),
            pltpu.VMEM((256, 256), jnp.bfloat16),
            pltpu.VMEM((TILES // 2, 2, 2 * ORI_DEV, TS), jnp.bfloat16),
            pltpu.SemaphoreType.DMA((4,)),
        ],
        out_specs=(HBM, VMEM, VMEM, VMEM),
    )(pinned(orient_list), pinned(micrograph), pinned(template_stack))
    pixels = lax.all_to_all(
        spread.reshape(TILES, 2 * ORI_DEV, TS), ("tile", "orient"), 0, 0, axis_index_groups=near_groups()
    )
    kept = [column_table(), row_table(), inverse_row_table(), inverse_column_table(), micrograph]
    columns, rows, *tables, own_block = call(
        load_kernel,
        tuple(shape_of(array.shape) for array in kept),
        [HBM] * 5 + [ANY],
        [pltpu.SemaphoreType.DMA((5,))],
        flops=10000000000,
    )(*[pinned(array) for array in kept], corner)
    corner = halo(corner, GRID_W + 1)
    right = halo(right, 1)
    below = halo(below, GRID_W)
    member = lax.axis_index("orient")[None]

    def sent(piece, bits):
        return lax.ppermute(piece, "orient", [(i, i ^ bits) for i in range(MEMBERS)])


    def spectra(group):
        return call(
            template_kernel,
            shape_of((ORI_DEV, 4 * PAIRS, HALF)),
            [VMEM] * 3,
            [pltpu.VMEM((TS * ORI_DEV, TS), jnp.float32)],
            flops=1000000000,
        )(group, columns, rows)

    spectrum = shape_of((4 * PAIRS, HALF))
    image_across, image_same, g = call(
        image_kernel,
        (spectrum, spectrum, shape_of((2, TILE, HALF))),
        [SMEM] + [VMEM] * 6,
        flops=1600000000,
    )(member, corner, right, below, own_block, columns, rows)
    inner = pltpu.VMEM((ORI_DEV * ROWS, TILE), jnp.bfloat16)
    piece, wide = shape_of((2, ROWS, CORE)), shape_of((2, ROWS, CORE), jnp.float32)

    def far(image, out):
        return call(far_kernel, out, [VMEM] * 4, [inner], flops=10000000000)(image, mine, *tables)

    mine = spectra(pixels)
    across = sent(far(image_across, piece), CORE_BIT)
    same = far(image_same, wide)
    merged, again = call(merge_kernel, (piece, shape_of(pixels.shape)), [VMEM] * 3, flops=100000000)(same, across, pixels)
    part, image_own = call(
        own_kernel,
        (wide, spectrum),
        [SMEM] + [VMEM] * 5 + [ANY],
        [inner],
        flops=20000000000,
    )(member, rows, g, mine, *tables, merged)
    merged = sent(merged, CHIP_BIT)
    other = spectra(sent(again, CORE_BIT))
    own = call(rest_kernel, wide, [VMEM] * 5, [inner], flops=1000000000)(image_own, other, *tables, part)
    out = shape_of((1, ROWS, CORE), jnp.float32)
    return call(finish_kernel, (out, out), [VMEM] * 2)(own, merged)


def solution(mesh):
    placed = (P("tile", None, None), P(None, "tile"), P())
    return jax.shard_map(
        shards,
        mesh=mesh,
        in_specs=placed,
        out_specs=(P("tile", "orient", None), P("tile", "orient", None)),
        check_vma=False,
    )
```

```python
import math

import jax
import jax.numpy as jnp
import numpy as np
from jax import lax
from jax.experimental import pallas as pl
from jax.experimental.pallas import tpu as pltpu
from jax.sharding import PartitionSpec as P

TILE = 512
TS = 128
CORE = 384
GRID_W = 8
TILES = 64
ORI_DEV = 8
MEMBERS = 4
ROWS = 96
ROWS_IN = 224
LENGTH = 256
PAIRS = LENGTH // 2
HALF = TILE // 2
CORE_BIT, CHIP_BIT = 1, 2


def bf16(table):
    return np.asarray(table, np.float64).astype(jnp.bfloat16)


def column_table():
    n = np.arange(TILE)[:, None]
    k = np.arange(HALF)[None, :]
    angle = (math.pi / TILE) * ((n * (2 * k + 1)) % (2 * TILE))
    return bf16(np.concatenate([np.cos(angle), -np.sin(angle)], 1))


def row_table():
    j = np.arange(PAIRS)[:, None]
    m = np.arange(ROWS_IN)[None, :]
    angle = (math.pi / LENGTH) * ((m * (2 * j + 1)) % (2 * LENGTH))
    c, s = np.cos(angle), np.sin(angle)
    parts = []
    for cut in (slice(0, TS), slice(TS, ROWS_IN)):
        u, v = c[:, cut], s[:, cut]
        parts.append(np.block([[u, v], [-v, u], [u, -v], [v, u]]))
    return bf16(np.concatenate(parts, 1))


def inverse_row_table():
    j = np.arange(PAIRS)[None, :]
    c = np.arange(ROWS)[:, None]
    angle = (math.pi / LENGTH) * ((c * (2 * j + 1)) % (2 * LENGTH))
    return bf16(np.concatenate([np.cos(angle), np.sin(angle)], 1))


def inverse_column_table():
    k = np.arange(HALF)[:, None]
    c = np.arange(CORE)[None, :]
    angle = (math.pi / TILE) * ((c * (2 * k + 1)) % (2 * TILE))
    scale = 2.0 / (LENGTH * TILE)
    return bf16(np.concatenate([np.cos(angle), -np.sin(angle)], 0) * scale)


def dot(a, b):
    return jnp.dot(a, b, preferred_element_type=jnp.float32)


def prepare_kernel(
    ids_hbm, micro_hbm, stack_hbm, out_hbm, right_ref, below_ref, corner_ref, ids_ref, micro_ref, stack_ref, out_ref, sems
):
    load_ids = pltpu.make_async_copy(ids_hbm, ids_ref, sems.at[0])
    load_stack = pltpu.make_async_copy(stack_hbm, stack_ref, sems.at[1])
    load_micro = pltpu.make_async_copy(micro_hbm.at[0], micro_ref, sems.at[2])
    load_ids.start()
    load_stack.start()
    load_micro.start()
    row = lax.broadcasted_iota(jnp.int32, (4 * ORI_DEV, 256), 0)
    lane = lax.broadcasted_iota(jnp.int32, (4 * ORI_DEV, 256), 1)
    wanted = jnp.zeros((4 * ORI_DEV, 256), jnp.int32)
    member, side = lax.axis_index("orient"), lax.axis_index("tile") % 2
    load_ids.wait()
    for to_side in range(2):
        first = (member ^ (CHIP_BIT * (side ^ to_side))) * ORI_DEV
        for o in range(ORI_DEV):
            here = (row % ORI_DEV == o) & (row // (2 * ORI_DEV) == to_side)
            wanted = jnp.where(here, ids_ref[first + o], wanted)
    hot = jnp.where(lane == wanted, 1.0, 0.0).astype(jnp.bfloat16)
    load_stack.wait()
    picked = dot(hot, stack_ref[...])
    for to_side in range(2):
        top, middle, end = (2 * to_side * ORI_DEV + k * ORI_DEV for k in range(3))
        both = jnp.concatenate([picked[top:middle, :TS], picked[middle:end, TS:]], 0).astype(jnp.bfloat16)
        out_ref[:, to_side] = jnp.broadcast_to(both[None], (TILES // 2, 2 * ORI_DEV, TS))
    store = pltpu.make_async_copy(out_ref, out_hbm, sems.at[3])
    store.start()
    load_micro.wait()
    right_ref[...] = micro_ref[:, :TS]
    below_ref[...] = micro_ref[:TS, :]
    corner_ref[...] = micro_ref[:TS, :TS]
    store.wait()


def load_kernel(*refs):
    sources, targets, sems = refs[:5], refs[6:11], refs[11]
    loads = [pltpu.make_async_copy(a, b, sems.at[i]) for i, (a, b) in enumerate(zip(sources, targets))]
    for load in loads:
        load.start()
    for load in loads:
        load.wait()


def template_kernel(pixels_ref, col_ref, row_ref, out_ref, shape_ref):
    values = pixels_ref[...].astype(jnp.float32).reshape(TS, ORI_DEV, TS)
    mean = jnp.sum(jnp.sum(values, 0), 1, keepdims=True) / (TS * TS)
    centered = values - mean[None]
    square = jnp.sum(jnp.sum(centered * centered, 0), 1, keepdims=True) / (TS * TS)
    spread = jnp.sqrt(square + 1e-06) * TS
    shape_ref[...] = (centered * (1.0 / spread)[None]).reshape(TS * ORI_DEV, TS)
    shapes = [shape_ref[pl.ds(o, TS, stride=ORI_DEV), :].astype(jnp.bfloat16) for o in range(ORI_DEV)]
    g = dot(jnp.concatenate(shapes, 0), col_ref[:TS]).astype(jnp.bfloat16)
    for o in range(ORI_DEV):
        mine = g[o * TS : (o + 1) * TS]
        mine = jnp.concatenate([mine[:, :HALF], mine[:, HALF:]], 0)
        out_ref[o] = dot(row_ref[:, : 2 * TS], mine).astype(jnp.bfloat16)


def image_columns(own_ref, right_ref, below_ref, corner_ref, col_ref, g_ref):
    def columns(first, second, start, count):
        g = dot(first, col_ref[:CORE]) + dot(second, col_ref[CORE:])
        g_ref[0, start : start + count] = g[:, :HALF].astype(jnp.bfloat16)
        g_ref[1, start : start + count] = g[:, HALF:].astype(jnp.bfloat16)

    columns(own_ref[0], right_ref[...], 0, CORE)
    columns(below_ref[...], corner_ref[...], CORE, TS)


def image_rows(member_ref, row_ref, g_ref, bits, out_ref):
    start = pl.multiple_of((member_ref[0] ^ bits) * ROWS, 32)
    cuts = [(start, TS), (pl.multiple_of(start + TS, 32), ROWS_IN - TS)]
    piece = jnp.concatenate([g_ref[p, pl.ds(*cut)] for cut in cuts for p in range(2)], 0)
    out_ref[...] = dot(row_ref[...], piece).astype(jnp.bfloat16)


def block(image_ref, template_refs, inv_row_ref, inv_col_ref, out_ref, inner_ref):
    def part(ref, p):
        return ref[p * PAIRS : (p + 1) * PAIRS]

    def corr(template_ref):
        for o in range(ORI_DEV):

            def cross(p):
                a, b = part(image_ref, 2 * p), part(image_ref, 2 * p + 1)
                c, d = part(template_ref.at[o], 2 * p), part(template_ref.at[o], 2 * p + 1)
                return a * c + b * d, b * c - a * d

            plus_re, plus_im = cross(0)
            minus_re, minus_im = cross(1)
            mixed = jnp.concatenate(
                [
                    jnp.concatenate([plus_re + minus_re, plus_im + minus_im], 1),
                    jnp.concatenate([minus_im - plus_im, plus_re - minus_re], 1),
                ],
                0,
            )
            inner_ref[o * ROWS : (o + 1) * ROWS] = dot(inv_row_ref[...], mixed).astype(jnp.bfloat16)
        out = dot(inner_ref[...], inv_col_ref[...]).reshape(ORI_DEV, ROWS, CORE)
        return jnp.max(out, 0), jnp.sum(out, 0)

    high, total = corr(template_refs[0])
    for template_ref in template_refs[1:]:
        more, added = corr(template_ref)
        high, total = jnp.maximum(high, more), total + added
    out_ref[0] = high.astype(out_ref.dtype)
    out_ref[1] = total.astype(out_ref.dtype)


def image_kernel(member_ref, *refs):
    corner_ref, below_ref, right_ref, own_ref, col_ref, row_ref, across_ref, same_ref, g_ref = refs
    image_columns(own_ref, right_ref, below_ref, corner_ref, col_ref, g_ref)
    image_rows(member_ref, row_ref, g_ref, CHIP_BIT + CORE_BIT, across_ref)
    image_rows(member_ref, row_ref, g_ref, CHIP_BIT, same_ref)


def far_kernel(image_ref, template_ref, inv_row_ref, inv_col_ref, out_ref, inner_ref):
    block(image_ref, (template_ref,), inv_row_ref, inv_col_ref, out_ref, inner_ref)


def merge_kernel(mine_ref, other_ref, out_ref):
    other = other_ref[...].astype(jnp.float32)
    out_ref[0] = jnp.maximum(mine_ref[0], other[0]).astype(out_ref.dtype)
    out_ref[1] = (mine_ref[1] + other[1]).astype(out_ref.dtype)


def own_kernel(member_ref, row_ref, g_ref, mine_ref, other_ref, inv_row_ref, inv_col_ref, out_ref, image_ref, inner_ref):
    image_rows(member_ref, row_ref, g_ref, 0, image_ref)
    block(image_ref, (mine_ref, other_ref), inv_row_ref, inv_col_ref, out_ref, inner_ref)


def finish_kernel(own_ref, far_ref, peak_ref, excess_ref):
    far = far_ref[...].astype(jnp.float32)
    peak = jnp.maximum(own_ref[0], far[0])
    peak_ref[0] = peak
    excess_ref[0] = peak - (own_ref[1] + far[1]) / (MEMBERS * ORI_DEV)


VMEM = pl.BlockSpec(memory_space=pltpu.VMEM)
SMEM = pl.BlockSpec(memory_space=pltpu.SMEM)
ANY = pl.BlockSpec(memory_space=pl.ANY)
HBM = pl.BlockSpec(memory_space=pltpu.HBM)
LIMIT = 24 * 1024 * 1024


def call(kernel, outs, specs, scratch=(), flops=0, out_specs=None):
    return pl.pallas_call(
        kernel,
        out_shape=outs,
        in_specs=specs,
        out_specs=out_specs or jax.tree.map(lambda _: VMEM, outs),
        scratch_shapes=list(scratch),
        compiler_params=pltpu.CompilerParams(vmem_limit_bytes=LIMIT),
        cost_estimate=pl.CostEstimate(flops=flops, bytes_accessed=2**21, transcendentals=0),
    )


def shape_of(dims, dtype=jnp.bfloat16):
    return jax.ShapeDtypeStruct(dims, dtype)


def pinned(array):
    return pltpu.with_memory_space_constraint(jnp.asarray(array), pltpu.HBM)


def near_groups():
    return [
        [t * MEMBERS + (chip ^ (CHIP_BIT * (t % 2))) + core for t in range(TILES)] for chip in (0, CHIP_BIT) for core in (0, 1)
    ]


def halo(block, distance):
    route = []
    crosses = distance % GRID_W
    for t in range(TILES):
        source = t + distance
        if t % GRID_W + crosses < GRID_W and source < TILES:
            for o in range(MEMBERS):
                route.append((source * MEMBERS + (o ^ 2 if crosses else o), t * MEMBERS + o))
    return lax.ppermute(block, ("tile", "orient"), route)


def shards(micrograph, template_stack, orient_list):
    spread, right, below, corner = call(
        prepare_kernel,
        (
            shape_of((TILES // 2, 2, 2 * ORI_DEV, TS)),
            shape_of((CORE, TS)),
            shape_of((TS, CORE)),
            shape_of((TS, TS)),
        ),
        [HBM] * 3,
        [
            pltpu.SMEM((MEMBERS * ORI_DEV,), jnp.int32),
            pltpu.VMEM((CORE, CORE), jnp.bfloat16),
            pltpu.VMEM((256, 256), jnp.bfloat16),
            pltpu.VMEM((TILES // 2, 2, 2 * ORI_DEV, TS), jnp.bfloat16),
            pltpu.SemaphoreType.DMA((4,)),
        ],
        out_specs=(HBM, VMEM, VMEM, VMEM),
    )(pinned(orient_list), pinned(micrograph), pinned(template_stack))
    pixels = lax.all_to_all(
        spread.reshape(TILES, 2 * ORI_DEV, TS), ("tile", "orient"), 0, 0, axis_index_groups=near_groups()
    )
    kept = [column_table(), row_table(), inverse_row_table(), inverse_column_table(), micrograph]
    columns, rows, *tables, own_block = call(
        load_kernel,
        tuple(shape_of(array.shape) for array in kept),
        [HBM] * 5 + [ANY],
        [pltpu.SemaphoreType.DMA((5,))],
        flops=10000000000,
    )(*[pinned(array) for array in kept], corner)
    corner = halo(corner, GRID_W + 1)
    below = halo(below, GRID_W)
    right = halo(right, 1)
    member = lax.axis_index("orient")[None]

    def sent(piece, bits):
        return lax.ppermute(piece, "orient", [(i, i ^ bits) for i in range(MEMBERS)])


    def spectra(group):
        return call(
            template_kernel,
            shape_of((ORI_DEV, 4 * PAIRS, HALF)),
            [VMEM] * 3,
            [pltpu.VMEM((TS * ORI_DEV, TS), jnp.float32)],
            flops=1000000000,
        )(group, columns, rows)

    spectrum = shape_of((4 * PAIRS, HALF))
    image_across, image_same, g = call(
        image_kernel,
        (spectrum, spectrum, shape_of((2, TILE, HALF))),
        [SMEM] + [VMEM] * 6,
        flops=1600000000,
    )(member, corner, below, right, own_block, columns, rows)
    inner = pltpu.VMEM((ORI_DEV * ROWS, TILE), jnp.bfloat16)
    piece, wide = shape_of((2, ROWS, CORE)), shape_of((2, ROWS, CORE), jnp.float32)

    def far(image, out):
        return call(far_kernel, out, [VMEM] * 4, [inner], flops=10000000000)(image, mine, *tables)

    mine = spectra(pixels)
    across = sent(far(image_across, piece), CORE_BIT)
    same = far(image_same, wide)
    merged = call(merge_kernel, piece, [VMEM] * 2, flops=100000000)(same, across)
    merged = sent(merged, CHIP_BIT)
    other = spectra(sent(pixels, CORE_BIT))
    own = call(
        own_kernel,
        wide,
        [SMEM] + [VMEM] * 6,
        [pltpu.VMEM((4 * PAIRS, HALF), jnp.bfloat16), inner],
        flops=2000000000,
    )(member, rows, g, mine, other, *tables)
    out = shape_of((1, ROWS, CORE), jnp.float32)
    return call(finish_kernel, (out, out), [VMEM] * 2)(own, merged)


def solution(mesh):
    placed = (P("tile", None, None), P(None, "tile"), P())
    return jax.shard_map(
        shards,
        mesh=mesh,
        in_specs=placed,
        out_specs=(P("tile", "orient", None), P("tile", "orient", None)),
        check_vma=False,
    )
```

```python
import math

import jax
import jax.numpy as jnp
import numpy as np
from jax import lax
from jax.experimental import pallas as pl
from jax.experimental.pallas import tpu as pltpu
from jax.sharding import PartitionSpec as P

TILE = 512
TS = 128
CORE = 384
GRID_W = 8
TILES = 64
ORI_DEV = 8
MEMBERS = 4
ROWS = 96
ROWS_IN = 224
LENGTH = 256
PAIRS = LENGTH // 2
HALF = TILE // 2
CORE_BIT, CHIP_BIT = 1, 2


def bf16(table):
    return np.asarray(table, np.float64).astype(jnp.bfloat16)


def column_table():
    n = np.arange(TILE)[:, None]
    k = np.arange(HALF)[None, :]
    angle = (math.pi / TILE) * ((n * (2 * k + 1)) % (2 * TILE))
    return bf16(np.concatenate([np.cos(angle), -np.sin(angle)], 1))


def row_table():
    j = np.arange(PAIRS)[:, None]
    m = np.arange(ROWS_IN)[None, :]
    angle = (math.pi / LENGTH) * ((m * (2 * j + 1)) % (2 * LENGTH))
    c, s = np.cos(angle), np.sin(angle)
    parts = []
    for cut in (slice(0, TS), slice(TS, ROWS_IN)):
        u, v = c[:, cut], s[:, cut]
        parts.append(np.block([[u, v], [-v, u], [u, -v], [v, u]]))
    return bf16(np.concatenate(parts, 1))


def inverse_row_table():
    j = np.arange(PAIRS)[None, :]
    c = np.arange(ROWS)[:, None]
    angle = (math.pi / LENGTH) * ((c * (2 * j + 1)) % (2 * LENGTH))
    return bf16(np.concatenate([np.cos(angle), np.sin(angle)], 1))


def inverse_column_table():
    k = np.arange(HALF)[:, None]
    c = np.arange(CORE)[None, :]
    angle = (math.pi / TILE) * ((c * (2 * k + 1)) % (2 * TILE))
    scale = 2.0 / (LENGTH * TILE)
    return bf16(np.concatenate([np.cos(angle), -np.sin(angle)], 0) * scale)


def dot(a, b):
    return jnp.dot(a, b, preferred_element_type=jnp.float32)


def prepare_kernel(
    ids_hbm, micro_hbm, stack_hbm, out_hbm, right_ref, below_ref, corner_ref, ids_ref, micro_ref, stack_ref, out_ref, sems
):
    load_ids = pltpu.make_async_copy(ids_hbm, ids_ref, sems.at[0])
    load_stack = pltpu.make_async_copy(stack_hbm, stack_ref, sems.at[1])
    load_micro = pltpu.make_async_copy(micro_hbm.at[0], micro_ref, sems.at[2])
    load_ids.start()
    load_stack.start()
    load_micro.start()
    row = lax.broadcasted_iota(jnp.int32, (4 * ORI_DEV, 256), 0)
    lane = lax.broadcasted_iota(jnp.int32, (4 * ORI_DEV, 256), 1)
    wanted = jnp.zeros((4 * ORI_DEV, 256), jnp.int32)
    member, side = lax.axis_index("orient"), lax.axis_index("tile") % 2
    load_ids.wait()
    for to_side in range(2):
        first = (member ^ (CHIP_BIT * (side ^ to_side))) * ORI_DEV
        for o in range(ORI_DEV):
            here = (row % ORI_DEV == o) & (row // (2 * ORI_DEV) == to_side)
            wanted = jnp.where(here, ids_ref[first + o], wanted)
    hot = jnp.where(lane == wanted, 1.0, 0.0).astype(jnp.bfloat16)
    load_stack.wait()
    picked = dot(hot, stack_ref[...])
    for to_side in range(2):
        top, middle, end = (2 * to_side * ORI_DEV + k * ORI_DEV for k in range(3))
        both = jnp.concatenate([picked[top:middle, :TS], picked[middle:end, TS:]], 0).astype(jnp.bfloat16)
        out_ref[:, to_side] = jnp.broadcast_to(both[None], (TILES // 2, 2 * ORI_DEV, TS))
    store = pltpu.make_async_copy(out_ref, out_hbm, sems.at[3])
    store.start()
    load_micro.wait()
    right_ref[...] = micro_ref[:, :TS]
    below_ref[...] = micro_ref[:TS, :]
    corner_ref[...] = micro_ref[:TS, :TS]
    store.wait()


def load_kernel(*refs):
    sources, targets, sems = refs[:5], refs[6:11], refs[11]
    loads = [pltpu.make_async_copy(a, b, sems.at[i]) for i, (a, b) in enumerate(zip(sources, targets))]
    for load in loads:
        load.start()
    for load in loads:
        load.wait()


def template_kernel(pixels_ref, col_ref, row_ref, out_ref, shape_ref):
    values = pixels_ref[...].astype(jnp.float32).reshape(TS, ORI_DEV, TS)
    mean = jnp.sum(jnp.sum(values, 0), 1, keepdims=True) / (TS * TS)
    centered = values - mean[None]
    square = jnp.sum(jnp.sum(centered * centered, 0), 1, keepdims=True) / (TS * TS)
    spread = jnp.sqrt(square + 1e-06) * TS
    shape_ref[...] = (centered * (1.0 / spread)[None]).reshape(TS * ORI_DEV, TS)
    shapes = [shape_ref[pl.ds(o, TS, stride=ORI_DEV), :].astype(jnp.bfloat16) for o in range(ORI_DEV)]
    g = dot(jnp.concatenate(shapes, 0), col_ref[:TS]).astype(jnp.bfloat16)
    for o in range(ORI_DEV):
        mine = g[o * TS : (o + 1) * TS]
        mine = jnp.concatenate([mine[:, :HALF], mine[:, HALF:]], 0)
        out_ref[o] = dot(row_ref[:, : 2 * TS], mine).astype(jnp.bfloat16)


def image_columns(own_ref, right_ref, below_ref, corner_ref, col_ref, g_ref):
    def columns(first, second, start, count):
        g = dot(first, col_ref[:CORE]) + dot(second, col_ref[CORE:])
        g_ref[0, start : start + count] = g[:, :HALF].astype(jnp.bfloat16)
        g_ref[1, start : start + count] = g[:, HALF:].astype(jnp.bfloat16)

    columns(own_ref[0], right_ref[...], 0, CORE)
    columns(below_ref[...], corner_ref[...], CORE, TS)


def image_rows(member_ref, row_ref, g_ref, bits, out_ref):
    start = pl.multiple_of((member_ref[0] ^ bits) * ROWS, 32)
    cuts = [(start, TS), (pl.multiple_of(start + TS, 32), ROWS_IN - TS)]
    piece = jnp.concatenate([g_ref[p, pl.ds(*cut)] for cut in cuts for p in range(2)], 0)
    out_ref[...] = dot(row_ref[...], piece).astype(jnp.bfloat16)


def block(image_ref, template_refs, inv_row_ref, inv_col_ref, out_ref, inner_ref):
    def part(ref, p):
        return ref[p * PAIRS : (p + 1) * PAIRS]

    def corr(template_ref):
        for o in range(ORI_DEV):

            def cross(p):
                a, b = part(image_ref, 2 * p), part(image_ref, 2 * p + 1)
                c, d = part(template_ref.at[o], 2 * p), part(template_ref.at[o], 2 * p + 1)
                return a * c + b * d, b * c - a * d

            plus_re, plus_im = cross(0)
            minus_re, minus_im = cross(1)
            mixed = jnp.concatenate(
                [
                    jnp.concatenate([plus_re + minus_re, plus_im + minus_im], 1),
                    jnp.concatenate([minus_im - plus_im, plus_re - minus_re], 1),
                ],
                0,
            )
            inner_ref[o * ROWS : (o + 1) * ROWS] = dot(inv_row_ref[...], mixed).astype(jnp.bfloat16)
        out = dot(inner_ref[...], inv_col_ref[...]).reshape(ORI_DEV, ROWS, CORE)
        return jnp.max(out, 0), jnp.sum(out, 0)

    high, total = corr(template_refs[0])
    for template_ref in template_refs[1:]:
        more, added = corr(template_ref)
        high, total = jnp.maximum(high, more), total + added
    out_ref[0] = high.astype(out_ref.dtype)
    out_ref[1] = total.astype(out_ref.dtype)


def image_kernel(member_ref, *refs):
    corner_ref, right_ref, below_ref, own_ref, col_ref, row_ref, across_ref, same_ref, g_ref = refs
    image_columns(own_ref, right_ref, below_ref, corner_ref, col_ref, g_ref)
    image_rows(member_ref, row_ref, g_ref, CHIP_BIT + CORE_BIT, across_ref)
    image_rows(member_ref, row_ref, g_ref, CHIP_BIT, same_ref)


def far_kernel(image_ref, template_ref, inv_row_ref, inv_col_ref, out_ref, inner_ref):
    block(image_ref, (template_ref,), inv_row_ref, inv_col_ref, out_ref, inner_ref)


def merge_kernel(mine_ref, other_ref, out_ref):
    other = other_ref[...].astype(jnp.float32)
    out_ref[0] = jnp.maximum(mine_ref[0], other[0]).astype(out_ref.dtype)
    out_ref[1] = (mine_ref[1] + other[1]).astype(out_ref.dtype)


def own_kernel(member_ref, row_ref, g_ref, mine_ref, other_ref, inv_row_ref, inv_col_ref, out_ref, image_ref, inner_ref):
    image_rows(member_ref, row_ref, g_ref, 0, image_ref)
    block(image_ref, (mine_ref, other_ref), inv_row_ref, inv_col_ref, out_ref, inner_ref)


def finish_kernel(own_ref, far_ref, peak_hbm, excess_hbm, out_ref, sems):
    half = ROWS // 2
    stores = []
    for k in range(2):
        rows = pl.ds(k * half, half)
        peak = jnp.maximum(own_ref[0, rows], far_ref[0, rows].astype(jnp.float32))
        total = own_ref[1, rows] + far_ref[1, rows].astype(jnp.float32)
        out_ref[0, rows] = peak
        out_ref[1, rows] = peak - total * (1.0 / (MEMBERS * ORI_DEV))
        for i, target in enumerate((peak_hbm, excess_hbm)):
            store = pltpu.make_async_copy(out_ref.at[i, rows], target.at[0, rows], sems.at[2 * k + i])
            store.start()
            stores.append(store)
    for store in stores:
        store.wait()


VMEM = pl.BlockSpec(memory_space=pltpu.VMEM)
SMEM = pl.BlockSpec(memory_space=pltpu.SMEM)
ANY = pl.BlockSpec(memory_space=pl.ANY)
HBM = pl.BlockSpec(memory_space=pltpu.HBM)
LIMIT = 24 * 1024 * 1024


def call(kernel, outs, specs, scratch=(), flops=0, out_specs=None):
    return pl.pallas_call(
        kernel,
        out_shape=outs,
        in_specs=specs,
        out_specs=out_specs or jax.tree.map(lambda _: VMEM, outs),
        scratch_shapes=list(scratch),
        compiler_params=pltpu.CompilerParams(vmem_limit_bytes=LIMIT),
        cost_estimate=pl.CostEstimate(flops=flops, bytes_accessed=2**21, transcendentals=0),
    )


def shape_of(dims, dtype=jnp.bfloat16):
    return jax.ShapeDtypeStruct(dims, dtype)


def pinned(array):
    return pltpu.with_memory_space_constraint(jnp.asarray(array), pltpu.HBM)


def near_groups():
    return [
        [t * MEMBERS + (chip ^ (CHIP_BIT * (t % 2))) + core for t in range(TILES)] for chip in (0, CHIP_BIT) for core in (0, 1)
    ]


def halo(block, distance):
    route = []
    crosses = distance % GRID_W
    for t in range(TILES):
        source = t + distance
        if t % GRID_W + crosses < GRID_W and source < TILES:
            for o in range(MEMBERS):
                route.append((source * MEMBERS + (o ^ 2 if crosses else o), t * MEMBERS + o))
    return lax.ppermute(block, ("tile", "orient"), route)


def shards(micrograph, template_stack, orient_list):
    spread, right, below, corner = call(
        prepare_kernel,
        (
            shape_of((TILES // 2, 2, 2 * ORI_DEV, TS)),
            shape_of((CORE, TS)),
            shape_of((TS, CORE)),
            shape_of((TS, TS)),
        ),
        [HBM] * 3,
        [
            pltpu.SMEM((MEMBERS * ORI_DEV,), jnp.int32),
            pltpu.VMEM((CORE, CORE), jnp.bfloat16),
            pltpu.VMEM((256, 256), jnp.bfloat16),
            pltpu.VMEM((TILES // 2, 2, 2 * ORI_DEV, TS), jnp.bfloat16),
            pltpu.SemaphoreType.DMA((4,)),
        ],
        out_specs=(HBM, VMEM, VMEM, VMEM),
    )(pinned(orient_list), pinned(micrograph), pinned(template_stack))
    pixels = lax.all_to_all(
        spread.reshape(TILES, 2 * ORI_DEV, TS), ("tile", "orient"), 0, 0, axis_index_groups=near_groups()
    )
    kept = [column_table(), row_table(), inverse_row_table(), inverse_column_table(), micrograph]
    columns, rows, *tables, own_block = call(
        load_kernel,
        tuple(shape_of(array.shape) for array in kept),
        [HBM] * 5 + [ANY],
        [pltpu.SemaphoreType.DMA((5,))],
        flops=10000000000,
    )(*[pinned(array) for array in kept], corner)
    corner = halo(corner, GRID_W + 1)
    right = halo(right, 1)
    below = halo(below, GRID_W)
    member = lax.axis_index("orient")[None]

    def sent(piece, bits):
        return lax.ppermute(piece, "orient", [(i, i ^ bits) for i in range(MEMBERS)])


    def spectra(group):
        return call(
            template_kernel,
            shape_of((ORI_DEV, 4 * PAIRS, HALF)),
            [VMEM] * 3,
            [pltpu.VMEM((TS * ORI_DEV, TS), jnp.float32)],
            flops=1000000000,
        )(group, columns, rows)

    spectrum = shape_of((4 * PAIRS, HALF))
    image_across, image_same, g = call(
        image_kernel,
        (spectrum, spectrum, shape_of((2, TILE, HALF))),
        [SMEM] + [VMEM] * 6,
        flops=1600000000,
    )(member, corner, right, below, own_block, columns, rows)
    inner = pltpu.VMEM((ORI_DEV * ROWS, TILE), jnp.bfloat16)
    piece, wide = shape_of((2, ROWS, CORE)), shape_of((2, ROWS, CORE), jnp.float32)

    def far(image, out):
        return call(far_kernel, out, [VMEM] * 4, [inner], flops=10000000000)(image, mine, *tables)

    mine = spectra(pixels)
    across = sent(far(image_across, piece), CORE_BIT)
    same = far(image_same, wide)
    merged = call(merge_kernel, piece, [VMEM] * 2, flops=100000000)(same, across)
    merged = sent(merged, CHIP_BIT)
    other = spectra(sent(pixels, CORE_BIT))
    own = call(
        own_kernel,
        wide,
        [SMEM] + [VMEM] * 6,
        [pltpu.VMEM((4 * PAIRS, HALF), jnp.bfloat16), inner],
        flops=2000000000,
    )(member, rows, g, mine, other, *tables)
    out = shape_of((1, ROWS, CORE), jnp.float32)
    scratch = [pltpu.VMEM((2, ROWS, CORE), jnp.float32), pltpu.SemaphoreType.DMA((4,))]
    return call(finish_kernel, (out, out), [VMEM] * 2, scratch, out_specs=(HBM, HBM))(own, merged)


def solution(mesh):
    placed = (P("tile", None, None), P(None, "tile"), P())
    return jax.shard_map(
        shards,
        mesh=mesh,
        in_specs=placed,
        out_specs=(P("tile", "orient", None), P("tile", "orient", None)),
        check_vma=False,
    )
```
